32 devices in a mesh: dp: 16 (over z, x, core), mp: 2 (over y).
Axes of the slice: x: 2, y: 2, z: 4, core: 2. Of those that a mesh axis runs over, the one named last changes fastest.
Arguments:
- tokens: bfloat16 [6272, 768], P(('dp', 'mp')), may hold values from -6 to 6
- keep_mask: int32 [32, 196], P('dp'), may hold values from 0 to 1, as said below
- cotangent: bfloat16 [6272, 768], P(('dp', 'mp')), may hold values from -6 to 6
- first_gain: float32 [2, 768], replicated, may hold values from 0.1 to 1.9
- first_shift: float32 [2, 768], replicated, may hold values from -2 to 2
- attention_in: bfloat16 [2, 768, 3, 768], P(None, None, None, 'mp'), may hold values from -0.21875 to 0.21875
- query_value_bias: float32 [2, 2, 768], P(None, None, 'mp'), may hold values from -3 to 3
- position_table: float32 [2, 24, 169], P(None, 'mp'), may hold values from -4 to 4
- attention_out: bfloat16 [2, 768, 768], P(None, 'mp'), may hold values from -0.875 to 0.875
- attention_bias: float32 [2, 768], replicated, may hold values from -2 to 2
- second_gain: float32 [2, 768], replicated, may hold values from 0.1 to 1.9
- second_shift: float32 [2, 768], replicated, may hold values from -2 to 2
- expand_weight: bfloat16 [2, 768, 3072], P(None, None, 'mp'), may hold values from -0.21875 to 0.21875
- expand_bias: float32 [2, 3072], P(None, 'mp'), may hold values from -3 to 3
- reduce_weight: bfloat16 [2, 3072, 768], P(None, 'mp'), may hold values from -0.15625 to 0.15625
- reduce_bias: float32 [2, 768], replicated, may hold values from -2 to 2
Outputs:
- block_output: bfloat16 [6272, 768], P(('dp', 'mp'))
- tokens_grad: float32 [6272, 768], P(('dp', 'mp'))
- attention_in_grad: float32 [2, 768, 3, 768], P(None, 'dp', None, 'mp')
- attention_out_grad: float32 [2, 768, 768], P(None, 'mp', 'dp')
- expand_grad: float32 [2, 768, 3072], P(None, 'dp', 'mp')
- reduce_grad: float32 [2, 3072, 768], P(None, 'mp', 'dp')
- query_value_bias_grad: float32 [2, 2, 768], P(None, None, 'mp')
- expand_bias_grad: float32 [2, 3072], P(None, 'mp')
- position_table_grad: float32 [2, 24, 169], P(None, 'mp')
- vector_grads: float32 [2, 6, 768], replicated
The draws below stay inside these ranges and needn't reach their ends.
Inputs may be any that keep to these rules, and one draw needn't show every extreme that they name: keep_mask[i, p] is 1 where patch p of image i is kept and 0 where it is dropped; the kept share differs from image to image.
All inputs are finite; a program needn't handle non-finite values.
Results may differ from the reference program's by a relative error of at most 0.025.
Values may be sent and summed in bfloat16 or wider, within the bound.
No kernel may reach another device: no remote copies, remote signals or barrier semaphores. Data moves between devices by JAX's collectives and lax.ppermute only.
A program may use at most 256 MiB of HBM per device.

```python
import jax
import jax.numpy as jnp
from jax import lax

D = 768
HEADS = 24
HEAD_DIM = 32
FF = 3072
GRID = 14
WIN = 7
SHIFT = 3
LAYERS = 2
IMG_DEV = 2
PATCHES = 196
OFFSETS = 169
IMAGES = 32
ROWS = 6272
N_DP = 16


def draw_keep_mask(key, part):
    key = jax.random.fold_in(key, 7)
    level_key, cell_key = jax.random.split(key)
    levels = jax.random.randint(level_key, (IMAGES, 1), 3, 17)
    cells = jax.random.randint(cell_key, (IMAGES, PATCHES), 0, 16)
    return (cells < levels).astype(jnp.int32)


def block_levels(stream_key, extent, shards, least, top_value):
    def one(position, shards_of):
        draws = jax.random.uniform(jax.random.fold_in(jax.random.fold_in(stream_key, 6), position), (shards_of,), jnp.float32, least / len(shards), top_value / len(shards))
        return jnp.repeat(jnp.exp(draws), extent[position] // shards_of).reshape((-1,) + (1,) * (len(extent) - position - 1))

    gain = one(*shards[0])
    for cut in shards[1:]:
        gain = gain * one(*cut)
    return gain


def centred(own_key, shape, scale, reach, cuts=(), kind=jnp.bfloat16):
    factor_of = block_levels(own_key, shape, cuts, -0.22, 0.18) if cuts else 1.0
    result = jax.random.normal(own_key, shape, jnp.float32) * scale * factor_of
    return jnp.minimum(jnp.maximum(result, -reach), reach).astype(kind)


def setup_inputs(seed: int = 0) -> dict:
    arg_keys = jax.random.split(jax.random.key(seed), 17)
    tokens = centred(arg_keys[0], (ROWS, D), 1.0, 6.0, ((0, 32),))
    keep_mask = draw_keep_mask(jax.random.fold_in(arg_keys[16], 71), 0)
    cotangent = centred(arg_keys[2], (ROWS, D), 1.0, 6.0, ((0, 32),))
    first_gain = jnp.clip(1.0 + 0.18 * jax.random.normal(arg_keys[3], (LAYERS, D), jnp.float32), 0.1, 1.9)
    first_shift = centred(arg_keys[4], (LAYERS, D), 0.3, 2.0, (), jnp.float32)
    attention_in = centred(arg_keys[5], (LAYERS, D, 3, D), D ** -0.5, 0.21875, ((3, 2),))
    query_value_bias = centred(arg_keys[6], (LAYERS, 2, D), 0.5, 3.0, ((2, 2),), jnp.float32)
    position_table = centred(arg_keys[7], (LAYERS, HEADS, OFFSETS), 1.0, 4.0, ((1, 2),), jnp.float32)
    attention_out = centred(arg_keys[8], (LAYERS, D, D), (D // 16) ** -0.5, 0.875, ((1, 2),))
    attention_bias = centred(arg_keys[9], (LAYERS, D), 0.3, 2.0, (), jnp.float32)
    second_gain = jnp.clip(1.0 + 0.18 * jax.random.normal(arg_keys[10], (LAYERS, D), jnp.float32), 0.1, 1.9)
    second_shift = centred(arg_keys[11], (LAYERS, D), 0.3, 2.0, (), jnp.float32)
    expand_weight = centred(arg_keys[12], (LAYERS, D, FF), D ** -0.5, 0.21875, ((2, 2),))
    expand_bias = centred(arg_keys[13], (LAYERS, FF), 0.5, 3.0, ((1, 2),), jnp.float32)
    reduce_weight = centred(arg_keys[14], (LAYERS, FF, D), (FF // 2) ** -0.5, 0.15625, ((1, 2),))
    reduce_bias = centred(arg_keys[15], (LAYERS, D), 0.3, 2.0, (), jnp.float32)
    return {"tokens": tokens, "keep_mask": keep_mask, "cotangent": cotangent, "first_gain": first_gain, "first_shift": first_shift, "attention_in": attention_in, "query_value_bias": query_value_bias, "position_table": position_table, "attention_out": attention_out, "attention_bias": attention_bias, "second_gain": second_gain, "second_shift": second_shift, "expand_weight": expand_weight, "expand_bias": expand_bias, "reduce_weight": reduce_weight, "reduce_bias": reduce_bias}


HIGHEST = lax.Precision.HIGHEST
EPSILON = 1e-05
MASKED = -1e+30

@jax.custom_vjp
def low(v):
    return lax.optimization_barrier(v.astype(jnp.bfloat16)).astype(jnp.float32)

@jax.custom_vjp
def low_back(v):
    return v

def low_keep(v):
    return (low(v), None)

def low_pass(kept, grad):
    return (grad,)

def back_keep(v):
    return (v, None)

def back_low(kept, grad):
    return (low(grad),)
low.defvjp(low_keep, low_pass)
low_back.defvjp(back_keep, back_low)

def layer_norm(stream, norm_gain, norm_shift):
    center = stream - lax.optimization_barrier(jnp.mean(stream, axis=-1, keepdims=True))
    spread = lax.optimization_barrier(jnp.mean(center * center, axis=-1, keepdims=True))
    return center * lax.rsqrt(spread + EPSILON) * norm_gain + norm_shift

def allowed_pairs(layer_index, keep_rows):
    coords = jnp.arange(GRID)
    groups = (coords + layer_index * (WIN - SHIFT)) // WIN
    row_group = jnp.repeat(groups, GRID)
    col_group = jnp.tile(groups, GRID)
    same_window = (row_group[:, None] == row_group[None, :]) & (col_group[:, None] == col_group[None, :])
    itself = jnp.eye(PATCHES, dtype=bool)
    return same_window[None] & ((keep_rows[:, None, :] == 1) | itself[None])

def offset_ids():
    coords = jnp.arange(PATCHES)
    row_pos = coords // GRID
    col_pos = coords % GRID
    span_side = 2 * WIN - 1
    found = (row_pos[:, None] - row_pos[None, :] + WIN - 1) * span_side + col_pos[:, None] - col_pos[None, :] + WIN - 1
    return jnp.clip(found, 0, span_side * span_side - 1).astype(jnp.int32)

def forward_group(stream, keep_rows, params):
    first_gain, first_shift, attention_in, query_value_bias, position_table, attention_out, attention_bias, second_gain, second_shift, expand_weight, expand_bias, reduce_weight, reduce_bias = params
    images = keep_rows.shape[0]
    offsets = offset_ids()
    for layer_index in range(LAYERS):
        normed = low(layer_norm(stream, first_gain[layer_index], first_shift[layer_index]))
        mixed_qkv = jnp.dot(normed, attention_in[layer_index].reshape(D, 3 * D), precision=HIGHEST).reshape(-1, 3, D)
        queries = low_back(low(mixed_qkv[:, 0] + query_value_bias[layer_index, 0])).reshape(images, PATCHES, HEADS, HEAD_DIM)
        keys = low_back(low(mixed_qkv[:, 1])).reshape(images, PATCHES, HEADS, HEAD_DIM)
        values = low_back(low(mixed_qkv[:, 2] + query_value_bias[layer_index, 1])).reshape(images, PATCHES, HEADS, HEAD_DIM)
        raw_scores = low_back(jnp.einsum('iqhd,ikhd->ihqk', queries, keys, precision=HIGHEST))
        pos_bias = position_table[layer_index][:, offsets]
        scores = raw_scores * HEAD_DIM ** (-0.5) + pos_bias[None]
        scores = jnp.where(allowed_pairs(layer_index, keep_rows)[:, None], scores, MASKED)
        weights = jax.nn.softmax(scores, axis=-1)
        attended = jnp.einsum('ihqk,ikhd->iqhd', low(weights), values, precision=HIGHEST)
        attended = low_back(low(attended)).reshape(-1, D)
        branch = low_back(jnp.dot(attended, attention_out[layer_index], precision=HIGHEST))
        stream = stream + branch + attention_bias[layer_index]
        normed = low(layer_norm(stream, second_gain[layer_index], second_shift[layer_index]))
        hidden = low_back(jnp.dot(normed, expand_weight[layer_index], precision=HIGHEST) + expand_bias[layer_index])
        active = low(jax.nn.gelu(hidden, approximate=False))
        branch = low_back(jnp.dot(active, reduce_weight[layer_index], precision=HIGHEST))
        stream = stream + branch + reduce_bias[layer_index]
    return stream

def reference(tokens, keep_mask, cotangent, first_gain, first_shift, attention_in, query_value_bias, position_table, attention_out, attention_bias, second_gain, second_shift, expand_weight, expand_bias, reduce_weight, reduce_bias):
    params = tuple((item.astype(jnp.float32) for item in (first_gain, first_shift, attention_in, query_value_bias, position_table, attention_out, attention_bias, second_gain, second_shift, expand_weight, expand_bias, reduce_weight, reduce_bias)))
    group_rows = IMG_DEV * PATCHES
    keep_weight = keep_mask.astype(jnp.float32).reshape(-1, 1)
    streams = tokens.astype(jnp.float32).reshape(N_DP, group_rows, D)
    keeps = keep_mask.reshape(N_DP, IMG_DEV, PATCHES)
    cotangents = (cotangent.astype(jnp.float32) * keep_weight).reshape(N_DP, group_rows, D)

    def one_group(totals, inputs):
        stream, keep_rows, grad_out = inputs

        def forward(stream_in, params_in):
            return forward_group(stream_in, keep_rows, params_in)
        output, pull_back = jax.vjp(forward, stream, params)
        grad_stream, grad_params = pull_back(grad_out)
        totals = jax.tree.map(jnp.add, totals, grad_params)
        return (totals, (output.astype(jnp.bfloat16), grad_stream))
    zeros = jax.tree.map(jnp.zeros_like, params)
    totals, (outputs, grads) = lax.scan(one_group, zeros, (streams, keeps, cotangents))
    first_gain_grad, first_shift_grad, attention_in_grad, query_value_bias_grad, position_table_grad, attention_out_grad, attention_bias_grad, second_gain_grad, second_shift_grad, expand_grad, expand_bias_grad, reduce_grad, reduce_bias_grad = totals
    vector_grads = jnp.stack([first_gain_grad, first_shift_grad, attention_bias_grad, second_gain_grad, second_shift_grad, reduce_bias_grad], axis=1)
    return (outputs.reshape(-1, D), grads.reshape(-1, D), attention_in_grad, attention_out_grad, expand_grad, reduce_grad, query_value_bias_grad, expand_bias_grad, position_table_grad, vector_grads)
```

```python
import jax
import jax.numpy as jnp
import numpy as np
from jax import lax
from jax.experimental import pallas as pl
from jax.experimental.pallas import tpu as pltpu
from jax.sharding import PartitionSpec as P

HEAD_DIM = 32
GRID = 14
WIN = 7
SHIFT = 3
PATCHES = 196
BLOCK = 98
SLOT = 128
KEYS = 112
LANES = 128
SPAN = 2 * WIN - 1
TURN = 256

EPSILON = 1e-05
MASKED = -1e30
F32 = jnp.float32
BF16 = jnp.bfloat16
VMEM_LIMIT = 14 * 1024 * 1024

IN_VMEM = pl.BlockSpec(memory_space=pltpu.VMEM)
IN_SMEM = pl.BlockSpec(memory_space=pltpu.SMEM)
ANYWHERE = pl.BlockSpec(memory_space=pl.ANY)
IN_HBM = pl.BlockSpec(memory_space=pltpu.HBM)


def shape(dims, kind):
    return jax.ShapeDtypeStruct(dims, kind)


LINE = []
COST = 1.1e9
WIDE = 20
ATTENTION_1_ORDER = (0, 1, 2, 3)


def kernel_call(body, outs, out_specs, ins, in_specs, scratch, name, micros):
    behind = [item for item in LINE if not any(item is used for used in ins)]
    skipped = len(behind)
    ins = [
        pltpu.with_memory_space_constraint(item, pltpu.HBM) if spec is IN_HBM else item
        for item, spec in zip(ins, in_specs)
    ]
    found = pl.pallas_call(
        lambda *refs: body(*refs[skipped:]),
        out_shape=outs,
        in_specs=[ANYWHERE] * skipped + in_specs,
        out_specs=out_specs,
        scratch_shapes=scratch,
        compiler_params=pltpu.CompilerParams(vmem_limit_bytes=VMEM_LIMIT),
        cost_estimate=pl.CostEstimate(
            flops=int(micros * COST), bytes_accessed=1024, transcendentals=0
        ),
        name=name,
    )(*behind, *ins)
    LINE[:] = [min(jax.tree.leaves(found), key=lambda item: item.size)]
    return found


def dot_nn(left, right):
    return lax.dot_general(left, right, (((1,), (0,)), ((), ())), preferred_element_type=F32)


def dot_nt(left, right):
    return lax.dot_general(left, right, (((1,), (1,)), ((), ())), preferred_element_type=F32)


def dot_tn(left, right):
    return lax.dot_general(left, right, (((0,), (0,)), ((), ())), preferred_element_type=F32)


def dot_tt(left, right):
    return lax.dot_general(left, right, (((0,), (1,)), ((), ())), preferred_element_type=F32)


def dot_full(left, right, contracted):
    return lax.dot_general(
        left,
        right,
        (contracted, ((), ())),
        preferred_element_type=F32,
        precision=lax.Precision.HIGHEST,
    )


def place_matrix(layer):
    row = lax.broadcasted_iota(jnp.int32, (2 * SLOT, PATCHES), 0)
    patch = lax.broadcasted_iota(jnp.int32, (2 * SLOT, PATCHES), 1)
    second = row >= SLOT
    within = jnp.where(second, row - SLOT, row)
    found = within + jnp.where(second, BLOCK, 0) + layer * SHIFT * GRID
    found = jnp.where(found >= PATCHES, found - PATCHES, found)
    return jnp.where((within < BLOCK) & (found == patch), 1.0, 0.0).astype(BF16)


def window_matrix(layer, block):
    def groups(place):
        turned_row = (place * 147) >> 11
        col = place - turned_row * GRID
        row = turned_row + block * WIN + layer * SHIFT
        row = jnp.where(row >= GRID, row - GRID, row)

        def group(position):
            moved = position + layer * (WIN - SHIFT)
            return jnp.where(moved >= 2 * WIN, 2, jnp.where(moved >= WIN, 1, 0))

        return group(row) * 4 + group(col)

    key = lax.broadcasted_iota(jnp.int32, (KEYS, LANES), 0)
    query = lax.broadcasted_iota(jnp.int32, (KEYS, LANES), 1)
    return (groups(key) == groups(query)) & (key < BLOCK) & (query < BLOCK)


def offset_matrix():
    offset = lax.broadcasted_iota(jnp.int32, (SPAN * SPAN, TURN), 0)
    lane = lax.broadcasted_iota(jnp.int32, (SPAN * SPAN, TURN), 1)
    row = (offset * 79) >> 10
    place = offset - row * SPAN + row * GRID - (WIN - 1) * (GRID + 1)
    return jnp.where(jnp.where(place < 0, place + TURN, place) == lane, 1.0, 0.0)


def heads_apart(value):
    rows = value.shape[0]
    parts = []
    for member in range(rows // HEAD_DIM):
        start = member * HEAD_DIM
        pieces = [value[start : start + HEAD_DIM]]
        if start:
            pieces.insert(0, jnp.zeros((start, value.shape[1]), value.dtype))
        if start + HEAD_DIM < rows:
            pieces.append(jnp.zeros((rows - start - HEAD_DIM, value.shape[1]), value.dtype))
        parts.append(jnp.concatenate(pieces, axis=0))
    return jnp.concatenate(parts, axis=1)


def heads_together(value):
    count = value.shape[0] // HEAD_DIM
    columns = value.shape[1] // count
    return jnp.concatenate(
        [
            value[
                member * HEAD_DIM : (member + 1) * HEAD_DIM,
                member * columns : (member + 1) * columns,
            ]
            for member in range(count)
        ],
        axis=0,
    )


def norm_rows(stream, gain, shift):
    center = stream - jnp.mean(stream, axis=-1, keepdims=True)
    spread = jnp.mean(center * center, axis=-1, keepdims=True)
    rstd = lax.rsqrt(spread + EPSILON)
    x_hat = center * rstd
    return x_hat, rstd, (x_hat * gain + shift).astype(BF16)


def norm_back(grad_normed, x_hat, rstd, gain):
    scaled = grad_normed * gain
    term = jnp.mean(scaled, axis=-1, keepdims=True)
    along = jnp.mean(scaled * x_hat, axis=-1, keepdims=True)
    return rstd * (scaled - term - x_hat * along)


def column_sum(value):
    return jnp.sum(value, axis=0, keepdims=True)


def put_sums(out, prior, sums):
    for row, found in enumerate(sums):
        out[row : row + 1] = found if prior is None else found + prior[row : row + 1]
    out[len(sums) :] = jnp.zeros((out.shape[0] - len(sums), out.shape[1]), F32)


FIRST_GAIN, FIRST_SHIFT, ATTENTION_BIAS, SECOND_GAIN, SECOND_SHIFT, REDUCE_BIAS = range(6)


def vector_row(vectors, member, layer):
    row = member * (vectors.shape[0] // 6) + layer
    return vectors[row : row + 1]


def head_lanes(rows, member):
    lane = lax.broadcasted_iota(jnp.int32, (rows, LANES), 1)
    return (lane >= member * HEAD_DIM) & (lane < (member + 1) * HEAD_DIM)


def head_rows(value):
    rows = value.shape[0]
    return jnp.concatenate(
        [
            jnp.where(head_lanes(rows, member), value, jnp.zeros_like(value))
            for member in range(LANES // HEAD_DIM)
        ],
        axis=0,
    )


def tables_body(heads, layers, refs):
    half = refs[0]
    in_hbm, refs = refs[1:12], refs[12:]
    biases, refs = refs[:layers], refs[layers:]
    masks, refs = refs[: 2 * layers], refs[2 * layers :]
    cot_out, vectors_out, up_out, pair_out = refs[:4]
    held, sems = refs[4:15], refs[15]
    copies = []
    for index, (source, target) in enumerate(zip(in_hbm, held)):
        copies.append(pltpu.make_async_copy(source, target, sems.at[index]))
        copies[-1].start()
    table, keep, cotangent, up_bias, pair_bias = held[:5]
    same = lax.broadcasted_iota(jnp.int32, (KEYS, LANES), 0) == lax.broadcasted_iota(
        jnp.int32, (KEYS, LANES), 1
    )
    offsets = offset_matrix()
    per_group = LANES // HEAD_DIM
    for copy in copies:
        copy.wait()
    own_first = half[0] == 0
    rows = [keep[image : image + 1].astype(F32) for image in range(2)]
    pair = jnp.concatenate(
        [jnp.where(own_first, rows[0], rows[1]), jnp.where(own_first, rows[1], rows[0])], axis=0
    ).astype(BF16)
    for layer in range(layers):
        line = dot_full(table[:, layer], offsets, ((1,), (0,)))
        for head in range(heads):
            wide = jnp.broadcast_to(line[head : head + 1], (KEYS, TURN))
            lanes = head % per_group * LANES
            biases[layer][head // per_group, :, lanes : lanes + LANES] = pltpu.roll(
                wide, 0, 1, stride=1, stride_axis=0
            )[:, :LANES]
        place = place_matrix(layer)
        kept = dot_nt(place, pair)
        for block in range(2):
            window = window_matrix(layer, block)
            for image in range(2):
                column = kept[block * SLOT : block * SLOT + KEYS, image : image + 1]
                fine = window & ((column > 0.5) | same)
                masks[layer * 2 + image][block] = jnp.where(fine, 0.0, MASKED)
        if layer == 0:
            column = dot_tn(place, kept.astype(BF16))[:, 0:1]
            cot_out[...] = (cotangent[...].astype(F32) * column).astype(BF16)
    for index, item in enumerate(held[5:]):
        vectors_out[index * layers : (index + 1) * layers] = item[...]
    up_out[...] = up_bias[...]
    pair_out[...] = pair_bias[...]


def make_tables(half, position_table, keep_mask, cotangent, up_bias, pair_bias, vectors):
    heads, layers, _ = position_table.shape
    groups = heads * HEAD_DIM // LANES
    width = vectors[0].shape[1]
    ins = (position_table, keep_mask, cotangent, up_bias, pair_bias, *vectors)
    outs = [shape((groups, KEYS, 4 * LANES), F32)] * layers + [shape((2, KEYS, LANES), F32)] * (
        2 * layers
    )
    outs += [
        shape(cotangent.shape, BF16),
        shape((len(vectors) * layers, width), F32),
        shape(up_bias.shape, F32),
        shape(pair_bias.shape, F32),
    ]
    found = kernel_call(
        lambda *refs: tables_body(heads, layers, refs),
        outs,
        [IN_VMEM] * len(outs),
        (half, *ins),
        [IN_SMEM] + [IN_HBM] * len(ins),
        [pltpu.VMEM(item.shape, item.dtype) for item in ins] + [pltpu.SemaphoreType.DMA((len(ins),))],
        "tables",
        1.6,
    )
    masks = [found[layers + 2 * layer : layers + 2 * layer + 2] for layer in range(layers)]
    return found[:layers], masks, found[3 * layers :]


def attention_body(layer, heads, chained, refs):
    if chained:
        base, mine, theirs = refs[:3]
        refs = refs[3:]
    else:
        base, refs = refs[0], refs[1:]
    vectors, pair_bias, bias, mask, in_hbm, out_hbm = refs[:6]
    refs = refs[6:]
    if chained:
        stream_out, refs = refs[0], refs[1:]
    normed_out, hat_out, rstd_out, qkv_out, weights_out, attended_out, partial_out = refs[:7]
    in_held, out_held, turned, sems = refs[7:]
    width = heads * HEAD_DIM
    fetch_in = pltpu.make_async_copy(in_hbm.at[layer], in_held, sems.at[0])
    fetch_out = pltpu.make_async_copy(out_hbm.at[layer], out_held, sems.at[1])
    fetch_in.start()
    fetch_out.start()
    stream = base[...].astype(F32)
    if chained:
        stream = (
            stream
            + (mine[...].astype(F32) + theirs[...].astype(F32))
            + vector_row(vectors, REDUCE_BIAS, layer - 1)
        )
        stream_out[...] = stream
    x_hat, rstd, normed = norm_rows(
        stream, vector_row(vectors, FIRST_GAIN, layer), vector_row(vectors, FIRST_SHIFT, layer)
    )
    normed_out[...] = normed
    hat_out[...] = x_hat.astype(BF16)
    rstd_out[...] = rstd
    place = place_matrix(layer)
    fetch_in.wait()
    parts = []
    for member in range(3):
        mixed = dot_nn(normed, in_held[member])
        if member != 1:
            mixed = mixed + pair_bias[layer, member // 2 : member // 2 + 1]
        parts.append(mixed.astype(BF16))
        qkv_out[:, member * width : (member + 1) * width] = parts[-1]
    queries = dot_tt(parts[0], place).astype(BF16)
    keys = dot_nn(place, parts[1]).astype(BF16)
    values = dot_tt(parts[2], place).astype(BF16)
    scale = HEAD_DIM ** (-0.5)
    groups = width // LANES
    for group in range(groups):
        lanes = slice(group * LANES, (group + 1) * LANES)
        for block in range(2):
            slots = slice(block * SLOT, (block + 1) * SLOT)
            own_keys = slice(block * SLOT, block * SLOT + KEYS)
            scores = dot_nn(keys[own_keys, lanes], heads_apart(queries[lanes, slots])) * scale
            scores = scores + bias[group] + jnp.concatenate([mask[block]] * 4, axis=1)
            raised = jnp.exp(scores - jnp.max(scores, axis=0, keepdims=True))
            weights = raised * (1.0 / jnp.sum(raised, axis=0, keepdims=True))
            weights = weights.astype(BF16)
            weights_out[group * 2 + block] = weights
            found = heads_together(dot_nn(values[lanes, own_keys], weights))
            turned[lanes, slots] = found.astype(BF16)
    attended = dot_tt(place, turned[...]).astype(BF16)
    attended_out[...] = attended
    fetch_out.wait()
    partial_out[...] = dot_nn(attended, out_held[...]).astype(BF16)


def attention_forward(layer, streams, vectors, pair_bias, bias, mask, matrix_in, matrix_out):
    chained = len(streams) > 1
    rows, width = streams[0].shape
    head_width = matrix_out.shape[1]
    heads = head_width // HEAD_DIM
    outs = [
        shape((rows, width), BF16),
        shape((rows, width), BF16),
        shape((rows, 1), F32),
        shape((rows, 3 * head_width), BF16),
        shape((2 * head_width // LANES, KEYS, 4 * LANES), BF16),
        shape((rows, head_width), BF16),
        shape((rows, width), BF16),
    ]
    if chained:
        outs = [shape((rows, width), F32)] + outs
    ins = (*streams, vectors, pair_bias, bias, mask, matrix_in, matrix_out)
    found = kernel_call(
        lambda *refs: attention_body(layer, heads, chained, refs),
        outs,
        [IN_VMEM] * len(outs),
        ins,
        [IN_VMEM] * (len(ins) - 2) + [IN_HBM] * 2,
        [
            pltpu.VMEM((3, width, head_width), BF16),
            pltpu.VMEM((head_width, width), BF16),
            pltpu.VMEM((head_width, 2 * SLOT), BF16),
            pltpu.SemaphoreType.DMA((2,)),
        ],
        f"attention_{layer}",
        4,
    )
    return found if chained else [streams[0], *found]


def gelu_parts(hidden):
    below = 0.5 * (1.0 + lax.erf(hidden * (0.5**0.5)))
    density = jnp.exp(-0.5 * hidden * hidden) * (0.5 / np.pi) ** 0.5
    return hidden * below, below + hidden * density


def fetch_slices(layer, step, up_hbm, down_hbm, up_held, down_held, sems):
    found = []
    for index in range(up_held.shape[1] // step):
        part = slice(index * step, (index + 1) * step)
        pair = (
            pltpu.make_async_copy(up_hbm.at[layer, :, part], up_held.at[:, part], sems.at[0, index]),
            pltpu.make_async_copy(down_hbm.at[layer, part], down_held.at[part], sems.at[1, index]),
        )
        for copy in pair:
            copy.start()
        found.append((part, *pair))
    return found


def ffn_body(layer, both, joined, step, refs):
    base, mine, theirs, vectors, up_bias = refs[:5]
    refs = refs[5:]
    if both:
        grad, refs = refs[0], refs[1:]
    if joined:
        prior_sums, refs = refs[0], refs[1:]
    up_hbm, down_hbm, *refs = refs
    if both:
        mid_out, normed_out, hat_out, rstd_out, active_out, slope_out, partial_out = refs[:7]
        back_out, sums_out = refs[7:9]
        up_held, down_held, sems = refs[9:]
    else:
        mid_out, normed_out, hat_out, rstd_out, active_out, slope_out, partial_out = refs[:7]
        up_held, down_held, sems = refs[7:]
    slices = fetch_slices(layer, step, up_hbm, down_hbm, up_held, down_held, sems)
    mid = (
        base[...].astype(F32)
        + (mine[...].astype(F32) + theirs[...].astype(F32))
        + vector_row(vectors, ATTENTION_BIAS, layer)
    )
    mid_out[...] = mid
    x_hat, rstd, normed = norm_rows(
        mid, vector_row(vectors, SECOND_GAIN, layer), vector_row(vectors, SECOND_SHIFT, layer)
    )
    normed_out[...] = normed
    hat_out[...] = x_hat.astype(BF16)
    rstd_out[...] = rstd
    if both:
        grad_rows = grad[...]
        put_sums(sums_out, prior_sums if joined else None, [column_sum(grad_rows.astype(F32))])
    forward, backward = None, None
    for part, fetch_up, fetch_down in slices:
        fetch_up.wait()
        fetch_down.wait()
        hidden = dot_nn(normed, up_held[:, part]) + up_bias[layer : layer + 1, part]
        active, slope = gelu_parts(hidden)
        active = active.astype(BF16)
        active_out[:, part] = active
        term = dot_nn(active, down_held[part])
        forward = term if forward is None else forward + term
        if both:
            grad_hidden = (slope * dot_nt(grad_rows, down_held[part])).astype(BF16)
            slope_out[:, part] = grad_hidden
            term = dot_nt(grad_hidden, up_held[:, part])
            backward = term if backward is None else backward + term
        else:
            slope_out[:, part] = slope.astype(BF16)
    partial_out[...] = forward.astype(BF16)
    if both:
        back_out[...] = backward.astype(BF16)


def ffn_forward(layer, streams, vectors, up_bias, up, down, grad=None, prior_sums=None):
    rows, width = streams[0].shape
    units = up.shape[2]
    both = grad is not None
    outs = [
        shape((rows, width), F32),
        shape((rows, width), BF16),
        shape((rows, width), BF16),
        shape((rows, 1), F32),
        shape((rows, units), BF16),
        shape((rows, units), BF16),
        shape((rows, width), BF16),
    ]
    ins = [*streams, vectors, up_bias]
    if both:
        outs += [shape((rows, width), BF16), shape((8, width), F32)]
        ins.append(grad)
    joined = prior_sums is not None
    if joined:
        ins.append(prior_sums)
    specs = [IN_VMEM] * len(ins) + [IN_HBM] * 2
    return kernel_call(
        lambda *refs: ffn_body(layer, both, joined, units // 3, refs),
        outs,
        [IN_VMEM] * len(outs),
        (*ins, up, down),
        specs,
        [
            pltpu.VMEM((width, units), BF16),
            pltpu.VMEM((units, width), BF16),
            pltpu.SemaphoreType.DMA((2, 4)),
        ],
        f"ffn_both_{layer}" if both else f"ffn_{layer}",
        4.6 if both else 3,
    )


def ffn_back_body(layer, joined, step, refs):
    base, mine, theirs, hat, rstd, vectors, slope = refs[:7]
    refs = refs[7:]
    if joined:
        prior_sums, refs = refs[0], refs[1:]
    up_hbm, down_hbm = refs[:2]
    grad_out, low_out, hidden_out, partial_out, sums_out = refs[2:7]
    up_held, down_held, sems = refs[7:]
    slices = fetch_slices(layer, step, up_hbm, down_hbm, up_held, down_held, sems)
    grad_normed = mine[...].astype(F32) + theirs[...].astype(F32)
    x_hat = hat[...].astype(F32)
    grad = base[...] + norm_back(
        grad_normed, x_hat, rstd[...], vector_row(vectors, FIRST_GAIN, layer + 1)
    )
    grad_out[...] = grad
    low = grad.astype(BF16)
    low_out[...] = low
    sums = [column_sum(grad_normed * x_hat), column_sum(grad_normed), column_sum(grad)]
    put_sums(sums_out, prior_sums if joined else None, sums)
    backward = None
    for part, fetch_up, fetch_down in slices:
        fetch_down.wait()
        fetch_up.wait()
        grad_hidden = (slope[:, part].astype(F32) * dot_nt(low, down_held[part])).astype(BF16)
        hidden_out[:, part] = grad_hidden
        term = dot_nt(grad_hidden, up_held[:, part])
        backward = term if backward is None else backward + term
    partial_out[...] = backward.astype(BF16)


def ffn_backward(layer, grads, hat, rstd, vectors, slope, up, down, prior_sums=None, micros=4):
    rows, width = grads[0].shape
    units = up.shape[2]
    outs = [
        shape((rows, width), F32),
        shape((rows, width), BF16),
        shape((rows, units), BF16),
        shape((rows, width), BF16),
        shape((8, width), F32),
    ]
    ins = [*grads, hat, rstd, vectors, slope]
    joined = prior_sums is not None
    if joined:
        ins.append(prior_sums)
    return kernel_call(
        lambda *refs: ffn_back_body(layer, joined, units // 4, refs),
        outs,
        [IN_VMEM] * len(outs),
        (*ins, up, down),
        [IN_VMEM] * len(ins) + [IN_HBM] * 2,
        [
            pltpu.VMEM((width, units), BF16),
            pltpu.VMEM((units, width), BF16),
            pltpu.SemaphoreType.DMA((2, 4)),
        ],
        f"ffn_back_{layer}",
        micros,
    )


def attention_back_body(layer, heads, joined, refs):
    base, mine, theirs, hat, rstd, vectors, first_hat, qkv, weights = refs[:9]
    refs = refs[9:]
    if joined:
        prior_sums, prior_table = refs[:2]
        refs = refs[2:]
    in_hbm, out_hbm = refs[:2]
    grad_out, low_out, mixed_out, partial_out, sums_out, table_out = refs[2:8]
    in_held, out_held, turned, merged, diagonals, sems = refs[8:]
    width = heads * HEAD_DIM
    per_group = LANES // HEAD_DIM
    fetch_out = pltpu.make_async_copy(out_hbm.at[layer], out_held, sems.at[1])
    fetch_in = pltpu.make_async_copy(in_hbm.at[layer], in_held, sems.at[0])
    fetch_out.start()
    fetch_in.start()
    grad_normed = mine[...].astype(F32) + theirs[...].astype(F32)
    x_hat = hat[...].astype(F32)
    grad = base[...].astype(F32) + norm_back(
        grad_normed, x_hat, rstd[...], vector_row(vectors, SECOND_GAIN, layer)
    )
    grad_out[...] = grad
    low = grad.astype(BF16)
    low_out[...] = low
    sums = [column_sum(grad_normed * x_hat), column_sum(grad_normed), column_sum(grad)]
    place = place_matrix(layer)
    queries = dot_nn(place, qkv[:, :width]).astype(BF16)
    turned_keys = dot_tt(qkv[:, width : 2 * width], place).astype(BF16)
    values = dot_nn(place, qkv[:, 2 * width :]).astype(BF16)
    fetch_out.wait()
    grad_attended = dot_nt(low, out_held[...]).astype(BF16)
    grad_slots = dot_nn(place, grad_attended).astype(BF16)
    grad_turned = dot_tt(grad_attended, place).astype(BF16)
    scale = HEAD_DIM ** (-0.5)
    empty = jnp.zeros((SLOT - KEYS, LANES), BF16)
    for group in range(width // LANES):
        lanes = slice(group * LANES, (group + 1) * LANES)
        total = None
        for block in range(2):
            top_row = block * SLOT
            slots = slice(top_row, top_row + SLOT)
            own_keys = slice(top_row, top_row + KEYS)
            low_weights = weights[group * 2 + block]
            full = low_weights.astype(F32)
            grad_weights = dot_nn(values[own_keys, lanes], heads_apart(grad_turned[lanes, slots]))
            spread = jnp.sum(full * grad_weights, axis=0, keepdims=True)
            grad_scores = full * (grad_weights - spread)
            total = grad_scores if total is None else total + grad_scores
            grad_raw = (grad_scores * scale).astype(BF16)
            grad_query = heads_together(dot_nn(turned_keys[lanes, own_keys], grad_raw))
            grad_key = dot_nn(grad_raw, head_rows(queries[slots, lanes]))
            grad_value = dot_nn(low_weights, head_rows(grad_slots[slots, lanes]))
            turned[lanes, slots] = grad_query.astype(BF16)
            for at, found in ((0, grad_key), (width, grad_value)):
                columns = slice(at + group * LANES, at + (group + 1) * LANES)
                merged[own_keys, columns] = found.astype(BF16)
                merged[top_row + KEYS : top_row + SLOT, columns] = empty
        for member in range(per_group):
            head = group * per_group + member
            own = total[:, member * LANES : (member + 1) * LANES]
            wide = jnp.concatenate([own, jnp.zeros_like(own)], axis=1)
            line = None
            for start in range(0, KEYS, 8):
                rows = wide[start : start + 8]
                if start:
                    rows = pltpu.roll(rows, TURN - start, 1)
                line = rows if line is None else line + rows
            diagonals[head * 8 : head * 8 + 8] = line
    mixed = [dot_tt(place, turned[...]).astype(BF16)]
    both = dot_tn(place, merged[...]).astype(BF16)
    mixed += [both[:, :width], both[:, width:]]
    mixed_out[:, :width] = mixed[0]
    mixed_out[:, width:] = both
    fetch_in.wait()
    partial = dot_nt(mixed[0], in_held[0])
    partial = partial + dot_nt(mixed[1], in_held[1])
    partial = partial + dot_nt(mixed[2], in_held[2])
    partial_out[...] = partial.astype(BF16)
    sums += [column_sum(partial * first_hat[...].astype(F32)), column_sum(partial)]
    put_sums(sums_out, prior_sums if joined else None, sums)
    lines = diagonals[...]
    row = lax.broadcasted_iota(jnp.int32, lines.shape, 0)
    for bit in range(3):
        moved = pltpu.roll(lines, TURN - (1 << bit), 1)
        lines = jnp.where(((row >> bit) & 1) == 1, moved, lines)
    lines = jnp.sum(lines.reshape(heads, 8, TURN), axis=1)
    table = dot_full(lines, offset_matrix(), ((1,), (1,)))
    table_out[...] = table + prior_table[...] if joined else table


def attention_backward(
    layer, grads, hat, rstd, vectors, first_hat, qkv, weights, matrix_in, matrix_out,
    prior=(), micros=5,
):
    rows, width = grads[0].shape
    head_width = matrix_out.shape[1]
    heads = head_width // HEAD_DIM
    outs = [
        shape((rows, width), F32),
        shape((rows, width), BF16),
        shape((rows, 3 * head_width), BF16),
        shape((rows, width), BF16),
        shape((8, width), F32),
        shape((heads, SPAN * SPAN), F32),
    ]
    ins = (*grads, hat, rstd, vectors, first_hat, qkv, weights, *prior)
    return kernel_call(
        lambda *refs: attention_back_body(layer, heads, bool(prior), refs),
        outs,
        [IN_VMEM] * len(outs),
        (*ins, matrix_in, matrix_out),
        [IN_VMEM] * len(ins) + [IN_HBM] * 2,
        [
            pltpu.VMEM((3, width, head_width), BF16),
            pltpu.VMEM((head_width, width), BF16),
            pltpu.VMEM((head_width, 2 * SLOT), BF16),
            pltpu.VMEM((2 * SLOT, 2 * head_width), BF16),
            pltpu.VMEM((heads * 8, TURN), F32),
            pltpu.SemaphoreType.DMA((2,)),
        ],
        f"attention_back_{layer}",
        micros,
    )


def finish_body(base, mine, theirs, hat, rstd, vectors, out):
    grad_normed = mine[...].astype(F32) + theirs[...].astype(F32)
    out[...] = base[...] + norm_back(
        grad_normed, hat[...].astype(F32), rstd[...], vector_row(vectors, FIRST_GAIN, 0)
    )


def output_body(layer, base, mine, theirs, vectors, out):
    total = base[...] + (mine[...].astype(F32) + theirs[...].astype(F32))
    out[...] = (total + vector_row(vectors, REDUCE_BIAS, layer)).astype(BF16)


def finish(body, kind, name, micros, *ins):
    return kernel_call(
        body, shape(ins[0].shape, kind), IN_VMEM, ins, [IN_VMEM] * len(ins), [], name, micros
    )


def group_place(group, top, order):
    place = 0
    for step, bit in enumerate(order):
        place = place + ((((group >> bit) & 1) ^ ((top >> bit) & 1)) << (len(order) - 1 - step))
    return place


def grads_body(pairs, groups, order, step, summed, refs):
    top = refs[0][0]
    lefts = 1 + max(left for left, _ in pairs)
    rights = len(pairs)
    refs = refs[1:]
    left_refs, refs = refs[: 2 * lefts], refs[2 * lefts :]
    right_refs, refs = refs[: 2 * rights], refs[2 * rights :]
    keep_out, send_out, sums_out, held, turned, wide, sems = refs
    rows = left_refs[0].shape[0]
    space = wide.shape[0] // 2
    empty = space - rows
    block = keep_out.shape[1]
    copies = []
    for left in range(lefts):
        for image in range(2):
            start = image * space
            turned[left, :, start + LANES : start + space] = jnp.zeros(
                (turned.shape[1], space - LANES), BF16
            )
            turned[left, :, start : start + rows] = left_refs[2 * left + image][...].T
    at = 0
    sum_at = 0
    for right, (left, _) in enumerate(pairs):
        columns = right_refs[2 * right].shape[1]
        for image in range(2):
            start = image * space
            wide[start : start + rows, :columns] = right_refs[2 * right + image][...]
            wide[start + rows : start + space, :columns] = jnp.zeros((empty, columns), BF16)
        if summed[right]:
            sums_out[0:1, sum_at : sum_at + columns] = column_sum(wide[:, :columns].astype(F32))
            sum_at += columns
        for first in range(0, columns, step):
            found = dot_nn(turned[left], wide[:, first : first + step]).astype(BF16)
            for group in range(groups):
                held[group_place(group, top, order), :, at : at + step] = found[
                    group * block : (group + 1) * block
                ]
            for half, out in ((0, keep_out), (1, send_out)):
                copy = pltpu.make_async_copy(
                    held.at[half * groups // 2 : (half + 1) * groups // 2, :, at : at + step],
                    out.at[:, :, at : at + step],
                    sems.at[half, at // step],
                )
                copy.start()
                copies.append(copy)
            at += step
    for copy in copies:
        copy.wait()


def weight_grads(top, groups, order, pairs, lefts, rights, summed, name, micros):
    width = lefts[0].shape[1]
    step = 512 if all(item.shape[1] % 512 == 0 for item in rights) else 384
    columns = sum(item.shape[1] for item in rights[::2])
    widest = max(item.shape[1] for item in rights)
    space = 2 * LANES
    summed_columns = sum(item.shape[1] for item, used in zip(rights[::2], summed) if used)
    half = shape((groups // 2, width // groups, columns), BF16)
    outs = [half, half, shape((8, summed_columns), F32)]
    count = 1 + max(left for left, _ in pairs)
    return kernel_call(
        lambda *refs: grads_body(pairs, groups, order, step, summed, refs),
        outs,
        [ANYWHERE, ANYWHERE, IN_VMEM],
        (top, *lefts, *rights),
        [IN_SMEM] + [IN_VMEM] * (len(lefts) + len(rights)),
        [
            pltpu.VMEM((groups, width // groups, columns), BF16),
            pltpu.VMEM((count, width, 2 * space), BF16),
            pltpu.VMEM((2 * space, widest), BF16),
            pltpu.SemaphoreType.DMA((2, columns // step)),
        ],
        name,
        micros,
    )


def swap(value):
    return lax.ppermute(value, "mp", [(0, 1), (1, 0)])


def trade(value, bit, size):
    return lax.ppermute(value, "dp", [(source, source ^ bit) for source in range(size)])


def fold_body(kept, found, keep_out, send_out):
    half = keep_out.shape[0]
    for start, out in ((0, keep_out), (half, send_out)):
        for block in range(half):
            total = kept[start + block].astype(F32) + found[start + block].astype(F32)
            out[block] = total.astype(BF16)


def fold(kept, found, name):
    half = shape((kept.shape[0] // 2, *kept.shape[1:]), BF16)
    return kernel_call(
        fold_body, [half, half], [IN_VMEM] * 2, (kept, found), [IN_VMEM] * 2, [], name,
        kept.size * 0.5e-6,
    )


class Scatter:
    def __init__(self, kept, sent, order, size, name):
        self.kept, self.sent, self.order, self.size, self.name = kept, sent, order, size, name
        self.finer = size >> len(order)
        self.level = 0
        self.send()

    def send(self):
        self.found = trade(self.sent, self.finer << self.order[self.level], self.size)

    def step(self):
        if self.level + 1 < len(self.order):
            self.kept, self.sent = fold(self.kept, self.found, f"{self.name}_{self.level}")
            self.level += 1
            self.send()

    def finish(self):
        for _ in self.order:
            self.step()
        kept, found, finer = self.kept, self.found, self.finer
        rank = lax.axis_index("dp")
        while finer > 1:
            finer //= 2
            held = (kept.astype(F32) + found.astype(F32)).astype(BF16)
            halves = held.reshape((2, 1, held.shape[1] // 2, held.shape[2]))
            mine = (rank // finer) % 2
            kept = lax.dynamic_index_in_dim(halves, mine, 0, keepdims=False)
            found = trade(lax.dynamic_index_in_dim(halves, 1 - mine, 0, keepdims=False), finer, self.size)
        return kept, found

    def join(self):
        kept, found = self.finish()
        return (
            kernel_call(
                add_body, shape(kept.shape, F32), IN_VMEM, (kept, found), [IN_VMEM] * 2, [],
                f"{self.name}_end", 0.4,
            ),
        )


def add_body(left, right, out):
    out[...] = left[...].astype(F32) + right[...].astype(F32)


class Total:
    def __init__(self, value, size):
        bits = list(range(size.bit_length() - 1))
        self.value, self.size = value, size
        self.left = [1 << bit for bit in bits[:1] + bits[2:] + bits[1:2]]
        self.send()

    def send(self):
        self.found = trade(self.value, self.left.pop(0), self.size)

    def step(self):
        if self.left:
            self.value = kernel_call(
                add_body, shape(self.value.shape, F32), IN_VMEM, (self.value, self.found),
                [IN_VMEM] * 2, [], "total", 0.5,
            )
            self.send()

    def finish(self):
        while self.left:
            self.step()
        return self.value, self.found


def collect_body(counts, widths, refs):
    outs = refs[sum(counts) :]
    for layer, count in enumerate(counts):
        total = refs[0][0].astype(F32)
        if count == 2:
            total = total + refs[1][0].astype(F32)
        refs = refs[count:]
        at = 0
        for out, parts in zip(outs, widths):
            for part in range(parts):
                columns = out.shape[-1]
                if len(out.shape) == 4:
                    out[layer, part] = total[:, at : at + columns]
                else:
                    out[layer] = total[:, at : at + columns]
                at += columns


def collect(pairs, shapes, name):
    flat = [item for pair in pairs for item in pair]
    counts = [len(pair) for pair in pairs]
    return kernel_call(
        lambda *refs: collect_body(
            counts, [dims[1] if len(dims) == 4 else 1 for dims in shapes], refs
        ),
        [shape(dims, F32) for dims in shapes],
        [IN_VMEM] * len(shapes),
        flat,
        [IN_VMEM] * len(flat),
        [],
        name,
        1.5,
    )


def pack_body(width, layers, refs):
    sums_0, theirs_0, sums_low, sums_1, last = refs[:5]
    ups, mixes, tables = refs[5 : 5 + layers], refs[5 + layers : 5 + 2 * layers], refs[5 + 2 * layers : -1]
    out = refs[-1]
    out[...] = jnp.zeros(out.shape, F32)
    out[0:2] = sums_0[3:5] + theirs_0[3:5]
    out[2:3] = sums_0[2:3]
    out[3:5] = sums_0[0:2]
    out[5:6] = sums_low[2:3]
    out[6:8] = sums_low[0:2]
    out[8:9] = sums_1[2:3]
    out[9:11] = sums_1[0:2]
    out[11:12] = last[0:1]
    row = 6 * layers
    for item in ups:
        for start in range(0, item.shape[1], width):
            out[row : row + 1] = item[0:1, start : start + width]
            row += 1
    third = mixes[0].shape[1] // 3
    for item in mixes:
        out[row : row + 1, :third] = item[0:1, :third]
        out[row : row + 1, third : 2 * third] = item[0:1, 2 * third :]
        row += 1
    for item in tables:
        heads, offsets = item.shape
        for head in range(heads):
            lane = head * TURN % width
            out[row : row + 1, lane : lane + offsets] = item[head : head + 1]
            if (head + 1) * TURN % width == 0:
                row += 1


def unpack_body(refs):
    packed, found, vectors, up_bias, pair_bias, tables = refs
    width = packed.shape[1]
    layers, units = up_bias.shape
    total = packed[...] + found[...]
    for layer in range(layers):
        for member in range(6):
            vectors[member, layer : layer + 1] = total[6 * layer + member : 6 * layer + member + 1]
    row = 6 * layers
    for layer in range(layers):
        for start in range(0, units, width):
            up_bias[layer : layer + 1, start : start + width] = total[row : row + 1]
            row += 1
    third = pair_bias.shape[2]
    for layer in range(layers):
        for member in range(2):
            pair_bias[layer, member : member + 1] = total[
                row : row + 1, member * third : (member + 1) * third
            ]
        row += 1
    heads, _, offsets = tables.shape
    for layer in range(layers):
        for head in range(heads):
            lane = head * TURN % width
            tables[head, layer : layer + 1] = total[row : row + 1, lane : lane + offsets]
            if (head + 1) * TURN % width == 0:
                row += 1


def shards(
    tokens,
    keep_mask,
    cotangent,
    first_gain,
    first_shift,
    attention_in,
    query_value_bias,
    position_table,
    attention_out,
    attention_bias,
    second_gain,
    second_shift,
    expand_weight,
    expand_bias,
    reduce_weight,
    reduce_bias,
):
    LINE.clear()
    size = lax.axis_size("dp")
    half = lax.axis_index("mp")
    groups = min(16, size)
    top = (lax.axis_index("dp") // (size // groups)).astype(jnp.int32).reshape(1)
    layers, width = first_gain.shape
    head_width = attention_out.shape[1]
    units = expand_weight.shape[2]
    heads = head_width // HEAD_DIM
    matrix_in = jnp.transpose(attention_in, (0, 2, 1, 3))
    other_tokens = swap(tokens)
    own_half = half.astype(jnp.int32).reshape(1)
    bias, masks, (cot_own, vectors, up_bias, pair_bias) = make_tables(
        own_half, jnp.transpose(position_table, (1, 0, 2)), keep_mask, cotangent, expand_bias, query_value_bias,
        (first_gain, first_shift, attention_bias, second_gain, second_shift, reduce_bias),
    )

    def attend(layer, image, streams):
        return attention_forward(
            layer, streams, vectors, pair_bias, bias[layer], masks[layer][image], matrix_in,
            attention_out,
        )

    def feed(layer, streams, grad=None, prior_sums=None):
        return ffn_forward(
            layer, streams, vectors, up_bias, expand_weight, reduce_weight, grad, prior_sums
        )

    att, ffn = [[None, None], [None, None]], [[None, None], [None, None]]
    att[0][0] = attend(0, 0, (tokens,))
    sent_own = swap(att[0][0][7])
    att[0][1] = attend(0, 1, (other_tokens,))
    sent_other = swap(att[0][1][7])
    ffn[0][1] = feed(0, (att[0][1][0], att[0][1][7], sent_own))
    sent_2 = swap(ffn[0][1][6])
    ffn[0][0] = feed(0, (att[0][0][0], att[0][0][7], sent_other))
    sent_1 = swap(ffn[0][0][6])
    att[1][0] = attend(1, 0, (ffn[0][0][0], ffn[0][0][6], sent_2))
    sent_own = swap(att[1][0][7])
    cot_other = swap(cot_own)
    att[1][1] = attend(1, 1, (ffn[0][1][0], ffn[0][1][6], sent_1))
    sent_other = swap(att[1][1][7])
    ffn[1][1] = feed(1, (att[1][1][0], att[1][1][7], sent_own), cot_other)
    back_2 = swap(ffn[1][1][7])
    block_sent = swap(ffn[1][1][6])
    ffn[1][0] = feed(1, (att[1][0][0], att[1][0][7], sent_other), cot_own, ffn[1][1][8])
    back_1 = swap(ffn[1][0][7])
    bits = groups.bit_length() - 1
    order = tuple(range(bits))
    turned = tuple(bit for bit in ATTENTION_1_ORDER if bit < bits)

    def ffn_grads(layer, low, hidden):
        normed = [ffn[layer][image][1] for image in range(2)]
        active = [ffn[layer][image][4] for image in range(2)]
        kept, sent, sums = weight_grads(
            top, groups, order, ((0, 0), (1, 1)), (*normed, *low), (*hidden, *active),
            (True, False), f"ffn_grads_{layer}", 4.4,
        )
        return Scatter(kept, sent, order, size, f"ffn_fold_{layer}"), sums

    def attention_grads(layer, low, mixed, order):
        normed = [att[layer][image][1] for image in range(2)]
        attended = [att[layer][image][6] for image in range(2)]
        kept, sent, sums = weight_grads(
            top, groups, order, ((0, 0), (1, 1)), (*normed, *low), (*mixed, *attended),
            (True, False), f"attention_grads_{layer}", 3,
        )
        return Scatter(kept, sent, order, size, f"attention_fold_{layer}"), sums

    def attend_back(layer, image, grads, prior=(), micros=5):
        held = att[layer][image]
        return attention_backward(
            layer, grads, ffn[layer][image][2], ffn[layer][image][3], vectors, held[2],
            held[4], held[5], matrix_in, attention_out, prior, micros,
        )

    def feed_back(image, grads, prior_sums=None, micros=4):
        held = att[1][image]
        return ffn_backward(
            0, grads, held[2], held[3], vectors, ffn[0][image][5], expand_weight,
            reduce_weight, prior_sums, micros,
        )

    ffn_sum_1, up_bias_1 = ffn_grads(1, (cot_own, cot_other), (ffn[1][0][5], ffn[1][1][5]))
    back = [[None, None], [None, None]]
    back[1][0] = attend_back(1, 0, (cot_own, ffn[1][0][7], back_2), (), WIDE)
    sent_own = swap(back[1][0][3])
    ffn_sum_1.step()
    back[1][1] = attend_back(1, 1, (cot_other, ffn[1][1][7], back_1), back[1][0][4:6])
    sent_other = swap(back[1][1][3])
    attention_sum_1, mixed_1 = attention_grads(
        1, (back[1][0][1], back[1][1][1]), (back[1][0][2], back[1][1][2]), turned
    )
    low = [None, None]
    low[1] = feed_back(1, (back[1][1][0], back[1][1][3], sent_own), None, WIDE)
    back_2 = swap(low[1][3])
    attention_sum_1.step()
    low[0] = feed_back(0, (back[1][0][0], back[1][0][3], sent_other), low[1][4])
    back_1 = swap(low[0][3])
    ffn_sum_0, up_bias_0 = ffn_grads(0, (low[0][1], low[1][1]), (low[0][2], low[1][2]))
    ffn_sum_1.step()
    back[0][0] = attend_back(0, 0, (low[0][0], low[0][3], back_2), (), WIDE)
    ffn_sum_0.step()
    back[0][1] = attend_back(0, 1, (low[1][0], low[1][3], back_1), back[0][0][4:6])
    last = swap(back[0][1][3])
    their_sums = swap(back[0][1][4])
    attention_sum_0, mixed_0 = attention_grads(
        0, (back[0][0][1], back[0][1][1]), (back[0][0][2], back[0][1][2]), order
    )
    attention_sum_1.step()
    block_output = finish(
        lambda *refs: output_body(1, *refs), BF16, "output", 10,
        ffn[1][0][0], ffn[1][0][6], block_sent, vectors,
    )
    pieces = (
        back[0][1][4], their_sums, low[0][4], back[1][1][4], ffn[1][0][8],
        up_bias_0, up_bias_1, mixed_0, mixed_1, back[0][1][5], back[1][1][5],
    )
    per_row = width // TURN
    count = layers * (6 + units // width + 1 + heads // per_row)
    packed = kernel_call(
        lambda *refs: pack_body(width, layers, refs),
        shape((-(-count // 8) * 8, width), F32),
        IN_VMEM,
        pieces,
        [IN_VMEM] * len(pieces),
        [],
        "pack",
        1,
    )
    total = Total(packed, size)
    ffn_sum_1.step()
    total.step()
    attention_sum_0.step()
    tokens_grad = finish(
        finish_body, F32, "finish", 1,
        back[0][0][0], back[0][0][3], last, att[0][0][2], att[0][0][3], vectors,
    )
    attention_sum_1.step()
    total.step()
    ffn_end_1 = ffn_sum_1.join()
    ffn_sum_0.step()
    attention_end_1 = attention_sum_1.join()
    total.step()
    attention_sum_0.step()
    ffn_sum_0.step()
    attention_sum_0.step()
    packed, found = total.finish()
    vector_grads, expand_bias_grad, pair_grad, table_grad = kernel_call(
        lambda *refs: unpack_body(refs),
        [
            shape((6, layers, width), F32),
            shape((layers, units), F32),
            shape((layers, 2, head_width), F32),
            shape((heads, layers, SPAN * SPAN), F32),
        ],
        [IN_VMEM] * 4,
        (packed, found),
        [IN_VMEM] * 2,
        [],
        "unpack",
        0.6,
    )

    rows = width // size
    up_grad, down_grad = collect(
        (ffn_sum_0.finish(), ffn_end_1), [(layers, rows, units)] * 2, "ffn_collect"
    )
    in_grad, out_grad = collect(
        (attention_sum_0.finish(), attention_end_1),
        [(layers, 3, rows, head_width), (layers, rows, head_width)],
        "attention_collect",
    )
    return (
        block_output,
        tokens_grad,
        jnp.transpose(in_grad, (0, 2, 1, 3)),
        jnp.transpose(out_grad, (0, 2, 1)),
        up_grad,
        jnp.transpose(down_grad, (0, 2, 1)),
        pair_grad,
        expand_bias_grad,
        jnp.transpose(table_grad, (1, 0, 2)),
        jnp.transpose(vector_grads, (1, 0, 2)),
    )


def solution(mesh):
    return jax.shard_map(
        shards,
        mesh=mesh,
        in_specs=(
            P(("dp", "mp"), None),
            P("dp", None),
            P(("dp", "mp"), None),
            P(),
            P(),
            P(None, None, None, "mp"),
            P(None, None, "mp"),
            P(None, "mp", None),
            P(None, "mp", None),
            P(),
            P(),
            P(),
            P(None, None, "mp"),
            P(None, "mp"),
            P(None, "mp", None),
            P(),
        ),
        out_specs=(
            P(("dp", "mp"), None),
            P(("dp", "mp"), None),
            P(None, "dp", None, "mp"),
            P(None, "mp", "dp"),
            P(None, "dp", "mp"),
            P(None, "mp", "dp"),
            P(None, None, "mp"),
            P(None, "mp"),
            P(None, "mp", None),
            P(),
        ),
        check_vma=False,
    )
```

```python
import jax
import jax.numpy as jnp
import numpy as np
from jax import lax
from jax.experimental import pallas as pl
from jax.experimental.pallas import tpu as pltpu
from jax.sharding import PartitionSpec as P

HEAD_DIM = 32
GRID = 14
WIN = 7
SHIFT = 3
PATCHES = 196
BLOCK = 98
SLOT = 128
KEYS = 112
LANES = 128
SPAN = 2 * WIN - 1
TURN = 256

EPSILON = 1e-05
MASKED = -1e30
F32 = jnp.float32
BF16 = jnp.bfloat16
VMEM_LIMIT = 14 * 1024 * 1024

IN_VMEM = pl.BlockSpec(memory_space=pltpu.VMEM)
IN_SMEM = pl.BlockSpec(memory_space=pltpu.SMEM)
ANYWHERE = pl.BlockSpec(memory_space=pl.ANY)
IN_HBM = pl.BlockSpec(memory_space=pltpu.HBM)


def shape(dims, kind):
    return jax.ShapeDtypeStruct(dims, kind)


LINE = []
COST = 1.0e9
PLAN = (
    "ffn_1_other",
    "ffn_1_own",
    "ffn_grads_1",
    "attention_back_1_own",
    "ffn_sum_1",
    "attention_back_1_other",
    "attention_grads_1",
    "ffn_back_0_other",
    "ffn_back_0_own",
    "ffn_grads_0",
    "attention_sum_1",
    "ffn_sum_1",
    "ffn_sum_0",
    "attention_back_0_own",
    "attention_sum_1",
    "attention_back_0_other",
    "attention_grads_0",
    "ffn_sum_1",
    "pack",
    "attention_sum_0",
    "ffn_sum_0",
    "ffn_end_1",
    "attention_sum_0",
    "attention_sum_1",
    "attention_sum_0",
    "tokens_grad",
    "ffn_sum_0",
    "total",
    "attention_end_1",
    "block_output",
    "attention_outputs",
    "total",
    "total",
    "ffn_outputs",
    "unpack",
)
MICROS = {
    "attention_back_1_own": 14.22,
    "attention_back_1_other": 0.06,
    "attention_grads_1": 0.81,
    "ffn_back_0_other": 1.81,
    "ffn_back_0_own": 0.26,
    "ffn_grads_0": 0.1,
    "attention_back_0_own": 0.36,
    "attention_back_0_other": 0.33,
    "attention_grads_0": 0.17,
    "pack": 0.44,
    "ffn_grads_1": 0.3,
}
PIECES = {"ffn": 3, "attention": 2}
BIT_ORDER = {
    "ffn_1": (0, 2, 1, 3),
    "attention_1": (0, 1, 2, 3),
    "ffn_0": (0, 2, 1, 3),
    "attention_0": (0, 1, 2, 3),
    "total": (0, 2, 1, 3),
}


def kernel_call(body, outs, out_specs, ins, in_specs, scratch, name, micros):
    behind = [item for item in LINE if not any(item is used for used in ins)]
    skipped = len(behind)
    ins = [
        pltpu.with_memory_space_constraint(item, pltpu.HBM) if spec is IN_HBM else item
        for item, spec in zip(ins, in_specs)
    ]
    found = pl.pallas_call(
        lambda *refs: body(*refs[skipped:]),
        out_shape=outs,
        in_specs=[ANYWHERE] * skipped + in_specs,
        out_specs=out_specs,
        scratch_shapes=scratch,
        compiler_params=pltpu.CompilerParams(vmem_limit_bytes=VMEM_LIMIT),
        cost_estimate=pl.CostEstimate(
            flops=int(micros * COST), bytes_accessed=1024, transcendentals=0
        ),
        name=name,
    )(*behind, *ins)
    LINE[:] = [min(jax.tree.leaves(found), key=lambda item: item.size)]
    return found


def dot_nn(left, right):
    return lax.dot_general(left, right, (((1,), (0,)), ((), ())), preferred_element_type=F32)


def dot_nt(left, right):
    return lax.dot_general(left, right, (((1,), (1,)), ((), ())), preferred_element_type=F32)


def dot_tn(left, right):
    return lax.dot_general(left, right, (((0,), (0,)), ((), ())), preferred_element_type=F32)


def dot_tt(left, right):
    return lax.dot_general(left, right, (((0,), (1,)), ((), ())), preferred_element_type=F32)


def dot_full(left, right, contracted):
    return lax.dot_general(
        left,
        right,
        (contracted, ((), ())),
        preferred_element_type=F32,
        precision=lax.Precision.HIGHEST,
    )


def place_matrix(layer):
    row = lax.broadcasted_iota(jnp.int32, (2 * SLOT, PATCHES), 0)
    patch = lax.broadcasted_iota(jnp.int32, (2 * SLOT, PATCHES), 1)
    second = row >= SLOT
    within = jnp.where(second, row - SLOT, row)
    found = within + jnp.where(second, BLOCK, 0) + layer * SHIFT * GRID
    found = jnp.where(found >= PATCHES, found - PATCHES, found)
    return jnp.where((within < BLOCK) & (found == patch), 1.0, 0.0).astype(BF16)


def window_matrix(layer, block):
    def groups(place):
        turned_row = (place * 147) >> 11
        col = place - turned_row * GRID
        row = turned_row + block * WIN + layer * SHIFT
        row = jnp.where(row >= GRID, row - GRID, row)

        def group(position):
            moved = position + layer * (WIN - SHIFT)
            return jnp.where(moved >= 2 * WIN, 2, jnp.where(moved >= WIN, 1, 0))

        return group(row) * 4 + group(col)

    key = lax.broadcasted_iota(jnp.int32, (KEYS, LANES), 0)
    query = lax.broadcasted_iota(jnp.int32, (KEYS, LANES), 1)
    return (groups(key) == groups(query)) & (key < BLOCK) & (query < BLOCK)


def offset_matrix():
    offset = lax.broadcasted_iota(jnp.int32, (SPAN * SPAN, TURN), 0)
    lane = lax.broadcasted_iota(jnp.int32, (SPAN * SPAN, TURN), 1)
    row = (offset * 79) >> 10
    place = offset - row * SPAN + row * GRID - (WIN - 1) * (GRID + 1)
    return jnp.where(jnp.where(place < 0, place + TURN, place) == lane, 1.0, 0.0)


def heads_apart(value):
    rows = value.shape[0]
    parts = []
    for member in range(rows // HEAD_DIM):
        start = member * HEAD_DIM
        pieces = [value[start : start + HEAD_DIM]]
        if start:
            pieces.insert(0, jnp.zeros((start, value.shape[1]), value.dtype))
        if start + HEAD_DIM < rows:
            pieces.append(jnp.zeros((rows - start - HEAD_DIM, value.shape[1]), value.dtype))
        parts.append(jnp.concatenate(pieces, axis=0))
    return jnp.concatenate(parts, axis=1)


def heads_together(value):
    count = value.shape[0] // HEAD_DIM
    columns = value.shape[1] // count
    return jnp.concatenate(
        [
            value[
                member * HEAD_DIM : (member + 1) * HEAD_DIM,
                member * columns : (member + 1) * columns,
            ]
            for member in range(count)
        ],
        axis=0,
    )


def norm_rows(stream, gain, shift):
    center = stream - jnp.mean(stream, axis=-1, keepdims=True)
    spread = jnp.mean(center * center, axis=-1, keepdims=True)
    rstd = lax.rsqrt(spread + EPSILON)
    x_hat = center * rstd
    return x_hat, rstd, (x_hat * gain + shift).astype(BF16)


def norm_back(grad_normed, x_hat, rstd, gain):
    scaled = grad_normed * gain
    term = jnp.mean(scaled, axis=-1, keepdims=True)
    along = jnp.mean(scaled * x_hat, axis=-1, keepdims=True)
    return rstd * (scaled - term - x_hat * along)


def column_sum(value):
    return jnp.sum(value, axis=0, keepdims=True)


def put_sums(out, prior, sums):
    for row, found in enumerate(sums):
        out[row : row + 1] = found if prior is None else found + prior[row : row + 1]
    out[len(sums) :] = jnp.zeros((out.shape[0] - len(sums), out.shape[1]), F32)


FIRST_GAIN, FIRST_SHIFT, ATTENTION_BIAS, SECOND_GAIN, SECOND_SHIFT, REDUCE_BIAS = range(6)


def vector_row(vectors, member, layer):
    row = member * (vectors.shape[0] // 6) + layer
    return vectors[row : row + 1]


def head_lanes(rows, member):
    lane = lax.broadcasted_iota(jnp.int32, (rows, LANES), 1)
    return (lane >= member * HEAD_DIM) & (lane < (member + 1) * HEAD_DIM)


def head_rows(value):
    rows = value.shape[0]
    return jnp.concatenate(
        [
            jnp.where(head_lanes(rows, member), value, jnp.zeros_like(value))
            for member in range(LANES // HEAD_DIM)
        ],
        axis=0,
    )


def tables_body(heads, layers, refs):
    half = refs[0]
    in_hbm, refs = refs[1:13], refs[13:]
    biases, refs = refs[:layers], refs[layers:]
    masks, refs = refs[: 2 * layers], refs[2 * layers :]
    keep_out, vectors_out = refs[:2]
    held = [refs[6], refs[7], *refs[2:6], *refs[8:14]]
    sems = refs[14]
    copies = []
    for index, (source, target) in enumerate(zip(in_hbm, held)):
        copies.append(pltpu.make_async_copy(source, target, sems.at[index]))
        copies[-1].start()
    table, keep = held[:2]
    same = lax.broadcasted_iota(jnp.int32, (KEYS, LANES), 0) == lax.broadcasted_iota(
        jnp.int32, (KEYS, LANES), 1
    )
    offsets = offset_matrix()
    per_group = LANES // HEAD_DIM
    for copy in copies:
        copy.wait()
    own_first = half[0] == 0
    rows = [keep[image : image + 1].astype(F32) for image in range(2)]
    pair = jnp.concatenate(
        [jnp.where(own_first, rows[0], rows[1]), jnp.where(own_first, rows[1], rows[0])], axis=0
    ).astype(BF16)
    for layer in range(layers):
        line = dot_full(table[:, layer], offsets, ((1,), (0,)))
        for head in range(heads):
            wide = jnp.broadcast_to(line[head : head + 1], (KEYS, TURN))
            lanes = head % per_group * LANES
            biases[layer][head // per_group, :, lanes : lanes + LANES] = pltpu.roll(
                wide, 0, 1, stride=1, stride_axis=0
            )[:, :LANES]
        place = place_matrix(layer)
        kept = dot_nt(place, pair)
        for block in range(2):
            window = window_matrix(layer, block)
            for image in range(2):
                column = kept[block * SLOT : block * SLOT + KEYS, image : image + 1]
                fine = window & ((column > 0.5) | same)
                masks[layer * 2 + image][block] = jnp.where(fine, 0.0, MASKED)
        if layer == 0:
            keep_out[...] = dot_tn(place, kept.astype(BF16))
    for index, item in enumerate(held[6:]):
        vectors_out[index * layers : (index + 1) * layers] = item[...]


def make_tables(half, position_table, keep_mask, moved, vectors):
    heads, layers, _ = position_table.shape
    groups = heads * HEAD_DIM // LANES
    width = vectors[0].shape[1]
    ins = (position_table, keep_mask, *moved, *vectors)
    outs = [shape((groups, KEYS, 4 * LANES), F32)] * layers + [shape((2, KEYS, LANES), F32)] * (
        2 * layers
    )
    outs += [
        shape((PATCHES, 2), F32),
        shape((len(vectors) * layers, width), F32),
        *[shape(item.shape, item.dtype) for item in moved],
    ]
    found = kernel_call(
        lambda *refs: tables_body(heads, layers, refs),
        outs,
        [IN_VMEM] * len(outs),
        (half, *ins),
        [IN_SMEM] + [IN_HBM] * len(ins),
        [pltpu.VMEM(item.shape, item.dtype) for item in (*ins[:2], *vectors)]
        + [pltpu.SemaphoreType.DMA((len(ins),))],
        "tables",
        1.6,
    )
    masks = [found[layers + 2 * layer : layers + 2 * layer + 2] for layer in range(layers)]
    return found[:layers], masks, found[3 * layers :]


def attention_body(layer, heads, chained, refs):
    if chained:
        base, mine, theirs = refs[:3]
        refs = refs[3:]
    else:
        base, refs = refs[0], refs[1:]
    vectors, pair_bias, bias, mask, in_hbm, out_hbm = refs[:6]
    refs = refs[6:]
    if chained:
        stream_out, refs = refs[0], refs[1:]
    normed_out, hat_out, rstd_out, qkv_out, weights_out, attended_out, partial_out = refs[:7]
    in_held, out_held, turned, sems = refs[7:]
    width = heads * HEAD_DIM
    fetch_in = pltpu.make_async_copy(in_hbm.at[layer], in_held, sems.at[0])
    fetch_out = pltpu.make_async_copy(out_hbm.at[layer], out_held, sems.at[1])
    fetch_in.start()
    fetch_out.start()
    stream = base[...].astype(F32)
    if chained:
        stream = (
            stream
            + (mine[...].astype(F32) + theirs[...].astype(F32))
            + vector_row(vectors, REDUCE_BIAS, layer - 1)
        )
        stream_out[...] = stream
    x_hat, rstd, normed = norm_rows(
        stream, vector_row(vectors, FIRST_GAIN, layer), vector_row(vectors, FIRST_SHIFT, layer)
    )
    normed_out[...] = normed
    hat_out[...] = x_hat.astype(BF16)
    rstd_out[...] = rstd
    place = place_matrix(layer)
    fetch_in.wait()
    parts = []
    for member in range(3):
        mixed = dot_nn(normed, in_held[member])
        if member != 1:
            mixed = mixed + pair_bias[layer, member // 2 : member // 2 + 1]
        parts.append(mixed.astype(BF16))
        qkv_out[:, member * width : (member + 1) * width] = parts[-1]
    queries = dot_tt(parts[0], place).astype(BF16)
    keys = dot_nn(place, parts[1]).astype(BF16)
    values = dot_tt(parts[2], place).astype(BF16)
    scale = HEAD_DIM ** (-0.5)
    groups = width // LANES
    for group in range(groups):
        lanes = slice(group * LANES, (group + 1) * LANES)
        for block in range(2):
            slots = slice(block * SLOT, (block + 1) * SLOT)
            own_keys = slice(block * SLOT, block * SLOT + KEYS)
            scores = dot_nn(keys[own_keys, lanes], heads_apart(queries[lanes, slots])) * scale
            scores = scores + bias[group] + jnp.concatenate([mask[block]] * 4, axis=1)
            raised = jnp.exp(scores - jnp.max(scores, axis=0, keepdims=True))
            weights = raised * (1.0 / jnp.sum(raised, axis=0, keepdims=True))
            weights = weights.astype(BF16)
            weights_out[group * 2 + block] = weights
            found = heads_together(dot_nn(values[lanes, own_keys], weights))
            turned[lanes, slots] = found.astype(BF16)
    attended = dot_tt(place, turned[...]).astype(BF16)
    attended_out[...] = attended
    fetch_out.wait()
    partial_out[...] = dot_nn(attended, out_held[...]).astype(BF16)


def attention_forward(layer, streams, vectors, pair_bias, bias, mask, matrix_in, matrix_out):
    chained = len(streams) > 1
    rows, width = streams[0].shape
    head_width = matrix_out.shape[1]
    heads = head_width // HEAD_DIM
    outs = [
        shape((rows, width), BF16),
        shape((rows, width), BF16),
        shape((rows, 1), F32),
        shape((rows, 3 * head_width), BF16),
        shape((2 * head_width // LANES, KEYS, 4 * LANES), BF16),
        shape((rows, head_width), BF16),
        shape((rows, width), BF16),
    ]
    if chained:
        outs = [shape((rows, width), F32)] + outs
    ins = (*streams, vectors, pair_bias, bias, mask, matrix_in, matrix_out)
    found = kernel_call(
        lambda *refs: attention_body(layer, heads, chained, refs),
        outs,
        [IN_VMEM] * len(outs),
        ins,
        [IN_VMEM] * (len(ins) - 2) + [IN_HBM] * 2,
        [
            pltpu.VMEM((3, width, head_width), BF16),
            pltpu.VMEM((head_width, width), BF16),
            pltpu.VMEM((head_width, 2 * SLOT), BF16),
            pltpu.SemaphoreType.DMA((2,)),
        ],
        f"attention_{layer}",
        4,
    )
    return found if chained else [streams[0], *found]


def gelu_parts(hidden):
    below = 0.5 * (1.0 + lax.erf(hidden * (0.5**0.5)))
    density = jnp.exp(-0.5 * hidden * hidden) * (0.5 / np.pi) ** 0.5
    return hidden * below, below + hidden * density


def fetch_slices(layer, step, up_hbm, down_hbm, up_held, down_held, sems):
    found = []
    for index in range(up_held.shape[1] // step):
        part = slice(index * step, (index + 1) * step)
        pair = (
            pltpu.make_async_copy(up_hbm.at[layer, :, part], up_held.at[:, part], sems.at[0, index]),
            pltpu.make_async_copy(down_hbm.at[layer, part], down_held.at[part], sems.at[1, index]),
        )
        for copy in pair:
            copy.start()
        found.append((part, *pair))
    return found


def ffn_body(layer, both, image, joined, step, refs):
    base, mine, theirs, vectors, up_bias = refs[:5]
    refs = refs[5:]
    if both:
        grad, keep, refs = refs[0], refs[1], refs[2:]
    if joined:
        prior_sums, refs = refs[0], refs[1:]
    up_hbm, down_hbm, *refs = refs
    if both:
        mid_out, normed_out, hat_out, rstd_out, active_out, slope_out, partial_out = refs[:7]
        back_out, sums_out, grad_out = refs[7:10]
        up_held, down_held, sems = refs[10:]
    else:
        mid_out, normed_out, hat_out, rstd_out, active_out, slope_out, partial_out = refs[:7]
        up_held, down_held, sems = refs[7:]
    slices = fetch_slices(layer, step, up_hbm, down_hbm, up_held, down_held, sems)
    mid = (
        base[...].astype(F32)
        + (mine[...].astype(F32) + theirs[...].astype(F32))
        + vector_row(vectors, ATTENTION_BIAS, layer)
    )
    mid_out[...] = mid
    x_hat, rstd, normed = norm_rows(
        mid, vector_row(vectors, SECOND_GAIN, layer), vector_row(vectors, SECOND_SHIFT, layer)
    )
    normed_out[...] = normed
    hat_out[...] = x_hat.astype(BF16)
    rstd_out[...] = rstd
    if both:
        grad_rows = (grad[...].astype(F32) * keep[:, image : image + 1]).astype(BF16)
        grad_out[...] = grad_rows
        put_sums(sums_out, prior_sums if joined else None, [column_sum(grad_rows.astype(F32))])
    forward, backward = None, None
    for part, fetch_up, fetch_down in slices:
        fetch_up.wait()
        fetch_down.wait()
        hidden = dot_nn(normed, up_held[:, part]) + up_bias[layer : layer + 1, part]
        active, slope = gelu_parts(hidden)
        active = active.astype(BF16)
        active_out[:, part] = active
        term = dot_nn(active, down_held[part])
        forward = term if forward is None else forward + term
        if both:
            grad_hidden = (slope * dot_nt(grad_rows, down_held[part])).astype(BF16)
            slope_out[:, part] = grad_hidden
            term = dot_nt(grad_hidden, up_held[:, part])
            backward = term if backward is None else backward + term
        else:
            slope_out[:, part] = slope.astype(BF16)
    partial_out[...] = forward.astype(BF16)
    if both:
        back_out[...] = backward.astype(BF16)


def ffn_forward(layer, image, streams, vectors, up_bias, up, down, grad=None, keep=None, prior_sums=None):
    rows, width = streams[0].shape
    units = up.shape[2]
    both = grad is not None
    outs = [
        shape((rows, width), F32),
        shape((rows, width), BF16),
        shape((rows, width), BF16),
        shape((rows, 1), F32),
        shape((rows, units), BF16),
        shape((rows, units), BF16),
        shape((rows, width), BF16),
    ]
    ins = [*streams, vectors, up_bias]
    if both:
        outs += [shape((rows, width), BF16), shape((8, width), F32), shape((rows, width), BF16)]
        ins += [grad, keep]
    joined = prior_sums is not None
    if joined:
        ins.append(prior_sums)
    specs = [IN_VMEM] * len(ins) + [IN_HBM] * 2
    return kernel_call(
        lambda *refs: ffn_body(layer, both, image, joined, units // 3, refs),
        outs,
        [IN_VMEM] * len(outs),
        (*ins, up, down),
        specs,
        [
            pltpu.VMEM((width, units), BF16),
            pltpu.VMEM((units, width), BF16),
            pltpu.SemaphoreType.DMA((2, 4)),
        ],
        f"ffn_both_{layer}" if both else f"ffn_{layer}",
        4.6 if both else 3,
    )


def ffn_back_body(layer, joined, step, refs):
    base, mine, theirs, hat, rstd, vectors, slope = refs[:7]
    refs = refs[7:]
    if joined:
        prior_sums, refs = refs[0], refs[1:]
    up_hbm, down_hbm = refs[:2]
    grad_out, low_out, hidden_out, partial_out, sums_out = refs[2:7]
    up_held, down_held, sems = refs[7:]
    slices = fetch_slices(layer, step, up_hbm, down_hbm, up_held, down_held, sems)
    grad_normed = mine[...].astype(F32) + theirs[...].astype(F32)
    x_hat = hat[...].astype(F32)
    grad = base[...] + norm_back(
        grad_normed, x_hat, rstd[...], vector_row(vectors, FIRST_GAIN, layer + 1)
    )
    grad_out[...] = grad
    low = grad.astype(BF16)
    low_out[...] = low
    sums = [column_sum(grad_normed * x_hat), column_sum(grad_normed), column_sum(grad)]
    put_sums(sums_out, prior_sums if joined else None, sums)
    backward = None
    for part, fetch_up, fetch_down in slices:
        fetch_down.wait()
        fetch_up.wait()
        grad_hidden = (slope[:, part].astype(F32) * dot_nt(low, down_held[part])).astype(BF16)
        hidden_out[:, part] = grad_hidden
        term = dot_nt(grad_hidden, up_held[:, part])
        backward = term if backward is None else backward + term
    partial_out[...] = backward.astype(BF16)


def ffn_backward(layer, grads, hat, rstd, vectors, slope, up, down, prior_sums=None, micros=4):
    rows, width = grads[0].shape
    units = up.shape[2]
    outs = [
        shape((rows, width), F32),
        shape((rows, width), BF16),
        shape((rows, units), BF16),
        shape((rows, width), BF16),
        shape((8, width), F32),
    ]
    ins = [*grads, hat, rstd, vectors, slope]
    joined = prior_sums is not None
    if joined:
        ins.append(prior_sums)
    return kernel_call(
        lambda *refs: ffn_back_body(layer, joined, units // 4, refs),
        outs,
        [IN_VMEM] * len(outs),
        (*ins, up, down),
        [IN_VMEM] * len(ins) + [IN_HBM] * 2,
        [
            pltpu.VMEM((width, units), BF16),
            pltpu.VMEM((units, width), BF16),
            pltpu.SemaphoreType.DMA((2, 4)),
        ],
        f"ffn_back_{layer}",
        micros,
    )


def attention_back_body(layer, heads, joined, refs):
    base, mine, theirs, hat, rstd, vectors, first_hat, qkv, weights = refs[:9]
    refs = refs[9:]
    if joined:
        prior_sums, prior_table = refs[:2]
        refs = refs[2:]
    in_hbm, out_hbm = refs[:2]
    grad_out, low_out, mixed_out, partial_out, sums_out, table_out = refs[2:8]
    in_held, out_held, turned, merged, diagonals, sems = refs[8:]
    width = heads * HEAD_DIM
    per_group = LANES // HEAD_DIM
    fetch_out = pltpu.make_async_copy(out_hbm.at[layer], out_held, sems.at[1])
    fetch_in = pltpu.make_async_copy(in_hbm.at[layer], in_held, sems.at[0])
    fetch_out.start()
    fetch_in.start()
    grad_normed = mine[...].astype(F32) + theirs[...].astype(F32)
    x_hat = hat[...].astype(F32)
    grad = base[...].astype(F32) + norm_back(
        grad_normed, x_hat, rstd[...], vector_row(vectors, SECOND_GAIN, layer)
    )
    grad_out[...] = grad
    low = grad.astype(BF16)
    low_out[...] = low
    sums = [column_sum(grad_normed * x_hat), column_sum(grad_normed), column_sum(grad)]
    place = place_matrix(layer)
    queries = dot_nn(place, qkv[:, :width]).astype(BF16)
    turned_keys = dot_tt(qkv[:, width : 2 * width], place).astype(BF16)
    values = dot_nn(place, qkv[:, 2 * width :]).astype(BF16)
    fetch_out.wait()
    grad_attended = dot_nt(low, out_held[...]).astype(BF16)
    grad_slots = dot_nn(place, grad_attended).astype(BF16)
    grad_turned = dot_tt(grad_attended, place).astype(BF16)
    scale = HEAD_DIM ** (-0.5)
    empty = jnp.zeros((SLOT - KEYS, LANES), BF16)
    for group in range(width // LANES):
        lanes = slice(group * LANES, (group + 1) * LANES)
        total = None
        for block in range(2):
            top_row = block * SLOT
            slots = slice(top_row, top_row + SLOT)
            own_keys = slice(top_row, top_row + KEYS)
            low_weights = weights[group * 2 + block]
            full = low_weights.astype(F32)
            grad_weights = dot_nn(values[own_keys, lanes], heads_apart(grad_turned[lanes, slots]))
            spread = jnp.sum(full * grad_weights, axis=0, keepdims=True)
            grad_scores = full * (grad_weights - spread)
            total = grad_scores if total is None else total + grad_scores
            grad_raw = (grad_scores * scale).astype(BF16)
            grad_query = heads_together(dot_nn(turned_keys[lanes, own_keys], grad_raw))
            grad_key = dot_nn(grad_raw, head_rows(queries[slots, lanes]))
            grad_value = dot_nn(low_weights, head_rows(grad_slots[slots, lanes]))
            turned[lanes, slots] = grad_query.astype(BF16)
            for at, found in ((0, grad_key), (width, grad_value)):
                columns = slice(at + group * LANES, at + (group + 1) * LANES)
                merged[own_keys, columns] = found.astype(BF16)
                merged[top_row + KEYS : top_row + SLOT, columns] = empty
        for member in range(per_group):
            head = group * per_group + member
            own = total[:, member * LANES : (member + 1) * LANES]
            wide = jnp.concatenate([own, jnp.zeros_like(own)], axis=1)
            line = None
            for start in range(0, KEYS, 8):
                rows = wide[start : start + 8]
                if start:
                    rows = pltpu.roll(rows, TURN - start, 1)
                line = rows if line is None else line + rows
            diagonals[head * 8 : head * 8 + 8] = line
    mixed = [dot_tt(place, turned[...]).astype(BF16)]
    both = dot_tn(place, merged[...]).astype(BF16)
    mixed += [both[:, :width], both[:, width:]]
    mixed_out[:, :width] = mixed[0]
    mixed_out[:, width:] = both
    fetch_in.wait()
    partial = dot_nt(mixed[0], in_held[0])
    partial = partial + dot_nt(mixed[1], in_held[1])
    partial = partial + dot_nt(mixed[2], in_held[2])
    partial_out[...] = partial.astype(BF16)
    sums += [column_sum(partial * first_hat[...].astype(F32)), column_sum(partial)]
    put_sums(sums_out, prior_sums if joined else None, sums)
    lines = diagonals[...]
    row = lax.broadcasted_iota(jnp.int32, lines.shape, 0)
    for bit in range(3):
        moved = pltpu.roll(lines, TURN - (1 << bit), 1)
        lines = jnp.where(((row >> bit) & 1) == 1, moved, lines)
    lines = jnp.sum(lines.reshape(heads, 8, TURN), axis=1)
    table = dot_full(lines, offset_matrix(), ((1,), (1,)))
    table_out[...] = table + prior_table[...] if joined else table


def attention_backward(
    layer, grads, hat, rstd, vectors, first_hat, qkv, weights, matrix_in, matrix_out,
    prior=(), micros=5,
):
    rows, width = grads[0].shape
    head_width = matrix_out.shape[1]
    heads = head_width // HEAD_DIM
    outs = [
        shape((rows, width), F32),
        shape((rows, width), BF16),
        shape((rows, 3 * head_width), BF16),
        shape((rows, width), BF16),
        shape((8, width), F32),
        shape((heads, SPAN * SPAN), F32),
    ]
    ins = (*grads, hat, rstd, vectors, first_hat, qkv, weights, *prior)
    return kernel_call(
        lambda *refs: attention_back_body(layer, heads, bool(prior), refs),
        outs,
        [IN_VMEM] * len(outs),
        (*ins, matrix_in, matrix_out),
        [IN_VMEM] * len(ins) + [IN_HBM] * 2,
        [
            pltpu.VMEM((3, width, head_width), BF16),
            pltpu.VMEM((head_width, width), BF16),
            pltpu.VMEM((head_width, 2 * SLOT), BF16),
            pltpu.VMEM((2 * SLOT, 2 * head_width), BF16),
            pltpu.VMEM((heads * 8, TURN), F32),
            pltpu.SemaphoreType.DMA((2,)),
        ],
        f"attention_back_{layer}",
        micros,
    )


def finish_body(base, mine, theirs, hat, rstd, vectors, out):
    grad_normed = mine[...].astype(F32) + theirs[...].astype(F32)
    out[...] = base[...] + norm_back(
        grad_normed, hat[...].astype(F32), rstd[...], vector_row(vectors, FIRST_GAIN, 0)
    )


def output_body(layer, base, mine, theirs, vectors, out):
    total = base[...] + (mine[...].astype(F32) + theirs[...].astype(F32))
    out[...] = (total + vector_row(vectors, REDUCE_BIAS, layer)).astype(BF16)


def finish(body, kind, name, micros, *ins):
    return kernel_call(
        body, shape(ins[0].shape, kind), IN_VMEM, ins, [IN_VMEM] * len(ins), [], name, micros
    )


def group_place(group, top, order):
    place = 0
    for step, bit in enumerate(order):
        place = place + ((((group >> bit) & 1) ^ ((top >> bit) & 1)) << (len(order) - 1 - step))
    return place


def grads_body(pairs, groups, order, step, summed, refs):
    top = refs[0][0]
    lefts = 1 + max(left for left, _ in pairs)
    rights = len(pairs)
    refs = refs[1:]
    left_refs, refs = refs[: 2 * lefts], refs[2 * lefts :]
    right_refs, refs = refs[: 2 * rights], refs[2 * rights :]
    keep_out, sums_out, held, turned, wide, sems = (refs[0], *refs[-5:])
    send_outs = refs[1:-5]
    rows = left_refs[0].shape[0]
    space = wide.shape[0] // 2
    empty = space - rows
    block = keep_out.shape[1]
    copies = []
    for left in range(lefts):
        for image in range(2):
            start = image * space
            turned[left, :, start + LANES : start + space] = jnp.zeros(
                (turned.shape[1], space - LANES), BF16
            )
            turned[left, :, start : start + rows] = left_refs[2 * left + image][...].T
    at = 0
    sum_at = 0
    for right, (left, _) in enumerate(pairs):
        columns = right_refs[2 * right].shape[1]
        for image in range(2):
            start = image * space
            wide[start : start + rows, :columns] = right_refs[2 * right + image][...]
            wide[start + rows : start + space, :columns] = jnp.zeros((empty, columns), BF16)
        if summed[right]:
            sums_out[0:1, sum_at : sum_at + columns] = column_sum(wide[:, :columns].astype(F32))
            sum_at += columns
        for first in range(0, columns, step):
            found = dot_nn(turned[left], wide[:, first : first + step]).astype(BF16)
            for group in range(groups):
                held[group_place(group, top, order), :, at : at + step] = found[
                    group * block : (group + 1) * block
                ]
            sent = at // send_outs[0].shape[2]
            inner = at - sent * send_outs[0].shape[2]
            for half, out in (
                (0, keep_out.at[:, :, at : at + step]),
                (1, send_outs[sent].at[:, :, inner : inner + step]),
            ):
                copy = pltpu.make_async_copy(
                    held.at[half * groups // 2 : (half + 1) * groups // 2, :, at : at + step],
                    out,
                    sems.at[half, at // step],
                )
                copy.start()
                copies.append(copy)
            at += step
    for copy in copies:
        copy.wait()


def weight_grads(top, groups, order, pairs, lefts, rights, summed, pieces, name, micros):
    width = lefts[0].shape[1]
    step = 512 if all(item.shape[1] % 512 == 0 for item in rights) else 384
    columns = sum(item.shape[1] for item in rights[::2])
    widest = max(item.shape[1] for item in rights)
    space = 2 * LANES
    summed_columns = sum(item.shape[1] for item, used in zip(rights[::2], summed) if used)
    outs = [
        shape((groups // 2, width // groups, columns), BF16),
        *[shape((groups // 2, width // groups, columns // pieces), BF16)] * pieces,
        shape((8, summed_columns), F32),
    ]
    count = 1 + max(left for left, _ in pairs)
    kept, *sent, sums = kernel_call(
        lambda *refs: grads_body(pairs, groups, order, step, summed, refs),
        outs,
        [ANYWHERE] * (1 + pieces) + [IN_VMEM],
        (top, *lefts, *rights),
        [IN_SMEM] + [IN_VMEM] * (len(lefts) + len(rights)),
        [
            pltpu.VMEM((groups, width // groups, columns), BF16),
            pltpu.VMEM((count, width, 2 * space), BF16),
            pltpu.VMEM((2 * space, widest), BF16),
            pltpu.SemaphoreType.DMA((2, columns // step)),
        ],
        name,
        micros,
    )
    return kept, sent, sums


def swap(value):
    return lax.ppermute(value, "mp", [(0, 1), (1, 0)])


def trade(value, bit, size):
    return lax.ppermute(value, "dp", [(source, source ^ bit) for source in range(size)])


def fold_body(kept, *refs):
    *pieces, keep_out, send_out = refs
    half = keep_out.shape[0]
    at = 0
    for found in pieces:
        columns = slice(at, at + found.shape[2])
        at += found.shape[2]
        for start, out in ((0, keep_out), (half, send_out)):
            for block in range(half):
                total = kept[start + block, :, columns].astype(F32) + found[start + block].astype(F32)
                out[block, :, columns] = total.astype(BF16)


def fold(kept, found, name):
    half = shape((kept.shape[0] // 2, *kept.shape[1:]), BF16)
    return kernel_call(
        fold_body, [half, half], [IN_VMEM] * 2, (kept, *found), [IN_VMEM] * (1 + len(found)), [],
        name, 0.1,
    )


class Scatter:
    def __init__(self, kept, sent, order, size, name):
        self.kept, self.sent, self.order, self.size, self.name = kept, sent, order, size, name
        self.finer = size >> len(order)
        self.level = 0
        self.send()

    def send(self):
        self.found = [
            trade(item, self.finer << self.order[self.level], self.size) for item in self.sent
        ]

    def step(self):
        if self.level + 1 < len(self.order):
            self.kept, sent = fold(self.kept, self.found, f"{self.name}_{self.level}")
            self.sent = [sent]
            self.level += 1
            self.send()

    def finish(self):
        for _ in self.order:
            self.step()
        kept, finer = self.kept, self.finer
        found = jnp.concatenate(self.found, axis=2) if len(self.found) > 1 else self.found[0]
        rank = lax.axis_index("dp")
        while finer > 1:
            finer //= 2
            held = (kept.astype(F32) + found.astype(F32)).astype(BF16)
            halves = held.reshape((2, 1, held.shape[1] // 2, held.shape[2]))
            mine = (rank // finer) % 2
            kept = lax.dynamic_index_in_dim(halves, mine, 0, keepdims=False)
            found = trade(lax.dynamic_index_in_dim(halves, 1 - mine, 0, keepdims=False), finer, self.size)
        return kept, found

    def join(self):
        kept, found = self.finish()
        return (
            kernel_call(
                add_body, shape(kept.shape, F32), IN_VMEM, (kept, found), [IN_VMEM] * 2, [],
                f"{self.name}_end", 0.1,
            ),
        )


def add_body(left, right, out):
    out[...] = left[...].astype(F32) + right[...].astype(F32)


def some_bits(name, size):
    bits = range(size.bit_length() - 1)
    listed = [bit for bit in BIT_ORDER[name] if bit in bits]
    return tuple(listed + [bit for bit in bits if bit not in listed])


class Total:
    def __init__(self, value, size):
        self.value, self.size = value, size
        self.left = [1 << bit for bit in some_bits("total", size)]
        self.send()

    def send(self):
        self.found = trade(self.value, self.left.pop(0), self.size)

    def step(self):
        if self.left:
            self.value = kernel_call(
                add_body, shape(self.value.shape, F32), IN_VMEM, (self.value, self.found),
                [IN_VMEM] * 2, [], "total", 0.1,
            )
            self.send()

    def finish(self):
        while self.left:
            self.step()
        return self.value, self.found


def collect_body(counts, widths, refs):
    outs = refs[sum(counts) :]
    for layer, count in enumerate(counts):
        total = refs[0][0].astype(F32)
        if count == 2:
            total = total + refs[1][0].astype(F32)
        refs = refs[count:]
        at = 0
        for out, parts in zip(outs, widths):
            for part in range(parts):
                columns = out.shape[-1]
                if len(out.shape) == 4:
                    out[layer, part] = total[:, at : at + columns]
                else:
                    out[layer] = total[:, at : at + columns]
                at += columns


def collect(pairs, shapes, name):
    flat = [item for pair in pairs for item in pair]
    counts = [len(pair) for pair in pairs]
    return kernel_call(
        lambda *refs: collect_body(
            counts, [dims[1] if len(dims) == 4 else 1 for dims in shapes], refs
        ),
        [shape(dims, F32) for dims in shapes],
        [IN_VMEM] * len(shapes),
        flat,
        [IN_VMEM] * len(flat),
        [],
        name,
        0.1,
    )


def pack_body(width, layers, refs):
    sums_0, theirs_0, sums_low, sums_1, last = refs[:5]
    ups, mixes, tables = refs[5 : 5 + layers], refs[5 + layers : 5 + 2 * layers], refs[5 + 2 * layers : -1]
    out = refs[-1]
    out[...] = jnp.zeros(out.shape, F32)
    out[0:2] = sums_0[3:5] + theirs_0[3:5]
    out[2:3] = sums_0[2:3]
    out[3:5] = sums_0[0:2]
    out[5:6] = sums_low[2:3]
    out[6:8] = sums_low[0:2]
    out[8:9] = sums_1[2:3]
    out[9:11] = sums_1[0:2]
    out[11:12] = last[0:1]
    row = 6 * layers
    for item in ups:
        for start in range(0, item.shape[1], width):
            out[row : row + 1] = item[0:1, start : start + width]
            row += 1
    third = mixes[0].shape[1] // 3
    for item in mixes:
        out[row : row + 1, :third] = item[0:1, :third]
        out[row : row + 1, third : 2 * third] = item[0:1, 2 * third :]
        row += 1
    for item in tables:
        heads, offsets = item.shape
        for head in range(heads):
            lane = head * TURN % width
            out[row : row + 1, lane : lane + offsets] = item[head : head + 1]
            if (head + 1) * TURN % width == 0:
                row += 1


def unpack_body(refs):
    packed, found, vectors, up_bias, pair_bias, tables = refs
    width = packed.shape[1]
    layers, units = up_bias.shape
    total = packed[...] + found[...]
    for layer in range(layers):
        for member in range(6):
            vectors[member, layer : layer + 1] = total[6 * layer + member : 6 * layer + member + 1]
    row = 6 * layers
    for layer in range(layers):
        for start in range(0, units, width):
            up_bias[layer : layer + 1, start : start + width] = total[row : row + 1]
            row += 1
    third = pair_bias.shape[2]
    for layer in range(layers):
        for member in range(2):
            pair_bias[layer, member : member + 1] = total[
                row : row + 1, member * third : (member + 1) * third
            ]
        row += 1
    heads, _, offsets = tables.shape
    for layer in range(layers):
        for head in range(heads):
            lane = head * TURN % width
            tables[head, layer : layer + 1] = total[row : row + 1, lane : lane + offsets]
            if (head + 1) * TURN % width == 0:
                row += 1


def shards(
    tokens,
    keep_mask,
    cotangent,
    first_gain,
    first_shift,
    attention_in,
    query_value_bias,
    position_table,
    attention_out,
    attention_bias,
    second_gain,
    second_shift,
    expand_weight,
    expand_bias,
    reduce_weight,
    reduce_bias,
):
    LINE.clear()
    size = lax.axis_size("dp")
    half = lax.axis_index("mp")
    groups = min(16, size)
    top = (lax.axis_index("dp") // (size // groups)).astype(jnp.int32).reshape(1)
    layers, width = first_gain.shape
    head_width = attention_out.shape[1]
    units = expand_weight.shape[2]
    heads = head_width // HEAD_DIM
    matrix_in = jnp.transpose(attention_in, (0, 2, 1, 3))
    own_half = half.astype(jnp.int32).reshape(1)
    bias, masks, (keep_columns, vectors, tokens, cotangent, up_bias, pair_bias) = make_tables(
        own_half, jnp.transpose(position_table, (1, 0, 2)), keep_mask,
        (tokens, cotangent, expand_bias, query_value_bias),
        (first_gain, first_shift, attention_bias, second_gain, second_shift, reduce_bias),
    )
    other_tokens = swap(tokens)
    other_cotangent = swap(cotangent)

    def attend(layer, image, streams):
        return attention_forward(
            layer, streams, vectors, pair_bias, bias[layer], masks[layer][image], matrix_in,
            attention_out,
        )

    def feed(layer, image, streams, grad=None, prior_sums=None):
        return ffn_forward(
            layer, image, streams, vectors, up_bias, expand_weight, reduce_weight, grad,
            keep_columns, prior_sums,
        )

    att, ffn = [[None, None], [None, None]], [[None, None], [None, None]]
    att[0][0] = attend(0, 0, (tokens,))
    sent_own = swap(att[0][0][7])
    att[0][1] = attend(0, 1, (other_tokens,))
    sent_other = swap(att[0][1][7])
    ffn[0][1] = feed(0, 1, (att[0][1][0], att[0][1][7], sent_own))
    sent_2 = swap(ffn[0][1][6])
    ffn[0][0] = feed(0, 0, (att[0][0][0], att[0][0][7], sent_other))
    sent_1 = swap(ffn[0][0][6])
    att[1][0] = attend(1, 0, (ffn[0][0][0], ffn[0][0][6], sent_2))
    sent_own = swap(att[1][0][7])
    att[1][1] = attend(1, 1, (ffn[0][1][0], ffn[0][1][6], sent_1))
    sent_other = swap(att[1][1][7])

    def ffn_grads(layer, low, hidden, name):
        normed = [ffn[layer][image][1] for image in range(2)]
        active = [ffn[layer][image][4] for image in range(2)]
        order = some_bits(f"ffn_{layer}", groups)
        kept, sent, sums = weight_grads(
            top, groups, order, ((0, 0), (1, 1)), (*normed, *low), (*hidden, *active),
            (True, False), PIECES["ffn"], name, MICROS[name],
        )
        return Scatter(kept, sent, order, size, f"ffn_fold_{layer}"), sums

    def attention_grads(layer, low, mixed, name):
        normed = [att[layer][image][1] for image in range(2)]
        attended = [att[layer][image][6] for image in range(2)]
        order = some_bits(f"attention_{layer}", groups)
        kept, sent, sums = weight_grads(
            top, groups, order, ((0, 0), (1, 1)), (*normed, *low), (*mixed, *attended),
            (True, False), PIECES["attention"], name, MICROS[name],
        )
        return Scatter(kept, sent, order, size, f"attention_fold_{layer}"), sums

    def attend_back(layer, image, grads, prior=(), micros=5):
        held = att[layer][image]
        return attention_backward(
            layer, grads, ffn[layer][image][2], ffn[layer][image][3], vectors, held[2],
            held[4], held[5], matrix_in, attention_out, prior, micros,
        )

    def feed_back(image, grads, prior_sums=None, micros=4):
        held = att[1][image]
        return ffn_backward(
            0, grads, held[2], held[3], vectors, ffn[0][image][5], expand_weight,
            reduce_weight, prior_sums, micros,
        )

    back, low = [[None, None], [None, None]], [None, None]
    sent, sums, extra, outs = {}, {}, {}, {}
    rows = width // size

    def ffn_1_other():
        ffn[1][1] = feed(1, 1, (att[1][1][0], att[1][1][7], sent_own), other_cotangent)
        sent["ffn_1_other"] = swap(ffn[1][1][7])
        sent["block"] = swap(ffn[1][1][6])

    def ffn_1_own():
        ffn[1][0] = feed(1, 0, (att[1][0][0], att[1][0][7], sent_other), cotangent, ffn[1][1][8])
        sent["ffn_1_own"] = swap(ffn[1][0][7])

    def ffn_grads_1():
        sums["ffn_sum_1"], extra["up_1"] = ffn_grads(
            1, (ffn[1][0][9], ffn[1][1][9]), (ffn[1][0][5], ffn[1][1][5]), "ffn_grads_1"
        )

    def attention_back_1_own():
        back[1][0] = attend_back(
            1, 0, (ffn[1][0][9], ffn[1][0][7], sent["ffn_1_other"]), (),
            MICROS["attention_back_1_own"],
        )
        sent["back_1_own"] = swap(back[1][0][3])

    def attention_back_1_other():
        back[1][1] = attend_back(
            1, 1, (ffn[1][1][9], ffn[1][1][7], sent["ffn_1_own"]), back[1][0][4:6],
            MICROS["attention_back_1_other"],
        )
        sent["back_1_other"] = swap(back[1][1][3])

    def attention_grads_1():
        sums["attention_sum_1"], extra["mixed_1"] = attention_grads(
            1, (back[1][0][1], back[1][1][1]), (back[1][0][2], back[1][1][2]), "attention_grads_1"
        )

    def ffn_back_0_other():
        low[1] = feed_back(
            1, (back[1][1][0], back[1][1][3], sent["back_1_own"]), None, MICROS["ffn_back_0_other"]
        )
        sent["low_other"] = swap(low[1][3])

    def ffn_back_0_own():
        low[0] = feed_back(
            0, (back[1][0][0], back[1][0][3], sent["back_1_other"]), low[1][4],
            MICROS["ffn_back_0_own"],
        )
        sent["low_own"] = swap(low[0][3])

    def ffn_grads_0():
        sums["ffn_sum_0"], extra["up_0"] = ffn_grads(
            0, (low[0][1], low[1][1]), (low[0][2], low[1][2]), "ffn_grads_0"
        )

    def attention_back_0_own():
        back[0][0] = attend_back(
            0, 0, (low[0][0], low[0][3], sent["low_other"]), (), MICROS["attention_back_0_own"]
        )

    def attention_back_0_other():
        back[0][1] = attend_back(
            0, 1, (low[1][0], low[1][3], sent["low_own"]), back[0][0][4:6],
            MICROS["attention_back_0_other"],
        )
        sent["last"] = swap(back[0][1][3])
        sent["sums"] = swap(back[0][1][4])

    def attention_grads_0():
        sums["attention_sum_0"], extra["mixed_0"] = attention_grads(
            0, (back[0][0][1], back[0][1][1]), (back[0][0][2], back[0][1][2]), "attention_grads_0"
        )

    def pack():
        pieces = (
            back[0][1][4], sent["sums"], low[0][4], back[1][1][4], ffn[1][0][8],
            extra["up_0"], extra["up_1"], extra["mixed_0"], extra["mixed_1"],
            back[0][1][5], back[1][1][5],
        )
        per_row = width // TURN
        count = layers * (6 + units // width + 1 + heads // per_row)
        packed = kernel_call(
            lambda *refs: pack_body(width, layers, refs),
            shape((-(-count // 8) * 8, width), F32),
            IN_VMEM,
            pieces,
            [IN_VMEM] * len(pieces),
            [],
            "pack",
            MICROS["pack"],
        )
        sums["total"] = Total(packed, size)

    def unpack():
        outs["small"] = kernel_call(
            lambda *refs: unpack_body(refs),
            [
                shape((6, layers, width), F32),
                shape((layers, units), F32),
                shape((layers, 2, head_width), F32),
                shape((heads, layers, SPAN * SPAN), F32),
            ],
            [IN_VMEM] * 4,
            sums["total"].finish(),
            [IN_VMEM] * 2,
            [],
            "unpack",
            0.1,
        )

    def tokens_grad():
        outs["tokens_grad"] = finish(
            finish_body, F32, "finish", 0.1,
            back[0][0][0], back[0][0][3], sent["last"], att[0][0][2], att[0][0][3], vectors,
        )

    def block_output():
        outs["block_output"] = finish(
            lambda *refs: output_body(1, *refs), BF16, "output", 0.1,
            ffn[1][0][0], ffn[1][0][6], sent["block"], vectors,
        )

    def attention_end_1():
        extra["attention_1"] = sums["attention_sum_1"].join()

    def ffn_end_1():
        extra["ffn_1"] = sums["ffn_sum_1"].join()

    def attention_outputs():
        outs["attention"] = collect(
            (sums["attention_sum_0"].finish(), extra["attention_1"]),
            [(layers, 3, rows, head_width), (layers, rows, head_width)],
            "attention_collect",
        )

    def ffn_outputs():
        outs["ffn"] = collect(
            (sums["ffn_sum_0"].finish(), extra["ffn_1"]), [(layers, rows, units)] * 2, "ffn_collect"
        )

    steps = {
        item.__name__: item
        for item in (
            ffn_1_other, ffn_1_own, ffn_grads_1, attention_back_1_own, attention_back_1_other,
            attention_grads_1, ffn_back_0_other, ffn_back_0_own, ffn_grads_0,
            attention_back_0_own, attention_back_0_other, attention_grads_0, pack, unpack,
            tokens_grad, block_output, attention_end_1, ffn_end_1, attention_outputs, ffn_outputs,
        )
    }
    for name in PLAN:
        if name in steps:
            steps[name]()
        else:
            sums[name].step()

    in_grad, out_grad = outs["attention"]
    up_grad, down_grad = outs["ffn"]
    vector_grads, expand_bias_grad, pair_grad, table_grad = outs["small"]
    return (
        outs["block_output"],
        outs["tokens_grad"],
        jnp.transpose(in_grad, (0, 2, 1, 3)),
        jnp.transpose(out_grad, (0, 2, 1)),
        up_grad,
        jnp.transpose(down_grad, (0, 2, 1)),
        pair_grad,
        expand_bias_grad,
        jnp.transpose(table_grad, (1, 0, 2)),
        jnp.transpose(vector_grads, (1, 0, 2)),
    )


def solution(mesh):
    return jax.shard_map(
        shards,
        mesh=mesh,
        in_specs=(
            P(("dp", "mp"), None),
            P("dp", None),
            P(("dp", "mp"), None),
            P(),
            P(),
            P(None, None, None, "mp"),
            P(None, None, "mp"),
            P(None, "mp", None),
            P(None, "mp", None),
            P(),
            P(),
            P(),
            P(None, None, "mp"),
            P(None, "mp"),
            P(None, "mp", None),
            P(),
        ),
        out_specs=(
            P(("dp", "mp"), None),
            P(("dp", "mp"), None),
            P(None, "dp", None, "mp"),
            P(None, "mp", "dp"),
            P(None, "dp", "mp"),
            P(None, "mp", "dp"),
            P(None, None, "mp"),
            P(None, "mp"),
            P(None, "mp", None),
            P(),
        ),
        check_vma=False,
    )
```

```python
import jax
import jax.numpy as jnp
import numpy as np
from jax import lax
from jax.experimental import pallas as pl
from jax.experimental.pallas import tpu as pltpu
from jax.sharding import PartitionSpec as P

HEAD_DIM = 32
GRID = 14
WIN = 7
SHIFT = 3
PATCHES = 196
BLOCK = 98
SLOT = 128
KEYS = 112
LANES = 128
SPAN = 2 * WIN - 1
TURN = 256

EPSILON = 1e-05
MASKED = -1e30
F32 = jnp.float32
BF16 = jnp.bfloat16
VMEM_LIMIT = 14 * 1024 * 1024

IN_VMEM = pl.BlockSpec(memory_space=pltpu.VMEM)
IN_SMEM = pl.BlockSpec(memory_space=pltpu.SMEM)
ANYWHERE = pl.BlockSpec(memory_space=pl.ANY)
IN_HBM = pl.BlockSpec(memory_space=pltpu.HBM)


def shape(dims, kind):
    return jax.ShapeDtypeStruct(dims, kind)


def far(dims, kind):
    return pltpu.HBM(dims, kind)


class Saver:
    def __init__(self, held, outs, sems):
        self.held, self.outs, self.sems = held, outs, sems
        self.copies = []

    def put(self, index, value):
        self.held[index][...] = value
        self.start(index)

    def start(self, index):
        copy = pltpu.make_async_copy(self.held[index], self.outs[index], self.sems.at[index])
        copy.start()
        self.copies.append(copy)

    def wait(self):
        for copy in self.copies:
            copy.wait()


class Loader:
    def __init__(self, sources, held, sems):
        self.held = held
        self.copies = [
            pltpu.make_async_copy(source, target, sems.at[index])
            for index, (source, target) in enumerate(zip(sources, held))
        ]
        self.waiting = set(range(len(held)))
        for copy in self.copies:
            copy.start()

    def get(self, index):
        if index in self.waiting:
            self.waiting.remove(index)
            self.copies[index].wait()
        return self.held[index]


LINE = []
COST = 1.0e9
PLAN = (
    "ffn_1_other",
    "ffn_1_own",
    "ffn_grads_1",
    "attention_back_1_own",
    "ffn_sum_1",
    "attention_back_1_other",
    "attention_grads_1",
    "ffn_back_0_other",
    "ffn_back_0_own",
    "ffn_grads_0",
    "attention_sum_1",
    "ffn_sum_1",
    "ffn_sum_0",
    "attention_back_0_own",
    "attention_sum_1",
    "attention_back_0_other",
    "attention_grads_0",
    "ffn_sum_1",
    "pack",
    "attention_sum_0",
    "ffn_sum_0",
    "ffn_end_1",
    "attention_sum_0",
    "attention_sum_1",
    "attention_sum_0",
    "tokens_grad",
    "ffn_sum_0",
    "total",
    "attention_end_1",
    "block_output",
    "attention_outputs",
    "total",
    "total",
    "ffn_outputs",
    "unpack",
)
MICROS = {
    "attention_back_1_own": 14.22,
    "attention_back_1_other": 0.06,
    "attention_grads_1": 0.81,
    "ffn_back_0_other": 1.81,
    "ffn_back_0_own": 0.26,
    "ffn_grads_0": 0.1,
    "attention_back_0_own": 0.36,
    "attention_back_0_other": 0.33,
    "attention_grads_0": 0.17,
    "pack": 0.44,
    "ffn_grads_1": 0.3,
}
PIECES = {"ffn": 3, "attention": 2}
BIT_ORDER = {
    "ffn_1": (0, 2, 1, 3),
    "attention_1": (0, 1, 2, 3),
    "ffn_0": (0, 2, 1, 3),
    "attention_0": (0, 1, 2, 3),
    "total": (0, 2, 1, 3),
}


def kernel_call(body, outs, out_specs, ins, in_specs, scratch, name, micros, also=(), limit=None):
    behind = [item for item in (*LINE, *also) if not any(item is used for used in ins)]
    skipped = len(behind)
    ins = [
        pltpu.with_memory_space_constraint(item, pltpu.HBM) if spec is IN_HBM else item
        for item, spec in zip(ins, in_specs)
    ]
    found = pl.pallas_call(
        lambda *refs: body(*refs[skipped:]),
        out_shape=outs,
        in_specs=[ANYWHERE] * skipped + in_specs,
        out_specs=out_specs,
        scratch_shapes=scratch,
        compiler_params=pltpu.CompilerParams(vmem_limit_bytes=limit or VMEM_LIMIT),
        cost_estimate=pl.CostEstimate(
            flops=int(micros * COST), bytes_accessed=1024, transcendentals=0
        ),
        name=name,
    )(*behind, *ins)
    near = [
        item
        for item, kind in zip(jax.tree.leaves(found), jax.tree.leaves(outs))
        if isinstance(kind, jax.ShapeDtypeStruct)
    ]
    if near:
        LINE[:] = [min(near, key=lambda item: item.size)]
    else:
        LINE[:] = [pltpu.with_memory_space_constraint(jax.tree.leaves(found)[0], pltpu.HBM)]
    return found


def dot_nn(left, right):
    return lax.dot_general(left, right, (((1,), (0,)), ((), ())), preferred_element_type=F32)


def dot_nt(left, right):
    return lax.dot_general(left, right, (((1,), (1,)), ((), ())), preferred_element_type=F32)


def dot_tn(left, right):
    return lax.dot_general(left, right, (((0,), (0,)), ((), ())), preferred_element_type=F32)


def dot_tt(left, right):
    return lax.dot_general(left, right, (((0,), (1,)), ((), ())), preferred_element_type=F32)


def dot_full(left, right, contracted):
    return lax.dot_general(
        left,
        right,
        (contracted, ((), ())),
        preferred_element_type=F32,
        precision=lax.Precision.HIGHEST,
    )


def place_matrix(layer):
    row = lax.broadcasted_iota(jnp.int32, (2 * SLOT, PATCHES), 0)
    patch = lax.broadcasted_iota(jnp.int32, (2 * SLOT, PATCHES), 1)
    second = row >= SLOT
    within = jnp.where(second, row - SLOT, row)
    found = within + jnp.where(second, BLOCK, 0) + layer * SHIFT * GRID
    found = jnp.where(found >= PATCHES, found - PATCHES, found)
    return jnp.where((within < BLOCK) & (found == patch), 1.0, 0.0).astype(BF16)


def window_matrix(layer, block):
    def groups(place):
        turned_row = (place * 147) >> 11
        col = place - turned_row * GRID
        row = turned_row + block * WIN + layer * SHIFT
        row = jnp.where(row >= GRID, row - GRID, row)

        def group(position):
            moved = position + layer * (WIN - SHIFT)
            return jnp.where(moved >= 2 * WIN, 2, jnp.where(moved >= WIN, 1, 0))

        return group(row) * 4 + group(col)

    key = lax.broadcasted_iota(jnp.int32, (KEYS, LANES), 0)
    query = lax.broadcasted_iota(jnp.int32, (KEYS, LANES), 1)
    return (groups(key) == groups(query)) & (key < BLOCK) & (query < BLOCK)


def offset_matrix():
    offset = lax.broadcasted_iota(jnp.int32, (SPAN * SPAN, TURN), 0)
    lane = lax.broadcasted_iota(jnp.int32, (SPAN * SPAN, TURN), 1)
    row = (offset * 79) >> 10
    place = offset - row * SPAN + row * GRID - (WIN - 1) * (GRID + 1)
    return jnp.where(jnp.where(place < 0, place + TURN, place) == lane, 1.0, 0.0)


def heads_apart(value):
    rows = value.shape[0]
    parts = []
    for member in range(rows // HEAD_DIM):
        start = member * HEAD_DIM
        pieces = [value[start : start + HEAD_DIM]]
        if start:
            pieces.insert(0, jnp.zeros((start, value.shape[1]), value.dtype))
        if start + HEAD_DIM < rows:
            pieces.append(jnp.zeros((rows - start - HEAD_DIM, value.shape[1]), value.dtype))
        parts.append(jnp.concatenate(pieces, axis=0))
    return jnp.concatenate(parts, axis=1)


def heads_together(value):
    count = value.shape[0] // HEAD_DIM
    columns = value.shape[1] // count
    return jnp.concatenate(
        [
            value[
                member * HEAD_DIM : (member + 1) * HEAD_DIM,
                member * columns : (member + 1) * columns,
            ]
            for member in range(count)
        ],
        axis=0,
    )


def norm_rows(stream, gain, shift):
    center = stream - jnp.mean(stream, axis=-1, keepdims=True)
    spread = jnp.mean(center * center, axis=-1, keepdims=True)
    rstd = lax.rsqrt(spread + EPSILON)
    x_hat = center * rstd
    return x_hat, rstd, (x_hat * gain + shift).astype(BF16)


def norm_back(grad_normed, x_hat, rstd, gain):
    scaled = grad_normed * gain
    term = jnp.mean(scaled, axis=-1, keepdims=True)
    along = jnp.mean(scaled * x_hat, axis=-1, keepdims=True)
    return rstd * (scaled - term - x_hat * along)


def column_sum(value):
    return jnp.sum(value, axis=0, keepdims=True)


def put_sums(out, prior, sums):
    for row, found in enumerate(sums):
        out[row : row + 1] = found if prior is None else found + prior[row : row + 1]
    out[len(sums) :] = jnp.zeros((out.shape[0] - len(sums), out.shape[1]), F32)


FIRST_GAIN, FIRST_SHIFT, ATTENTION_BIAS, SECOND_GAIN, SECOND_SHIFT, REDUCE_BIAS = range(6)


def vector_row(vectors, member, layer):
    row = member * (vectors.shape[0] // 6) + layer
    return vectors[row : row + 1]


def head_lanes(rows, member):
    lane = lax.broadcasted_iota(jnp.int32, (rows, LANES), 1)
    return (lane >= member * HEAD_DIM) & (lane < (member + 1) * HEAD_DIM)


def head_rows(value):
    rows = value.shape[0]
    return jnp.concatenate(
        [
            jnp.where(head_lanes(rows, member), value, jnp.zeros_like(value))
            for member in range(LANES // HEAD_DIM)
        ],
        axis=0,
    )


def tables_body(heads, layers, refs):
    half = refs[0]
    in_hbm, refs = refs[1:13], refs[13:]
    biases, refs = refs[:layers], refs[layers:]
    masks, refs = refs[: 2 * layers], refs[2 * layers :]
    keep_out, vectors_out = refs[:2]
    held = [refs[6], refs[7], *refs[2:6], *refs[8:14]]
    sems = refs[14]
    copies = []
    for index, (source, target) in enumerate(zip(in_hbm, held)):
        copies.append(pltpu.make_async_copy(source, target, sems.at[index]))
        copies[-1].start()
    table, keep = held[:2]
    same = lax.broadcasted_iota(jnp.int32, (KEYS, LANES), 0) == lax.broadcasted_iota(
        jnp.int32, (KEYS, LANES), 1
    )
    offsets = offset_matrix()
    per_group = LANES // HEAD_DIM
    for copy in copies:
        copy.wait()
    own_first = half[0] == 0
    rows = [keep[image : image + 1].astype(F32) for image in range(2)]
    pair = jnp.concatenate(
        [jnp.where(own_first, rows[0], rows[1]), jnp.where(own_first, rows[1], rows[0])], axis=0
    ).astype(BF16)
    for layer in range(layers):
        line = dot_full(table[:, layer], offsets, ((1,), (0,)))
        for head in range(heads):
            wide = jnp.broadcast_to(line[head : head + 1], (KEYS, TURN))
            lanes = head % per_group * LANES
            biases[layer][head // per_group, :, lanes : lanes + LANES] = pltpu.roll(
                wide, 0, 1, stride=1, stride_axis=0
            )[:, :LANES]
        place = place_matrix(layer)
        kept = dot_nt(place, pair)
        for block in range(2):
            window = window_matrix(layer, block)
            for image in range(2):
                column = kept[block * SLOT : block * SLOT + KEYS, image : image + 1]
                fine = window & ((column > 0.5) | same)
                masks[layer * 2 + image][block] = jnp.where(fine, 0.0, MASKED)
        if layer == 0:
            keep_out[...] = dot_tn(place, kept.astype(BF16))
    for index, item in enumerate(held[6:]):
        vectors_out[index * layers : (index + 1) * layers] = item[...]


def make_tables(half, position_table, keep_mask, moved, vectors):
    heads, layers, _ = position_table.shape
    groups = heads * HEAD_DIM // LANES
    width = vectors[0].shape[1]
    ins = (position_table, keep_mask, *moved, *vectors)
    outs = [shape((groups, KEYS, 4 * LANES), F32)] * layers + [shape((2, KEYS, LANES), F32)] * (
        2 * layers
    )
    outs += [
        shape((PATCHES, 2), F32),
        shape((len(vectors) * layers, width), F32),
        *[shape(item.shape, item.dtype) for item in moved],
    ]
    found = kernel_call(
        lambda *refs: tables_body(heads, layers, refs),
        outs,
        [IN_VMEM] * len(outs),
        (half, *ins),
        [IN_SMEM] + [IN_HBM] * len(ins),
        [pltpu.VMEM(item.shape, item.dtype) for item in (*ins[:2], *vectors)]
        + [pltpu.SemaphoreType.DMA((len(ins),))],
        "tables",
        1.6,
    )
    masks = [found[layers + 2 * layer : layers + 2 * layer + 2] for layer in range(layers)]
    return found[:layers], masks, found[3 * layers :]


def attention_body(layer, heads, chained, refs):
    if chained:
        base, mine, theirs = refs[:3]
        refs = refs[3:]
    else:
        base, refs = refs[0], refs[1:]
    vectors, pair_bias, bias, mask, in_hbm, out_hbm = refs[:6]
    refs = refs[6:]
    if chained:
        stream_out, refs = refs[0], refs[1:]
    hat_out, rstd_out, partial_out = refs[1], refs[2], refs[6]
    in_held, out_held, turned, sems = refs[7:11]
    save = Saver(refs[11:15], (refs[0], refs[3], refs[4], refs[5]), refs[15])
    qkv_out, weights_out = save.held[1:3]
    width = heads * HEAD_DIM
    fetch_in = pltpu.make_async_copy(in_hbm.at[layer], in_held, sems.at[0])
    fetch_out = pltpu.make_async_copy(out_hbm.at[layer], out_held, sems.at[1])
    fetch_in.start()
    fetch_out.start()
    stream = base[...].astype(F32)
    if chained:
        stream = (
            stream
            + (mine[...].astype(F32) + theirs[...].astype(F32))
            + vector_row(vectors, REDUCE_BIAS, layer - 1)
        )
        stream_out[...] = stream
    x_hat, rstd, normed = norm_rows(
        stream, vector_row(vectors, FIRST_GAIN, layer), vector_row(vectors, FIRST_SHIFT, layer)
    )
    save.put(0, normed)
    hat_out[...] = x_hat.astype(BF16)
    rstd_out[...] = rstd
    place = place_matrix(layer)
    fetch_in.wait()
    parts = []
    for member in range(3):
        mixed = dot_nn(normed, in_held[member])
        if member != 1:
            mixed = mixed + pair_bias[layer, member // 2 : member // 2 + 1]
        parts.append(mixed.astype(BF16))
        qkv_out[:, member * width : (member + 1) * width] = parts[-1]
    save.start(1)
    queries = dot_tt(parts[0], place).astype(BF16)
    keys = dot_nn(place, parts[1]).astype(BF16)
    values = dot_tt(parts[2], place).astype(BF16)
    scale = HEAD_DIM ** (-0.5)
    groups = width // LANES
    for group in range(groups):
        lanes = slice(group * LANES, (group + 1) * LANES)
        for block in range(2):
            slots = slice(block * SLOT, (block + 1) * SLOT)
            own_keys = slice(block * SLOT, block * SLOT + KEYS)
            scores = dot_nn(keys[own_keys, lanes], heads_apart(queries[lanes, slots])) * scale
            scores = scores + bias[group] + jnp.concatenate([mask[block]] * 4, axis=1)
            raised = jnp.exp(scores - jnp.max(scores, axis=0, keepdims=True))
            weights = raised * (1.0 / jnp.sum(raised, axis=0, keepdims=True))
            weights = weights.astype(BF16)
            weights_out[group * 2 + block] = weights
            found = heads_together(dot_nn(values[lanes, own_keys], weights))
            turned[lanes, slots] = found.astype(BF16)
    attended = dot_tt(place, turned[...]).astype(BF16)
    save.start(2)
    save.put(3, attended)
    fetch_out.wait()
    partial_out[...] = dot_nn(attended, out_held[...]).astype(BF16)
    save.wait()


def attention_forward(layer, streams, vectors, pair_bias, bias, mask, matrix_in, matrix_out, also=()):
    chained = len(streams) > 1
    rows, width = streams[0].shape
    head_width = matrix_out.shape[1]
    heads = head_width // HEAD_DIM
    saved = [
        (rows, width),
        (rows, 3 * head_width),
        (2 * head_width // LANES, KEYS, 4 * LANES),
        (rows, head_width),
    ]
    outs = [
        far(saved[0], BF16),
        shape((rows, width), BF16),
        shape((rows, 1), F32),
        *[far(dims, BF16) for dims in saved[1:]],
        shape((rows, width), BF16),
    ]
    out_specs = [IN_HBM, IN_VMEM, IN_VMEM, IN_HBM, IN_HBM, IN_HBM, IN_VMEM]
    if chained:
        outs = [shape((rows, width), F32)] + outs
        out_specs = [IN_VMEM] + out_specs
    ins = (*streams, vectors, pair_bias, bias, mask, matrix_in, matrix_out)
    found = kernel_call(
        lambda *refs: attention_body(layer, heads, chained, refs),
        outs,
        out_specs,
        ins,
        [IN_VMEM] * (len(ins) - 2) + [IN_HBM] * 2,
        [
            pltpu.VMEM((3, width, head_width), BF16),
            pltpu.VMEM((head_width, width), BF16),
            pltpu.VMEM((head_width, 2 * SLOT), BF16),
            pltpu.SemaphoreType.DMA((2,)),
            *[pltpu.VMEM(dims, BF16) for dims in saved],
            pltpu.SemaphoreType.DMA((4,)),
        ],
        f"attention_{layer}",
        4,
        also,
    )
    return found if chained else [streams[0], *found]


def gelu_parts(hidden):
    below = 0.5 * (1.0 + lax.erf(hidden * (0.5**0.5)))
    density = jnp.exp(-0.5 * hidden * hidden) * (0.5 / np.pi) ** 0.5
    return hidden * below, below + hidden * density


def fetch_slices(layer, step, up_hbm, down_hbm, up_held, down_held, sems):
    found = []
    for index in range(up_held.shape[1] // step):
        part = slice(index * step, (index + 1) * step)
        pair = (
            pltpu.make_async_copy(up_hbm.at[layer, :, part], up_held.at[:, part], sems.at[0, index]),
            pltpu.make_async_copy(down_hbm.at[layer, part], down_held.at[part], sems.at[1, index]),
        )
        for copy in pair:
            copy.start()
        found.append((part, *pair))
    return found


def ffn_body(layer, both, image, joined, step, refs):
    base, mine, theirs, vectors, up_bias = refs[:5]
    refs = refs[5:]
    if both:
        grad, keep, refs = refs[0], refs[1], refs[2:]
    if joined:
        prior_sums, refs = refs[0], refs[1:]
    up_hbm, down_hbm, *refs = refs
    mid_out, hat_out, rstd_out, partial_out = refs[0], refs[2], refs[3], refs[6]
    far_outs = (refs[1], refs[4], refs[5])
    if both:
        back_out, sums_out, grad_out = refs[7:10]
    up_held, down_held, sems, *held = refs[10 if both else 7 :]
    save = Saver(held[:3], far_outs, held[3])
    active_out, slope_out = save.held[1:]
    slices = fetch_slices(layer, step, up_hbm, down_hbm, up_held, down_held, sems)
    mid = (
        base[...].astype(F32)
        + (mine[...].astype(F32) + theirs[...].astype(F32))
        + vector_row(vectors, ATTENTION_BIAS, layer)
    )
    mid_out[...] = mid
    x_hat, rstd, normed = norm_rows(
        mid, vector_row(vectors, SECOND_GAIN, layer), vector_row(vectors, SECOND_SHIFT, layer)
    )
    save.put(0, normed)
    hat_out[...] = x_hat.astype(BF16)
    rstd_out[...] = rstd
    if both:
        grad_rows = (grad[...].astype(F32) * keep[:, image : image + 1]).astype(BF16)
        grad_out[...] = grad_rows
        put_sums(sums_out, prior_sums if joined else None, [column_sum(grad_rows.astype(F32))])
    forward, backward = None, None
    for part, fetch_up, fetch_down in slices:
        fetch_up.wait()
        fetch_down.wait()
        hidden = dot_nn(normed, up_held[:, part]) + up_bias[layer : layer + 1, part]
        active, slope = gelu_parts(hidden)
        active = active.astype(BF16)
        active_out[:, part] = active
        term = dot_nn(active, down_held[part])
        forward = term if forward is None else forward + term
        if both:
            grad_hidden = (slope * dot_nt(grad_rows, down_held[part])).astype(BF16)
            slope_out[:, part] = grad_hidden
            term = dot_nt(grad_hidden, up_held[:, part])
            backward = term if backward is None else backward + term
        else:
            slope_out[:, part] = slope.astype(BF16)
    save.start(1)
    save.start(2)
    partial_out[...] = forward.astype(BF16)
    if both:
        back_out[...] = backward.astype(BF16)
    save.wait()


def ffn_forward(layer, image, streams, vectors, up_bias, up, down, grad=None, keep=None, prior_sums=None):
    rows, width = streams[0].shape
    units = up.shape[2]
    both = grad is not None
    saved = [(rows, width), (rows, units), (rows, units)]
    outs = [
        shape((rows, width), F32),
        far(saved[0], BF16),
        shape((rows, width), BF16),
        shape((rows, 1), F32),
        far(saved[1], BF16),
        far(saved[2], BF16),
        shape((rows, width), BF16),
    ]
    ins = [*streams, vectors, up_bias]
    if both:
        outs += [shape((rows, width), BF16), shape((8, width), F32), shape((rows, width), BF16)]
        ins += [grad, keep]
    joined = prior_sums is not None
    if joined:
        ins.append(prior_sums)
    specs = [IN_VMEM] * len(ins) + [IN_HBM] * 2
    return kernel_call(
        lambda *refs: ffn_body(layer, both, image, joined, units // 3, refs),
        outs,
        [IN_HBM if index in (1, 4, 5) else IN_VMEM for index in range(len(outs))],
        (*ins, up, down),
        specs,
        [
            pltpu.VMEM((width, units), BF16),
            pltpu.VMEM((units, width), BF16),
            pltpu.SemaphoreType.DMA((2, 4)),
            *[pltpu.VMEM(dims, BF16) for dims in saved],
            pltpu.SemaphoreType.DMA((3,)),
        ],
        f"ffn_both_{layer}" if both else f"ffn_{layer}",
        4.6 if both else 3,
    )


def ffn_back_body(layer, joined, step, refs):
    base, mine, theirs, hat, rstd, vectors = refs[:6]
    refs = refs[6:]
    if joined:
        prior_sums, refs = refs[0], refs[1:]
    slope_hbm, up_hbm, down_hbm = refs[:3]
    grad_out, low_out, _, partial_out, sums_out = refs[3:8]
    up_held, down_held, sems, slope, hidden_out, more_sems = refs[8:]
    load = Loader([slope_hbm], [slope], more_sems)
    save = Saver([hidden_out], [refs[5]], more_sems.at[1:2])
    slices = fetch_slices(layer, step, up_hbm, down_hbm, up_held, down_held, sems)
    grad_normed = mine[...].astype(F32) + theirs[...].astype(F32)
    x_hat = hat[...].astype(F32)
    grad = base[...] + norm_back(
        grad_normed, x_hat, rstd[...], vector_row(vectors, FIRST_GAIN, layer + 1)
    )
    grad_out[...] = grad
    low = grad.astype(BF16)
    low_out[...] = low
    sums = [column_sum(grad_normed * x_hat), column_sum(grad_normed), column_sum(grad)]
    put_sums(sums_out, prior_sums if joined else None, sums)
    backward = None
    load.get(0)
    for part, fetch_up, fetch_down in slices:
        fetch_down.wait()
        fetch_up.wait()
        grad_hidden = (slope[:, part].astype(F32) * dot_nt(low, down_held[part])).astype(BF16)
        hidden_out[:, part] = grad_hidden
        term = dot_nt(grad_hidden, up_held[:, part])
        backward = term if backward is None else backward + term
    save.start(0)
    partial_out[...] = backward.astype(BF16)
    save.wait()


def ffn_backward(layer, grads, hat, rstd, vectors, slope, up, down, prior_sums=None, micros=4):
    rows, width = grads[0].shape
    units = up.shape[2]
    outs = [
        shape((rows, width), F32),
        shape((rows, width), BF16),
        far((rows, units), BF16),
        shape((rows, width), BF16),
        shape((8, width), F32),
    ]
    ins = [*grads, hat, rstd, vectors]
    joined = prior_sums is not None
    if joined:
        ins.append(prior_sums)
    return kernel_call(
        lambda *refs: ffn_back_body(layer, joined, units // 4, refs),
        outs,
        [IN_VMEM, IN_VMEM, IN_HBM, IN_VMEM, IN_VMEM],
        (*ins, slope, up, down),
        [IN_VMEM] * len(ins) + [IN_HBM] * 3,
        [
            pltpu.VMEM((width, units), BF16),
            pltpu.VMEM((units, width), BF16),
            pltpu.SemaphoreType.DMA((2, 4)),
            pltpu.VMEM((rows, units), BF16),
            pltpu.VMEM((rows, units), BF16),
            pltpu.SemaphoreType.DMA((2,)),
        ],
        f"ffn_back_{layer}",
        micros,
    )


def attention_back_body(layer, heads, joined, refs):
    base, mine, theirs, hat, rstd, vectors, first_hat = refs[:7]
    refs = refs[7:]
    if joined:
        prior_sums, prior_table = refs[:2]
        refs = refs[2:]
    qkv_hbm, weights_hbm, in_hbm, out_hbm = refs[:4]
    grad_out, low_out, mixed_hbm, partial_out, sums_out, table_out = refs[4:10]
    in_held, out_held, turned, merged, diagonals, sems, qkv, weights, mixed_out, more_sems = refs[10:]
    width = heads * HEAD_DIM
    per_group = LANES // HEAD_DIM
    fetch_out = pltpu.make_async_copy(out_hbm.at[layer], out_held, sems.at[1])
    fetch_in = pltpu.make_async_copy(in_hbm.at[layer], in_held, sems.at[0])
    fetch_out.start()
    load = Loader([qkv_hbm, weights_hbm], [qkv, weights], more_sems)
    save = Saver([mixed_out], [mixed_hbm], more_sems.at[2:3])
    fetch_in.start()
    grad_normed = mine[...].astype(F32) + theirs[...].astype(F32)
    x_hat = hat[...].astype(F32)
    grad = base[...].astype(F32) + norm_back(
        grad_normed, x_hat, rstd[...], vector_row(vectors, SECOND_GAIN, layer)
    )
    grad_out[...] = grad
    low = grad.astype(BF16)
    low_out[...] = low
    sums = [column_sum(grad_normed * x_hat), column_sum(grad_normed), column_sum(grad)]
    place = place_matrix(layer)
    load.get(0)
    queries = dot_nn(place, qkv[:, :width]).astype(BF16)
    turned_keys = dot_tt(qkv[:, width : 2 * width], place).astype(BF16)
    values = dot_nn(place, qkv[:, 2 * width :]).astype(BF16)
    fetch_out.wait()
    grad_attended = dot_nt(low, out_held[...]).astype(BF16)
    grad_slots = dot_nn(place, grad_attended).astype(BF16)
    grad_turned = dot_tt(grad_attended, place).astype(BF16)
    load.get(1)
    scale = HEAD_DIM ** (-0.5)
    empty = jnp.zeros((SLOT - KEYS, LANES), BF16)
    for group in range(width // LANES):
        lanes = slice(group * LANES, (group + 1) * LANES)
        total = None
        for block in range(2):
            top_row = block * SLOT
            slots = slice(top_row, top_row + SLOT)
            own_keys = slice(top_row, top_row + KEYS)
            low_weights = weights[group * 2 + block]
            full = low_weights.astype(F32)
            grad_weights = dot_nn(values[own_keys, lanes], heads_apart(grad_turned[lanes, slots]))
            spread = jnp.sum(full * grad_weights, axis=0, keepdims=True)
            grad_scores = full * (grad_weights - spread)
            total = grad_scores if total is None else total + grad_scores
            grad_raw = (grad_scores * scale).astype(BF16)
            grad_query = heads_together(dot_nn(turned_keys[lanes, own_keys], grad_raw))
            grad_key = dot_nn(grad_raw, head_rows(queries[slots, lanes]))
            grad_value = dot_nn(low_weights, head_rows(grad_slots[slots, lanes]))
            turned[lanes, slots] = grad_query.astype(BF16)
            for at, found in ((0, grad_key), (width, grad_value)):
                columns = slice(at + group * LANES, at + (group + 1) * LANES)
                merged[own_keys, columns] = found.astype(BF16)
                merged[top_row + KEYS : top_row + SLOT, columns] = empty
        for member in range(per_group):
            head = group * per_group + member
            own = total[:, member * LANES : (member + 1) * LANES]
            wide = jnp.concatenate([own, jnp.zeros_like(own)], axis=1)
            line = None
            for start in range(0, KEYS, 8):
                rows = wide[start : start + 8]
                if start:
                    rows = pltpu.roll(rows, TURN - start, 1)
                line = rows if line is None else line + rows
            diagonals[head * 8 : head * 8 + 8] = line
    mixed = [dot_tt(place, turned[...]).astype(BF16)]
    both = dot_tn(place, merged[...]).astype(BF16)
    mixed += [both[:, :width], both[:, width:]]
    mixed_out[:, :width] = mixed[0]
    mixed_out[:, width:] = both
    save.start(0)
    fetch_in.wait()
    partial = dot_nt(mixed[0], in_held[0])
    partial = partial + dot_nt(mixed[1], in_held[1])
    partial = partial + dot_nt(mixed[2], in_held[2])
    partial_out[...] = partial.astype(BF16)
    sums += [column_sum(partial * first_hat[...].astype(F32)), column_sum(partial)]
    put_sums(sums_out, prior_sums if joined else None, sums)
    lines = diagonals[...]
    row = lax.broadcasted_iota(jnp.int32, lines.shape, 0)
    for bit in range(3):
        moved = pltpu.roll(lines, TURN - (1 << bit), 1)
        lines = jnp.where(((row >> bit) & 1) == 1, moved, lines)
    lines = jnp.sum(lines.reshape(heads, 8, TURN), axis=1)
    table = dot_full(lines, offset_matrix(), ((1,), (1,)))
    table_out[...] = table + prior_table[...] if joined else table
    save.wait()


def attention_backward(
    layer, grads, hat, rstd, vectors, first_hat, qkv, weights, matrix_in, matrix_out,
    prior=(), micros=5,
):
    rows, width = grads[0].shape
    head_width = matrix_out.shape[1]
    heads = head_width // HEAD_DIM
    outs = [
        shape((rows, width), F32),
        shape((rows, width), BF16),
        far((rows, 3 * head_width), BF16),
        shape((rows, width), BF16),
        shape((8, width), F32),
        shape((heads, SPAN * SPAN), F32),
    ]
    ins = (*grads, hat, rstd, vectors, first_hat, *prior)
    return kernel_call(
        lambda *refs: attention_back_body(layer, heads, bool(prior), refs),
        outs,
        [IN_VMEM, IN_VMEM, IN_HBM, IN_VMEM, IN_VMEM, IN_VMEM],
        (*ins, qkv, weights, matrix_in, matrix_out),
        [IN_VMEM] * len(ins) + [IN_HBM] * 4,
        [
            pltpu.VMEM((3, width, head_width), BF16),
            pltpu.VMEM((head_width, width), BF16),
            pltpu.VMEM((head_width, 2 * SLOT), BF16),
            pltpu.VMEM((2 * SLOT, 2 * head_width), BF16),
            pltpu.VMEM((heads * 8, TURN), F32),
            pltpu.SemaphoreType.DMA((2,)),
            pltpu.VMEM(qkv.shape, BF16),
            pltpu.VMEM(weights.shape, BF16),
            pltpu.VMEM((rows, 3 * head_width), BF16),
            pltpu.SemaphoreType.DMA((3,)),
        ],
        f"attention_back_{layer}",
        micros,
    )


def finish_body(base, mine, theirs, hat, rstd, vectors, out):
    grad_normed = mine[...].astype(F32) + theirs[...].astype(F32)
    out[...] = base[...] + norm_back(
        grad_normed, hat[...].astype(F32), rstd[...], vector_row(vectors, FIRST_GAIN, 0)
    )


def output_body(layer, base, mine, theirs, vectors, out):
    total = base[...] + (mine[...].astype(F32) + theirs[...].astype(F32))
    out[...] = (total + vector_row(vectors, REDUCE_BIAS, layer)).astype(BF16)


def finish(body, kind, name, micros, *ins):
    return kernel_call(
        body, pltpu.HBM(ins[0].shape, kind), IN_VMEM, ins, [IN_VMEM] * len(ins), [], name, micros
    )


def group_place(group, top, order):
    place = 0
    for step, bit in enumerate(order):
        place = place + ((((group >> bit) & 1) ^ ((top >> bit) & 1)) << (len(order) - 1 - step))
    return place


def grads_body(pairs, groups, order, step, summed, refs):
    top = refs[0][0]
    lefts = 1 + max(left for left, _ in pairs)
    rights = len(pairs)
    refs = refs[1:]
    total = 2 * (lefts + rights)
    sources, refs = refs[:total], refs[total:]
    load = Loader(sources, refs[-total - 1 : -1], refs[-1])
    refs = refs[: -total - 1]
    keep_out, sums_out, held, turned, wide, sems = (refs[0], *refs[-5:])
    send_outs = refs[1:-5]
    rows = sources[0].shape[0]
    space = wide.shape[0] // 2
    empty = space - rows
    block = keep_out.shape[1]
    copies = []
    for left in range(lefts):
        for image in range(2):
            start = image * space
            turned[left, :, start + LANES : start + space] = jnp.zeros(
                (turned.shape[1], space - LANES), BF16
            )
            turned[left, :, start : start + rows] = load.get(2 * left + image)[...].T
    at = 0
    sum_at = 0
    for right, (left, _) in enumerate(pairs):
        columns = sources[2 * (lefts + right)].shape[1]
        for image in range(2):
            start = image * space
            wide[start : start + rows, :columns] = load.get(2 * (lefts + right) + image)[...]
            wide[start + rows : start + space, :columns] = jnp.zeros((empty, columns), BF16)
        if summed[right]:
            sums_out[0:1, sum_at : sum_at + columns] = column_sum(wide[:, :columns].astype(F32))
            sum_at += columns
        for first in range(0, columns, step):
            found = dot_nn(turned[left], wide[:, first : first + step]).astype(BF16)
            for group in range(groups):
                held[group_place(group, top, order), :, at : at + step] = found[
                    group * block : (group + 1) * block
                ]
            sent = at // send_outs[0].shape[2]
            inner = at - sent * send_outs[0].shape[2]
            for half, out in (
                (0, keep_out.at[:, :, at : at + step]),
                (1, send_outs[sent].at[:, :, inner : inner + step]),
            ):
                copy = pltpu.make_async_copy(
                    held.at[half * groups // 2 : (half + 1) * groups // 2, :, at : at + step],
                    out,
                    sems.at[half, at // step],
                )
                copy.start()
                copies.append(copy)
            at += step
    for copy in copies:
        copy.wait()


def weight_grads(top, groups, order, pairs, lefts, rights, summed, pieces, name, micros):
    width = lefts[0].shape[1]
    step = 512 if all(item.shape[1] % 512 == 0 for item in rights) else 384
    columns = sum(item.shape[1] for item in rights[::2])
    widest = max(item.shape[1] for item in rights)
    space = 2 * LANES
    summed_columns = sum(item.shape[1] for item, used in zip(rights[::2], summed) if used)
    outs = [
        shape((groups // 2, width // groups, columns), BF16),
        *[shape((groups // 2, width // groups, columns // pieces), BF16)] * pieces,
        shape((8, summed_columns), F32),
    ]
    count = 1 + max(left for left, _ in pairs)
    kept, *sent, sums = kernel_call(
        lambda *refs: grads_body(pairs, groups, order, step, summed, refs),
        outs,
        [ANYWHERE] * (1 + pieces) + [IN_VMEM],
        (top, *lefts, *rights),
        [IN_SMEM] + [IN_HBM] * 2 + [ANYWHERE] * 2 + [IN_HBM] * len(rights),
        [
            pltpu.VMEM((groups, width // groups, columns), BF16),
            pltpu.VMEM((count, width, 2 * space), BF16),
            pltpu.VMEM((2 * space, widest), BF16),
            pltpu.SemaphoreType.DMA((2, columns // step)),
            *[pltpu.VMEM(item.shape, item.dtype) for item in (*lefts, *rights)],
            pltpu.SemaphoreType.DMA((len(lefts) + len(rights),)),
        ],
        name,
        micros,
        (),
        20 * 1024 * 1024,
    )
    return kept, sent, sums


def swap(value):
    return lax.ppermute(value, "mp", [(0, 1), (1, 0)])


def trade(value, bit, size):
    return lax.ppermute(value, "dp", [(source, source ^ bit) for source in range(size)])


def fold_body(kept, *refs):
    *pieces, keep_out, send_out = refs
    half = keep_out.shape[0]
    at = 0
    for found in pieces:
        columns = slice(at, at + found.shape[2])
        at += found.shape[2]
        for start, out in ((0, keep_out), (half, send_out)):
            for block in range(half):
                total = kept[start + block, :, columns].astype(F32) + found[start + block].astype(F32)
                out[block, :, columns] = total.astype(BF16)


def fold(kept, found, name):
    half = shape((kept.shape[0] // 2, *kept.shape[1:]), BF16)
    return kernel_call(
        fold_body, [half, half], [IN_VMEM] * 2, (kept, *found), [IN_VMEM] * (1 + len(found)), [],
        name, 0.1,
    )


class Scatter:
    def __init__(self, kept, sent, order, size, name):
        self.kept, self.sent, self.order, self.size, self.name = kept, sent, order, size, name
        self.finer = size >> len(order)
        self.level = 0
        self.send()

    def send(self):
        self.found = [
            trade(item, self.finer << self.order[self.level], self.size) for item in self.sent
        ]

    def step(self):
        if self.level + 1 < len(self.order):
            self.kept, sent = fold(self.kept, self.found, f"{self.name}_{self.level}")
            self.sent = [sent]
            self.level += 1
            self.send()

    def finish(self):
        for _ in self.order:
            self.step()
        kept, finer = self.kept, self.finer
        found = jnp.concatenate(self.found, axis=2) if len(self.found) > 1 else self.found[0]
        rank = lax.axis_index("dp")
        while finer > 1:
            finer //= 2
            held = (kept.astype(F32) + found.astype(F32)).astype(BF16)
            halves = held.reshape((2, 1, held.shape[1] // 2, held.shape[2]))
            mine = (rank // finer) % 2
            kept = lax.dynamic_index_in_dim(halves, mine, 0, keepdims=False)
            found = trade(lax.dynamic_index_in_dim(halves, 1 - mine, 0, keepdims=False), finer, self.size)
        return kept, found

    def join(self):
        kept, found = self.finish()
        return (
            kernel_call(
                add_body, shape(kept.shape, F32), IN_VMEM, (kept, found), [IN_VMEM] * 2, [],
                f"{self.name}_end", 0.1,
            ),
        )


def add_body(left, right, out):
    out[...] = left[...].astype(F32) + right[...].astype(F32)


def some_bits(name, size):
    bits = range(size.bit_length() - 1)
    listed = [bit for bit in BIT_ORDER[name] if bit in bits]
    return tuple(listed + [bit for bit in bits if bit not in listed])


class Total:
    def __init__(self, value, size):
        self.value, self.size = value, size
        self.left = [1 << bit for bit in some_bits("total", size)]
        self.send()

    def send(self):
        self.found = trade(self.value, self.left.pop(0), self.size)

    def step(self):
        if self.left:
            self.value = kernel_call(
                add_body, shape(self.value.shape, F32), IN_VMEM, (self.value, self.found),
                [IN_VMEM] * 2, [], "total", 0.1,
            )
            self.send()

    def finish(self):
        while self.left:
            self.step()
        return self.value, self.found


def collect_body(counts, widths, refs):
    outs = refs[sum(counts) :]
    for layer, count in enumerate(counts):
        total = refs[0][0].astype(F32)
        if count == 2:
            total = total + refs[1][0].astype(F32)
        refs = refs[count:]
        at = 0
        for out, parts in zip(outs, widths):
            for part in range(parts):
                columns = out.shape[-1]
                if len(out.shape) == 4:
                    out[layer, part] = total[:, at : at + columns]
                else:
                    out[layer] = total[:, at : at + columns]
                at += columns


def collect(pairs, shapes, name):
    flat = [item for pair in pairs for item in pair]
    counts = [len(pair) for pair in pairs]
    return kernel_call(
        lambda *refs: collect_body(
            counts, [dims[1] if len(dims) == 4 else 1 for dims in shapes], refs
        ),
        [pltpu.HBM(dims, F32) for dims in shapes],
        [IN_VMEM] * len(shapes),
        flat,
        [IN_VMEM] * len(flat),
        [],
        name,
        0.1,
    )


def pack_body(width, layers, refs):
    sums_0, theirs_0, sums_low, sums_1, last = refs[:5]
    ups, mixes, tables = refs[5 : 5 + layers], refs[5 + layers : 5 + 2 * layers], refs[5 + 2 * layers : -1]
    out = refs[-1]
    out[...] = jnp.zeros(out.shape, F32)
    out[0:2] = sums_0[3:5] + theirs_0[3:5]
    out[2:3] = sums_0[2:3]
    out[3:5] = sums_0[0:2]
    out[5:6] = sums_low[2:3]
    out[6:8] = sums_low[0:2]
    out[8:9] = sums_1[2:3]
    out[9:11] = sums_1[0:2]
    out[11:12] = last[0:1]
    row = 6 * layers
    for item in ups:
        for start in range(0, item.shape[1], width):
            out[row : row + 1] = item[0:1, start : start + width]
            row += 1
    third = mixes[0].shape[1] // 3
    for item in mixes:
        out[row : row + 1, :third] = item[0:1, :third]
        out[row : row + 1, third : 2 * third] = item[0:1, 2 * third :]
        row += 1
    for item in tables:
        heads, offsets = item.shape
        for head in range(heads):
            lane = head * TURN % width
            out[row : row + 1, lane : lane + offsets] = item[head : head + 1]
            if (head + 1) * TURN % width == 0:
                row += 1


def unpack_body(refs):
    packed, found, vectors, up_bias, pair_bias, tables = refs
    width = packed.shape[1]
    layers, units = up_bias.shape
    total = packed[...] + found[...]
    for layer in range(layers):
        for member in range(6):
            vectors[member, layer : layer + 1] = total[6 * layer + member : 6 * layer + member + 1]
    row = 6 * layers
    for layer in range(layers):
        for start in range(0, units, width):
            up_bias[layer : layer + 1, start : start + width] = total[row : row + 1]
            row += 1
    third = pair_bias.shape[2]
    for layer in range(layers):
        for member in range(2):
            pair_bias[layer, member : member + 1] = total[
                row : row + 1, member * third : (member + 1) * third
            ]
        row += 1
    heads, _, offsets = tables.shape
    for layer in range(layers):
        for head in range(heads):
            lane = head * TURN % width
            tables[head, layer : layer + 1] = total[row : row + 1, lane : lane + offsets]
            if (head + 1) * TURN % width == 0:
                row += 1


def shards(
    tokens,
    keep_mask,
    cotangent,
    first_gain,
    first_shift,
    attention_in,
    query_value_bias,
    position_table,
    attention_out,
    attention_bias,
    second_gain,
    second_shift,
    expand_weight,
    expand_bias,
    reduce_weight,
    reduce_bias,
):
    LINE.clear()
    size = lax.axis_size("dp")
    half = lax.axis_index("mp")
    groups = min(16, size)
    top = (lax.axis_index("dp") // (size // groups)).astype(jnp.int32).reshape(1)
    layers, width = first_gain.shape
    head_width = attention_out.shape[1]
    units = expand_weight.shape[2]
    heads = head_width // HEAD_DIM
    matrix_in = jnp.transpose(attention_in, (0, 2, 1, 3))
    own_half = half.astype(jnp.int32).reshape(1)
    bias, masks, (keep_columns, vectors, tokens, cotangent, up_bias, pair_bias) = make_tables(
        own_half, jnp.transpose(position_table, (1, 0, 2)), keep_mask,
        (tokens, cotangent, expand_bias, query_value_bias),
        (first_gain, first_shift, attention_bias, second_gain, second_shift, reduce_bias),
    )
    other_tokens = swap(tokens)
    other_cotangent = swap(cotangent)

    def attend(layer, image, streams, also=()):
        return attention_forward(
            layer, streams, vectors, pair_bias, bias[layer], masks[layer][image], matrix_in,
            attention_out, also,
        )

    def feed(layer, image, streams, grad=None, prior_sums=None):
        return ffn_forward(
            layer, image, streams, vectors, up_bias, expand_weight, reduce_weight, grad,
            keep_columns, prior_sums,
        )

    att, ffn = [[None, None], [None, None]], [[None, None], [None, None]]
    att[0][0] = attend(0, 0, (tokens,))
    sent_own = swap(att[0][0][7])
    att[0][1] = attend(0, 1, (other_tokens,), (other_cotangent,))
    sent_other = swap(att[0][1][7])
    ffn[0][1] = feed(0, 1, (att[0][1][0], att[0][1][7], sent_own))
    sent_2 = swap(ffn[0][1][6])
    ffn[0][0] = feed(0, 0, (att[0][0][0], att[0][0][7], sent_other))
    sent_1 = swap(ffn[0][0][6])
    att[1][0] = attend(1, 0, (ffn[0][0][0], ffn[0][0][6], sent_2))
    sent_own = swap(att[1][0][7])
    att[1][1] = attend(1, 1, (ffn[0][1][0], ffn[0][1][6], sent_1))
    sent_other = swap(att[1][1][7])

    def ffn_grads(layer, low, hidden, name):
        normed = [ffn[layer][image][1] for image in range(2)]
        active = [ffn[layer][image][4] for image in range(2)]
        order = some_bits(f"ffn_{layer}", groups)
        kept, sent, sums = weight_grads(
            top, groups, order, ((0, 0), (1, 1)), (*normed, *low), (*hidden, *active),
            (True, False), PIECES["ffn"], name, MICROS[name],
        )
        return Scatter(kept, sent, order, size, f"ffn_fold_{layer}"), sums

    def attention_grads(layer, low, mixed, name):
        normed = [att[layer][image][1] for image in range(2)]
        attended = [att[layer][image][6] for image in range(2)]
        order = some_bits(f"attention_{layer}", groups)
        kept, sent, sums = weight_grads(
            top, groups, order, ((0, 0), (1, 1)), (*normed, *low), (*mixed, *attended),
            (True, False), PIECES["attention"], name, MICROS[name],
        )
        return Scatter(kept, sent, order, size, f"attention_fold_{layer}"), sums

    def attend_back(layer, image, grads, prior=(), micros=5):
        held = att[layer][image]
        return attention_backward(
            layer, grads, ffn[layer][image][2], ffn[layer][image][3], vectors, held[2],
            held[4], held[5], matrix_in, attention_out, prior, micros,
        )

    def feed_back(image, grads, prior_sums=None, micros=4):
        held = att[1][image]
        return ffn_backward(
            0, grads, held[2], held[3], vectors, ffn[0][image][5], expand_weight,
            reduce_weight, prior_sums, micros,
        )

    back, low = [[None, None], [None, None]], [None, None]
    sent, sums, extra, outs = {}, {}, {}, {}
    rows = width // size

    def ffn_1_other():
        ffn[1][1] = feed(1, 1, (att[1][1][0], att[1][1][7], sent_own), other_cotangent)
        sent["ffn_1_other"] = swap(ffn[1][1][7])
        sent["block"] = swap(ffn[1][1][6])

    def ffn_1_own():
        ffn[1][0] = feed(1, 0, (att[1][0][0], att[1][0][7], sent_other), cotangent, ffn[1][1][8])
        sent["ffn_1_own"] = swap(ffn[1][0][7])

    def ffn_grads_1():
        sums["ffn_sum_1"], extra["up_1"] = ffn_grads(
            1, (ffn[1][0][9], ffn[1][1][9]), (ffn[1][0][5], ffn[1][1][5]), "ffn_grads_1"
        )

    def attention_back_1_own():
        back[1][0] = attend_back(
            1, 0, (ffn[1][0][9], ffn[1][0][7], sent["ffn_1_other"]), (),
            MICROS["attention_back_1_own"],
        )
        sent["back_1_own"] = swap(back[1][0][3])

    def attention_back_1_other():
        back[1][1] = attend_back(
            1, 1, (ffn[1][1][9], ffn[1][1][7], sent["ffn_1_own"]), back[1][0][4:6],
            MICROS["attention_back_1_other"],
        )
        sent["back_1_other"] = swap(back[1][1][3])

    def attention_grads_1():
        sums["attention_sum_1"], extra["mixed_1"] = attention_grads(
            1, (back[1][0][1], back[1][1][1]), (back[1][0][2], back[1][1][2]), "attention_grads_1"
        )

    def ffn_back_0_other():
        low[1] = feed_back(
            1, (back[1][1][0], back[1][1][3], sent["back_1_own"]), None, MICROS["ffn_back_0_other"]
        )
        sent["low_other"] = swap(low[1][3])

    def ffn_back_0_own():
        low[0] = feed_back(
            0, (back[1][0][0], back[1][0][3], sent["back_1_other"]), low[1][4],
            MICROS["ffn_back_0_own"],
        )
        sent["low_own"] = swap(low[0][3])

    def ffn_grads_0():
        sums["ffn_sum_0"], extra["up_0"] = ffn_grads(
            0, (low[0][1], low[1][1]), (low[0][2], low[1][2]), "ffn_grads_0"
        )

    def attention_back_0_own():
        back[0][0] = attend_back(
            0, 0, (low[0][0], low[0][3], sent["low_other"]), (), MICROS["attention_back_0_own"]
        )

    def attention_back_0_other():
        back[0][1] = attend_back(
            0, 1, (low[1][0], low[1][3], sent["low_own"]), back[0][0][4:6],
            MICROS["attention_back_0_other"],
        )
        sent["last"] = swap(back[0][1][3])
        sent["sums"] = swap(back[0][1][4])

    def attention_grads_0():
        sums["attention_sum_0"], extra["mixed_0"] = attention_grads(
            0, (back[0][0][1], back[0][1][1]), (back[0][0][2], back[0][1][2]), "attention_grads_0"
        )

    def pack():
        pieces = (
            back[0][1][4], sent["sums"], low[0][4], back[1][1][4], ffn[1][0][8],
            extra["up_0"], extra["up_1"], extra["mixed_0"], extra["mixed_1"],
            back[0][1][5], back[1][1][5],
        )
        per_row = width // TURN
        count = layers * (6 + units // width + 1 + heads // per_row)
        packed = kernel_call(
            lambda *refs: pack_body(width, layers, refs),
            shape((-(-count // 8) * 8, width), F32),
            IN_VMEM,
            pieces,
            [IN_VMEM] * len(pieces),
            [],
            "pack",
            MICROS["pack"],
        )
        sums["total"] = Total(packed, size)

    def unpack():
        outs["small"] = kernel_call(
            lambda *refs: unpack_body(refs),
            [
                shape((6, layers, width), F32),
                shape((layers, units), F32),
                shape((layers, 2, head_width), F32),
                shape((heads, layers, SPAN * SPAN), F32),
            ],
            [IN_VMEM] * 4,
            sums["total"].finish(),
            [IN_VMEM] * 2,
            [],
            "unpack",
            0.1,
        )

    def tokens_grad():
        outs["tokens_grad"] = finish(
            finish_body, F32, "finish", 0.1,
            back[0][0][0], back[0][0][3], sent["last"], att[0][0][2], att[0][0][3], vectors,
        )

    def block_output():
        outs["block_output"] = finish(
            lambda *refs: output_body(1, *refs), BF16, "output", 0.1,
            ffn[1][0][0], ffn[1][0][6], sent["block"], vectors,
        )

    def attention_end_1():
        extra["attention_1"] = sums["attention_sum_1"].join()

    def ffn_end_1():
        extra["ffn_1"] = sums["ffn_sum_1"].join()

    def attention_outputs():
        outs["attention"] = collect(
            (sums["attention_sum_0"].finish(), extra["attention_1"]),
            [(layers, 3, rows, head_width), (layers, rows, head_width)],
            "attention_collect",
        )

    def ffn_outputs():
        outs["ffn"] = collect(
            (sums["ffn_sum_0"].finish(), extra["ffn_1"]), [(layers, rows, units)] * 2, "ffn_collect"
        )

    steps = {
        item.__name__: item
        for item in (
            ffn_1_other, ffn_1_own, ffn_grads_1, attention_back_1_own, attention_back_1_other,
            attention_grads_1, ffn_back_0_other, ffn_back_0_own, ffn_grads_0,
            attention_back_0_own, attention_back_0_other, attention_grads_0, pack, unpack,
            tokens_grad, block_output, attention_end_1, ffn_end_1, attention_outputs, ffn_outputs,
        )
    }
    for name in PLAN:
        if name in steps:
            steps[name]()
        else:
            sums[name].step()

    in_grad, out_grad = outs["attention"]
    up_grad, down_grad = outs["ffn"]
    vector_grads, expand_bias_grad, pair_grad, table_grad = outs["small"]
    return (
        outs["block_output"],
        outs["tokens_grad"],
        jnp.transpose(in_grad, (0, 2, 1, 3)),
        jnp.transpose(out_grad, (0, 2, 1)),
        up_grad,
        jnp.transpose(down_grad, (0, 2, 1)),
        pair_grad,
        expand_bias_grad,
        jnp.transpose(table_grad, (1, 0, 2)),
        jnp.transpose(vector_grads, (1, 0, 2)),
    )


def solution(mesh):
    return jax.shard_map(
        shards,
        mesh=mesh,
        in_specs=(
            P(("dp", "mp"), None),
            P("dp", None),
            P(("dp", "mp"), None),
            P(),
            P(),
            P(None, None, None, "mp"),
            P(None, None, "mp"),
            P(None, "mp", None),
            P(None, "mp", None),
            P(),
            P(),
            P(),
            P(None, None, "mp"),
            P(None, "mp"),
            P(None, "mp", None),
            P(),
        ),
        out_specs=(
            P(("dp", "mp"), None),
            P(("dp", "mp"), None),
            P(None, "dp", None, "mp"),
            P(None, "mp", "dp"),
            P(None, "dp", "mp"),
            P(None, "mp", "dp"),
            P(None, None, "mp"),
            P(None, "mp"),
            P(None, "mp", None),
            P(),
        ),
        check_vma=False,
    )
```

```python
import jax
import jax.numpy as jnp
import numpy as np
from jax import lax
from jax.experimental import pallas as pl
from jax.experimental.pallas import tpu as pltpu
from jax.sharding import PartitionSpec as P

HEAD_DIM = 32
GRID = 14
WIN = 7
SHIFT = 3
PATCHES = 196
BLOCK = 98
SLOT = 128
KEYS = 112
LANES = 128
SPAN = 2 * WIN - 1
TURN = 256

EPSILON = 1e-05
MASKED = -1e30
F32 = jnp.float32
BF16 = jnp.bfloat16
VMEM_LIMIT = 14 * 1024 * 1024

IN_VMEM = pl.BlockSpec(memory_space=pltpu.VMEM)
IN_SMEM = pl.BlockSpec(memory_space=pltpu.SMEM)
ANYWHERE = pl.BlockSpec(memory_space=pl.ANY)
IN_HBM = pl.BlockSpec(memory_space=pltpu.HBM)


def shape(dims, kind):
    return jax.ShapeDtypeStruct(dims, kind)


def far(dims, kind):
    return pltpu.HBM(dims, kind)


class Saver:
    def __init__(self, held, outs, sems):
        self.held, self.outs, self.sems = held, outs, sems
        self.copies = []

    def put(self, index, value):
        self.held[index][...] = value
        self.start(index)

    def start(self, index):
        copy = pltpu.make_async_copy(self.held[index], self.outs[index], self.sems.at[index])
        copy.start()
        self.copies.append(copy)

    def wait(self):
        for copy in self.copies:
            copy.wait()


class Near:
    def __init__(self, held):
        self.held = held

    def put(self, index, value):
        self.held[index][...] = value

    def get(self, index):
        return self.held[index]

    def start(self, index):
        pass

    def wait(self):
        pass


class Loader:
    def __init__(self, sources, held, sems):
        self.held = held
        self.copies = [
            pltpu.make_async_copy(source, target, sems.at[index])
            for index, (source, target) in enumerate(zip(sources, held))
        ]
        self.waiting = set(range(len(held)))
        for copy in self.copies:
            copy.start()

    def get(self, index):
        if index in self.waiting:
            self.waiting.remove(index)
            self.copies[index].wait()
        return self.held[index]


FETCHED = []
LINE = []
COST = 1.0e9
FAR_LAYERS = ()
PLAN = (
    "ffn_1_other",
    "ffn_1_own",
    "ffn_grads_1",
    "attention_back_1_own",
    "ffn_sum_1",
    "attention_back_1_other",
    "attention_grads_1",
    "ffn_back_0_other",
    "ffn_back_0_own",
    "ffn_grads_0",
    "attention_sum_1",
    "ffn_sum_1",
    "ffn_sum_0",
    "attention_back_0_own",
    "attention_sum_1",
    "attention_back_0_other",
    "attention_grads_0",
    "ffn_sum_1",
    "pack",
    "attention_sum_0",
    "ffn_sum_0",
    "ffn_end_1",
    "attention_sum_0",
    "attention_sum_1",
    "attention_sum_0",
    "tokens_grad",
    "ffn_sum_0",
    "total",
    "attention_end_1",
    "block_output",
    "attention_outputs",
    "total",
    "total",
    "ffn_outputs",
    "unpack",
)
MICROS = {
    "attention_back_1_own": 14.22,
    "attention_back_1_other": 0.06,
    "attention_grads_1": 0.81,
    "ffn_back_0_other": 1.81,
    "ffn_back_0_own": 0.26,
    "ffn_grads_0": 0.1,
    "attention_back_0_own": 0.36,
    "attention_back_0_other": 0.33,
    "attention_grads_0": 0.17,
    "pack": 0.44,
    "ffn_grads_1": 0.3,
}
PIECES = {"ffn": 3, "attention": 2}
BIT_ORDER = {
    "ffn_1": (0, 2, 1, 3),
    "attention_1": (0, 1, 2, 3),
    "ffn_0": (0, 2, 1, 3),
    "attention_0": (0, 1, 2, 3),
    "total": (0, 2, 1, 3),
}


def kernel_call(body, outs, out_specs, ins, in_specs, scratch, name, micros, also=(), limit=None, fetch=()
):
    behind = [item for item in (*LINE, *also) if not any(item is used for used in ins)]
    skipped = len(behind)
    ins = [
        pltpu.with_memory_space_constraint(item, pltpu.HBM) if spec is IN_HBM else item
        for item, spec in zip(ins, in_specs)
    ]
    flat = outs if isinstance(outs, list) else [outs]
    flat_specs = out_specs if isinstance(out_specs, list) else [out_specs]
    count, near_count = len(fetch), len(ins)

    def whole(*refs):
        refs = refs[skipped:]
        own_ins, sources, refs = refs[:near_count], refs[near_count : near_count + count], refs[near_count + count :]
        own_outs, targets, refs = refs[: len(flat)], refs[len(flat) : len(flat) + count], refs[len(flat) + count :]
        copies = []
        if count:
            refs, sems = refs[:-1], refs[-1]
            for index, (_, layer) in enumerate(fetch):
                copy = pltpu.make_async_copy(
                    sources[index].at[layer], targets[index], sems.at[index]
                )
                copy.start()
                copies.append(copy)
        body(*own_ins, *own_outs, *refs)
        for copy in copies:
            copy.wait()

    found = pl.pallas_call(
        whole,
        out_shape=flat + [shape(item.shape[1:], item.dtype) for item, _ in fetch],
        in_specs=[ANYWHERE] * skipped + in_specs + [IN_HBM] * count,
        out_specs=flat_specs + [IN_VMEM] * count,
        scratch_shapes=list(scratch) + ([pltpu.SemaphoreType.DMA((count,))] if count else []),
        compiler_params=pltpu.CompilerParams(vmem_limit_bytes=limit or VMEM_LIMIT),
        cost_estimate=pl.CostEstimate(
            flops=int(micros * COST), bytes_accessed=1024, transcendentals=0
        ),
        name=name,
    )(
        *behind,
        *ins,
        *[pltpu.with_memory_space_constraint(item, pltpu.HBM) for item, _ in fetch],
    )
    near = [item for item, kind in zip(found, flat) if isinstance(kind, jax.ShapeDtypeStruct)]
    if near:
        LINE[:] = [min(near, key=lambda item: item.size)]
    else:
        LINE[:] = [pltpu.with_memory_space_constraint(found[0], pltpu.HBM)]
    if count:
        found, FETCHED[:] = found[: len(flat)], found[len(flat) :]
    return found if isinstance(outs, list) else found[0]


def dot_nn(left, right):
    return lax.dot_general(left, right, (((1,), (0,)), ((), ())), preferred_element_type=F32)


def dot_nt(left, right):
    return lax.dot_general(left, right, (((1,), (1,)), ((), ())), preferred_element_type=F32)


def dot_tn(left, right):
    return lax.dot_general(left, right, (((0,), (0,)), ((), ())), preferred_element_type=F32)


def dot_tt(left, right):
    return lax.dot_general(left, right, (((0,), (1,)), ((), ())), preferred_element_type=F32)


def dot_full(left, right, contracted):
    return lax.dot_general(
        left,
        right,
        (contracted, ((), ())),
        preferred_element_type=F32,
        precision=lax.Precision.HIGHEST,
    )


def place_matrix(layer):
    row = lax.broadcasted_iota(jnp.int32, (2 * SLOT, PATCHES), 0)
    patch = lax.broadcasted_iota(jnp.int32, (2 * SLOT, PATCHES), 1)
    second = row >= SLOT
    within = jnp.where(second, row - SLOT, row)
    found = within + jnp.where(second, BLOCK, 0) + layer * SHIFT * GRID
    found = jnp.where(found >= PATCHES, found - PATCHES, found)
    return jnp.where((within < BLOCK) & (found == patch), 1.0, 0.0).astype(BF16)


def window_matrix(layer, block):
    def groups(place):
        turned_row = (place * 147) >> 11
        col = place - turned_row * GRID
        row = turned_row + block * WIN + layer * SHIFT
        row = jnp.where(row >= GRID, row - GRID, row)

        def group(position):
            moved = position + layer * (WIN - SHIFT)
            return jnp.where(moved >= 2 * WIN, 2, jnp.where(moved >= WIN, 1, 0))

        return group(row) * 4 + group(col)

    key = lax.broadcasted_iota(jnp.int32, (KEYS, LANES), 0)
    query = lax.broadcasted_iota(jnp.int32, (KEYS, LANES), 1)
    return (groups(key) == groups(query)) & (key < BLOCK) & (query < BLOCK)


def offset_matrix():
    offset = lax.broadcasted_iota(jnp.int32, (SPAN * SPAN, TURN), 0)
    lane = lax.broadcasted_iota(jnp.int32, (SPAN * SPAN, TURN), 1)
    row = (offset * 79) >> 10
    place = offset - row * SPAN + row * GRID - (WIN - 1) * (GRID + 1)
    return jnp.where(jnp.where(place < 0, place + TURN, place) == lane, 1.0, 0.0)


def heads_apart(value):
    rows = value.shape[0]
    parts = []
    for member in range(rows // HEAD_DIM):
        start = member * HEAD_DIM
        pieces = [value[start : start + HEAD_DIM]]
        if start:
            pieces.insert(0, jnp.zeros((start, value.shape[1]), value.dtype))
        if start + HEAD_DIM < rows:
            pieces.append(jnp.zeros((rows - start - HEAD_DIM, value.shape[1]), value.dtype))
        parts.append(jnp.concatenate(pieces, axis=0))
    return jnp.concatenate(parts, axis=1)


def heads_together(value):
    count = value.shape[0] // HEAD_DIM
    columns = value.shape[1] // count
    return jnp.concatenate(
        [
            value[
                member * HEAD_DIM : (member + 1) * HEAD_DIM,
                member * columns : (member + 1) * columns,
            ]
            for member in range(count)
        ],
        axis=0,
    )


def norm_rows(stream, gain, shift):
    center = stream - jnp.mean(stream, axis=-1, keepdims=True)
    spread = jnp.mean(center * center, axis=-1, keepdims=True)
    rstd = lax.rsqrt(spread + EPSILON)
    x_hat = center * rstd
    return x_hat, rstd, (x_hat * gain + shift).astype(BF16)


def norm_back(grad_normed, x_hat, rstd, gain):
    scaled = grad_normed * gain
    term = jnp.mean(scaled, axis=-1, keepdims=True)
    along = jnp.mean(scaled * x_hat, axis=-1, keepdims=True)
    return rstd * (scaled - term - x_hat * along)


def column_sum(value):
    return jnp.sum(value, axis=0, keepdims=True)


def put_sums(out, prior, sums):
    for row, found in enumerate(sums):
        out[row : row + 1] = found if prior is None else found + prior[row : row + 1]
    out[len(sums) :] = jnp.zeros((out.shape[0] - len(sums), out.shape[1]), F32)


FIRST_GAIN, FIRST_SHIFT, ATTENTION_BIAS, SECOND_GAIN, SECOND_SHIFT, REDUCE_BIAS = range(6)


def vector_row(vectors, member, layer):
    row = member * (vectors.shape[0] // 6) + layer
    return vectors[row : row + 1]


def head_lanes(rows, member):
    lane = lax.broadcasted_iota(jnp.int32, (rows, LANES), 1)
    return (lane >= member * HEAD_DIM) & (lane < (member + 1) * HEAD_DIM)


def head_rows(value):
    rows = value.shape[0]
    return jnp.concatenate(
        [
            jnp.where(head_lanes(rows, member), value, jnp.zeros_like(value))
            for member in range(LANES // HEAD_DIM)
        ],
        axis=0,
    )


def tables_body(heads, layers, refs):
    half = refs[0]
    in_hbm, refs = refs[1:13], refs[13:]
    biases, refs = refs[:layers], refs[layers:]
    masks, refs = refs[: 2 * layers], refs[2 * layers :]
    keep_out, vectors_out = refs[:2]
    held = [refs[6], refs[7], *refs[2:6], *refs[8:14]]
    sems = refs[14]
    copies = []
    for index, (source, target) in enumerate(zip(in_hbm, held)):
        copies.append(pltpu.make_async_copy(source, target, sems.at[index]))
        copies[-1].start()
    table, keep = held[:2]
    same = lax.broadcasted_iota(jnp.int32, (KEYS, LANES), 0) == lax.broadcasted_iota(
        jnp.int32, (KEYS, LANES), 1
    )
    offsets = offset_matrix()
    per_group = LANES // HEAD_DIM
    for copy in copies:
        copy.wait()
    own_first = half[0] == 0
    rows = [keep[image : image + 1].astype(F32) for image in range(2)]
    pair = jnp.concatenate(
        [jnp.where(own_first, rows[0], rows[1]), jnp.where(own_first, rows[1], rows[0])], axis=0
    ).astype(BF16)
    for layer in range(layers):
        line = dot_full(table[:, layer], offsets, ((1,), (0,)))
        for head in range(heads):
            wide = jnp.broadcast_to(line[head : head + 1], (KEYS, TURN))
            lanes = head % per_group * LANES
            biases[layer][head // per_group, :, lanes : lanes + LANES] = pltpu.roll(
                wide, 0, 1, stride=1, stride_axis=0
            )[:, :LANES]
        place = place_matrix(layer)
        kept = dot_nt(place, pair)
        for block in range(2):
            window = window_matrix(layer, block)
            for image in range(2):
                column = kept[block * SLOT : block * SLOT + KEYS, image : image + 1]
                fine = window & ((column > 0.5) | same)
                masks[layer * 2 + image][block] = jnp.where(fine, 0.0, MASKED)
        if layer == 0:
            keep_out[...] = dot_tn(place, kept.astype(BF16))
    for index, item in enumerate(held[6:]):
        vectors_out[index * layers : (index + 1) * layers] = item[...]


def make_tables(half, position_table, keep_mask, moved, vectors, fetch, also):
    heads, layers, _ = position_table.shape
    groups = heads * HEAD_DIM // LANES
    width = vectors[0].shape[1]
    ins = (position_table, keep_mask, *moved, *vectors)
    outs = [shape((groups, KEYS, 4 * LANES), F32)] * layers + [shape((2, KEYS, LANES), F32)] * (
        2 * layers
    )
    outs += [
        shape((PATCHES, 2), F32),
        shape((len(vectors) * layers, width), F32),
        *[shape(item.shape, item.dtype) for item in moved],
    ]
    found = kernel_call(
        lambda *refs: tables_body(heads, layers, refs),
        outs,
        [IN_VMEM] * len(outs),
        (half, *ins),
        [IN_SMEM] + [IN_HBM] * len(ins),
        [pltpu.VMEM(item.shape, item.dtype) for item in (*ins[:2], *vectors)]
        + [pltpu.SemaphoreType.DMA((len(ins),))],
        "tables",
        1.6,
        also,
        None,
        fetch,
    )
    masks = [found[layers + 2 * layer : layers + 2 * layer + 2] for layer in range(layers)]
    return found[:layers], masks, found[3 * layers :]


def attention_body(layer, heads, chained, refs):
    if chained:
        base, mine, theirs = refs[:3]
        refs = refs[3:]
    else:
        base, refs = refs[0], refs[1:]
    vectors, pair_bias, bias, mask, in_held, out_held = refs[:6]
    refs = refs[6:]
    if chained:
        stream_out, refs = refs[0], refs[1:]
    hat_out, rstd_out, partial_out = refs[1], refs[2], refs[6]
    far_outs = (refs[0], refs[3], refs[4], refs[5])
    turned = refs[7]
    save = Saver(refs[8:12], far_outs, refs[12]) if layer in FAR_LAYERS else Near(far_outs)
    qkv_out, weights_out = save.held[1:3]
    width = heads * HEAD_DIM
    stream = base[...].astype(F32)
    if chained:
        stream = (
            stream
            + (mine[...].astype(F32) + theirs[...].astype(F32))
            + vector_row(vectors, REDUCE_BIAS, layer - 1)
        )
        stream_out[...] = stream
    x_hat, rstd, normed = norm_rows(
        stream, vector_row(vectors, FIRST_GAIN, layer), vector_row(vectors, FIRST_SHIFT, layer)
    )
    save.put(0, normed)
    hat_out[...] = x_hat.astype(BF16)
    rstd_out[...] = rstd
    place = place_matrix(layer)
    parts = []
    for member in range(3):
        mixed = dot_nn(normed, in_held[member])
        if member != 1:
            mixed = mixed + pair_bias[layer, member // 2 : member // 2 + 1]
        parts.append(mixed.astype(BF16))
        qkv_out[:, member * width : (member + 1) * width] = parts[-1]
    save.start(1)
    queries = dot_tt(parts[0], place).astype(BF16)
    keys = dot_nn(place, parts[1]).astype(BF16)
    values = dot_tt(parts[2], place).astype(BF16)
    scale = HEAD_DIM ** (-0.5)
    groups = width // LANES
    for group in range(groups):
        lanes = slice(group * LANES, (group + 1) * LANES)
        for block in range(2):
            slots = slice(block * SLOT, (block + 1) * SLOT)
            own_keys = slice(block * SLOT, block * SLOT + KEYS)
            scores = dot_nn(keys[own_keys, lanes], heads_apart(queries[lanes, slots])) * scale
            scores = scores + bias[group] + jnp.concatenate([mask[block]] * 4, axis=1)
            raised = jnp.exp(scores - jnp.max(scores, axis=0, keepdims=True))
            weights = raised * (1.0 / jnp.sum(raised, axis=0, keepdims=True))
            weights = weights.astype(BF16)
            weights_out[group * 2 + block] = weights
            found = heads_together(dot_nn(values[lanes, own_keys], weights))
            turned[lanes, slots] = found.astype(BF16)
    attended = dot_tt(place, turned[...]).astype(BF16)
    save.start(2)
    save.put(3, attended)
    partial_out[...] = dot_nn(attended, out_held[...]).astype(BF16)
    save.wait()


def attention_forward(layer, streams, vectors, pair_bias, bias, mask, matrix_in, matrix_out, also=(), fetch=()):
    chained = len(streams) > 1
    rows, width = streams[0].shape
    head_width = matrix_out.shape[0]
    put = far if layer in FAR_LAYERS else shape
    spec = IN_HBM if layer in FAR_LAYERS else IN_VMEM
    heads = head_width // HEAD_DIM
    saved = [
        (rows, width),
        (rows, 3 * head_width),
        (2 * head_width // LANES, KEYS, 4 * LANES),
        (rows, head_width),
    ]
    outs = [
        put(saved[0], BF16),
        shape((rows, width), BF16),
        shape((rows, 1), F32),
        *[put(dims, BF16) for dims in saved[1:]],
        shape((rows, width), BF16),
    ]
    out_specs = [spec, IN_VMEM, IN_VMEM, spec, spec, spec, IN_VMEM]
    if chained:
        outs = [shape((rows, width), F32)] + outs
        out_specs = [IN_VMEM] + out_specs
    ins = (*streams, vectors, pair_bias, bias, mask, matrix_in, matrix_out)
    found = kernel_call(
        lambda *refs: attention_body(layer, heads, chained, refs),
        outs,
        out_specs,
        ins,
        [IN_VMEM] * len(ins),
        [pltpu.VMEM((head_width, 2 * SLOT), BF16)]
        + (
            [*[pltpu.VMEM(dims, BF16) for dims in saved], pltpu.SemaphoreType.DMA((4,))]
            if layer in FAR_LAYERS
            else []
        ),
        f"attention_{layer}",
        4,
        also,
        None,
        fetch,
    )
    return found if chained else [streams[0], *found]


def gelu_parts(hidden):
    below = 0.5 * (1.0 + lax.erf(hidden * (0.5**0.5)))
    density = jnp.exp(-0.5 * hidden * hidden) * (0.5 / np.pi) ** 0.5
    return hidden * below, below + hidden * density


def ffn_body(layer, both, image, joined, step, refs):
    base, mine, theirs, vectors, up_bias = refs[:5]
    refs = refs[5:]
    if both:
        grad, keep, refs = refs[0], refs[1], refs[2:]
    if joined:
        prior_sums, refs = refs[0], refs[1:]
    up_held, down_held, *refs = refs
    mid_out, hat_out, rstd_out, partial_out = refs[0], refs[2], refs[3], refs[6]
    far_outs = (refs[1], refs[4], refs[5])
    if both:
        back_out, sums_out, grad_out = refs[7:10]
    held = refs[7:]
    save = Saver(held[:3], far_outs, held[3]) if layer in FAR_LAYERS else Near(far_outs)
    active_out, slope_out = save.held[1:]
    mid = (
        base[...].astype(F32)
        + (mine[...].astype(F32) + theirs[...].astype(F32))
        + vector_row(vectors, ATTENTION_BIAS, layer)
    )
    mid_out[...] = mid
    x_hat, rstd, normed = norm_rows(
        mid, vector_row(vectors, SECOND_GAIN, layer), vector_row(vectors, SECOND_SHIFT, layer)
    )
    save.put(0, normed)
    hat_out[...] = x_hat.astype(BF16)
    rstd_out[...] = rstd
    if both:
        grad_rows = (grad[...].astype(F32) * keep[:, image : image + 1]).astype(BF16)
        grad_out[...] = grad_rows
        put_sums(sums_out, prior_sums if joined else None, [column_sum(grad_rows.astype(F32))])
    forward, backward = None, None
    for start in range(0, up_held.shape[1], step):
        part = slice(start, start + step)
        hidden = dot_nn(normed, up_held[:, part]) + up_bias[layer : layer + 1, part]
        active, slope = gelu_parts(hidden)
        active = active.astype(BF16)
        active_out[:, part] = active
        term = dot_nn(active, down_held[part])
        forward = term if forward is None else forward + term
        if both:
            grad_hidden = (slope * dot_nt(grad_rows, down_held[part])).astype(BF16)
            slope_out[:, part] = grad_hidden
            term = dot_nt(grad_hidden, up_held[:, part])
            backward = term if backward is None else backward + term
        else:
            slope_out[:, part] = slope.astype(BF16)
    save.start(1)
    save.start(2)
    partial_out[...] = forward.astype(BF16)
    if both:
        back_out[...] = backward.astype(BF16)
    save.wait()


def ffn_forward(layer, image, streams, vectors, up_bias, up, down, grad=None, keep=None, prior_sums=None, fetch=()):
    rows, width = streams[0].shape
    units = up.shape[1]
    both = grad is not None
    put = far if layer in FAR_LAYERS else shape
    saved = [(rows, width), (rows, units), (rows, units)]
    outs = [
        shape((rows, width), F32),
        put(saved[0], BF16),
        shape((rows, width), BF16),
        shape((rows, 1), F32),
        put(saved[1], BF16),
        put(saved[2], BF16),
        shape((rows, width), BF16),
    ]
    ins = [*streams, vectors, up_bias]
    if both:
        outs += [shape((rows, width), BF16), shape((8, width), F32), shape((rows, width), BF16)]
        ins += [grad, keep]
    joined = prior_sums is not None
    if joined:
        ins.append(prior_sums)
    specs = [IN_VMEM] * (len(ins) + 2)
    return kernel_call(
        lambda *refs: ffn_body(layer, both, image, joined, units // 3, refs),
        outs,
        [IN_VMEM if put is shape or index not in (1, 4, 5) else IN_HBM for index in range(len(outs))],
        (*ins, up, down),
        specs,
        []
        if put is shape
        else [*[pltpu.VMEM(dims, BF16) for dims in saved], pltpu.SemaphoreType.DMA((3,))],
        f"ffn_both_{layer}" if both else f"ffn_{layer}",
        4.6 if both else 3,
        (),
        None,
        fetch,
    )


def ffn_back_body(layer, joined, step, refs):
    base, mine, theirs, hat, rstd, vectors = refs[:6]
    refs = refs[6:]
    if joined:
        prior_sums, refs = refs[0], refs[1:]
    slope_hbm, up_held, down_held = refs[:3]
    grad_out, low_out, hidden_out, partial_out, sums_out = refs[3:8]
    slope, load = slope_hbm, Near([slope_hbm])
    if layer in FAR_LAYERS:
        slope = refs[8]
        load = Loader([slope_hbm], [slope], refs[9])
    grad_normed = mine[...].astype(F32) + theirs[...].astype(F32)
    x_hat = hat[...].astype(F32)
    grad = base[...] + norm_back(
        grad_normed, x_hat, rstd[...], vector_row(vectors, FIRST_GAIN, layer + 1)
    )
    grad_out[...] = grad
    low = grad.astype(BF16)
    low_out[...] = low
    sums = [column_sum(grad_normed * x_hat), column_sum(grad_normed), column_sum(grad)]
    put_sums(sums_out, prior_sums if joined else None, sums)
    backward = None
    load.get(0)
    for start in range(0, up_held.shape[1], step):
        part = slice(start, start + step)
        grad_hidden = (slope[:, part].astype(F32) * dot_nt(low, down_held[part])).astype(BF16)
        hidden_out[:, part] = grad_hidden
        term = dot_nt(grad_hidden, up_held[:, part])
        backward = term if backward is None else backward + term
    partial_out[...] = backward.astype(BF16)


def ffn_backward(layer, grads, hat, rstd, vectors, slope, up, down, prior_sums=None, micros=4, fetch=()):
    rows, width = grads[0].shape
    units = up.shape[1]
    outs = [
        shape((rows, width), F32),
        shape((rows, width), BF16),
        shape((rows, units), BF16),
        shape((rows, width), BF16),
        shape((8, width), F32),
    ]
    ins = [*grads, hat, rstd, vectors]
    joined = prior_sums is not None
    if joined:
        ins.append(prior_sums)
    return kernel_call(
        lambda *refs: ffn_back_body(layer, joined, units // 3, refs),
        outs,
        [IN_VMEM] * 5,
        (*ins, slope, up, down),
        [IN_VMEM] * len(ins) + [IN_HBM if layer in FAR_LAYERS else IN_VMEM] + [IN_VMEM] * 2,
        [pltpu.VMEM((rows, units), BF16), pltpu.SemaphoreType.DMA((1,))]
        if layer in FAR_LAYERS
        else [],
        f"ffn_back_{layer}",
        micros,
        (),
        None,
        fetch,
    )


def attention_back_body(layer, heads, joined, refs):
    base, mine, theirs, hat, rstd, vectors, first_hat = refs[:7]
    refs = refs[7:]
    if joined:
        prior_sums, prior_table = refs[:2]
        refs = refs[2:]
    qkv, weights, in_held, out_held = refs[:4]
    grad_out, low_out, mixed_out, partial_out, sums_out, table_out = refs[4:10]
    turned, merged, diagonals = refs[10:13]
    load = Near([qkv, weights])
    if layer in FAR_LAYERS:
        load = Loader([qkv, weights], refs[13:15], refs[15])
        qkv, weights = refs[13:15]
    width = heads * HEAD_DIM
    per_group = LANES // HEAD_DIM
    grad_normed = mine[...].astype(F32) + theirs[...].astype(F32)
    x_hat = hat[...].astype(F32)
    grad = base[...].astype(F32) + norm_back(
        grad_normed, x_hat, rstd[...], vector_row(vectors, SECOND_GAIN, layer)
    )
    grad_out[...] = grad
    low = grad.astype(BF16)
    low_out[...] = low
    sums = [column_sum(grad_normed * x_hat), column_sum(grad_normed), column_sum(grad)]
    place = place_matrix(layer)
    load.get(0)
    queries = dot_nn(place, qkv[:, :width]).astype(BF16)
    turned_keys = dot_tt(qkv[:, width : 2 * width], place).astype(BF16)
    values = dot_nn(place, qkv[:, 2 * width :]).astype(BF16)
    grad_attended = dot_nt(low, out_held[...]).astype(BF16)
    grad_slots = dot_nn(place, grad_attended).astype(BF16)
    grad_turned = dot_tt(grad_attended, place).astype(BF16)
    load.get(1)
    scale = HEAD_DIM ** (-0.5)
    empty = jnp.zeros((SLOT - KEYS, LANES), BF16)
    for group in range(width // LANES):
        lanes = slice(group * LANES, (group + 1) * LANES)
        total = None
        for block in range(2):
            top_row = block * SLOT
            slots = slice(top_row, top_row + SLOT)
            own_keys = slice(top_row, top_row + KEYS)
            low_weights = weights[group * 2 + block]
            full = low_weights.astype(F32)
            grad_weights = dot_nn(values[own_keys, lanes], heads_apart(grad_turned[lanes, slots]))
            spread = jnp.sum(full * grad_weights, axis=0, keepdims=True)
            grad_scores = full * (grad_weights - spread)
            total = grad_scores if total is None else total + grad_scores
            grad_raw = (grad_scores * scale).astype(BF16)
            grad_query = heads_together(dot_nn(turned_keys[lanes, own_keys], grad_raw))
            grad_key = dot_nn(grad_raw, head_rows(queries[slots, lanes]))
            grad_value = dot_nn(low_weights, head_rows(grad_slots[slots, lanes]))
            turned[lanes, slots] = grad_query.astype(BF16)
            for at, found in ((0, grad_key), (width, grad_value)):
                columns = slice(at + group * LANES, at + (group + 1) * LANES)
                merged[own_keys, columns] = found.astype(BF16)
                merged[top_row + KEYS : top_row + SLOT, columns] = empty
        for member in range(per_group):
            head = group * per_group + member
            own = total[:, member * LANES : (member + 1) * LANES]
            wide = jnp.concatenate([own, jnp.zeros_like(own)], axis=1)
            line = None
            for start in range(0, KEYS, 8):
                rows = wide[start : start + 8]
                if start:
                    rows = pltpu.roll(rows, TURN - start, 1)
                line = rows if line is None else line + rows
            diagonals[head * 8 : head * 8 + 8] = line
    mixed = [dot_tt(place, turned[...]).astype(BF16)]
    both = dot_tn(place, merged[...]).astype(BF16)
    mixed += [both[:, :width], both[:, width:]]
    mixed_out[:, :width] = mixed[0]
    mixed_out[:, width:] = both
    partial = dot_nt(mixed[0], in_held[0])
    partial = partial + dot_nt(mixed[1], in_held[1])
    partial = partial + dot_nt(mixed[2], in_held[2])
    partial_out[...] = partial.astype(BF16)
    sums += [column_sum(partial * first_hat[...].astype(F32)), column_sum(partial)]
    put_sums(sums_out, prior_sums if joined else None, sums)
    lines = diagonals[...]
    row = lax.broadcasted_iota(jnp.int32, lines.shape, 0)
    for bit in range(3):
        moved = pltpu.roll(lines, TURN - (1 << bit), 1)
        lines = jnp.where(((row >> bit) & 1) == 1, moved, lines)
    lines = jnp.sum(lines.reshape(heads, 8, TURN), axis=1)
    table = dot_full(lines, offset_matrix(), ((1,), (1,)))
    table_out[...] = table + prior_table[...] if joined else table


def attention_backward(
    layer, grads, hat, rstd, vectors, first_hat, qkv, weights, matrix_in, matrix_out,
    prior=(), micros=5, fetch=(),
):
    rows, width = grads[0].shape
    head_width = matrix_out.shape[0]
    heads = head_width // HEAD_DIM
    outs = [
        shape((rows, width), F32),
        shape((rows, width), BF16),
        shape((rows, 3 * head_width), BF16),
        shape((rows, width), BF16),
        shape((8, width), F32),
        shape((heads, SPAN * SPAN), F32),
    ]
    ins = (*grads, hat, rstd, vectors, first_hat, *prior)
    return kernel_call(
        lambda *refs: attention_back_body(layer, heads, bool(prior), refs),
        outs,
        [IN_VMEM] * 6,
        (*ins, qkv, weights, matrix_in, matrix_out),
        [IN_VMEM] * len(ins) + [IN_HBM if layer in FAR_LAYERS else IN_VMEM] * 2 + [IN_VMEM] * 2,
        [
            pltpu.VMEM((head_width, 2 * SLOT), BF16),
            pltpu.VMEM((2 * SLOT, 2 * head_width), BF16),
            pltpu.VMEM((heads * 8, TURN), F32),
        ]
        + (
            [
                pltpu.VMEM(qkv.shape, BF16),
                pltpu.VMEM(weights.shape, BF16),
                pltpu.SemaphoreType.DMA((2,)),
            ]
            if layer in FAR_LAYERS
            else []
        ),
        f"attention_back_{layer}",
        micros,
        (),
        None,
        fetch,
    )


def finish_body(base, mine, theirs, hat, rstd, vectors, out):
    grad_normed = mine[...].astype(F32) + theirs[...].astype(F32)
    out[...] = base[...] + norm_back(
        grad_normed, hat[...].astype(F32), rstd[...], vector_row(vectors, FIRST_GAIN, 0)
    )


def output_body(layer, base, mine, theirs, vectors, out):
    total = base[...] + (mine[...].astype(F32) + theirs[...].astype(F32))
    out[...] = (total + vector_row(vectors, REDUCE_BIAS, layer)).astype(BF16)


def finish(body, kind, name, micros, *ins):
    return kernel_call(
        body, pltpu.HBM(ins[0].shape, kind), IN_VMEM, ins, [IN_VMEM] * len(ins), [], name, micros
    )


def group_place(group, top, order):
    place = 0
    for step, bit in enumerate(order):
        place = place + ((((group >> bit) & 1) ^ ((top >> bit) & 1)) << (len(order) - 1 - step))
    return place


def grads_body(pairs, groups, order, step, summed, far_ins, refs):
    top = refs[0][0]
    lefts = 1 + max(left for left, _ in pairs)
    rights = len(pairs)
    refs = refs[1:]
    total = 2 * (lefts + rights)
    sources, refs = refs[:total], refs[total:]
    held_ins = list(sources)
    far_count = sum(far_ins)
    if far_count:
        scratch, sems, refs = refs[-far_count - 1 : -1], refs[-1], refs[: -far_count - 1]
        loader = Loader([item for item, is_far in zip(sources, far_ins) if is_far], scratch, sems)
        places = [index for index, is_far in enumerate(far_ins) if is_far]

    def get(index):
        return loader.get(places.index(index)) if far_ins[index] else held_ins[index]

    keep_out, sums_out, held, turned, wide, sems = (refs[0], *refs[-5:])
    send_outs = refs[1:-5]
    rows = sources[0].shape[0]
    space = wide.shape[0] // 2
    empty = space - rows
    block = keep_out.shape[1]
    copies = []
    for left in range(lefts):
        for image in range(2):
            start = image * space
            turned[left, :, start + LANES : start + space] = jnp.zeros(
                (turned.shape[1], space - LANES), BF16
            )
            turned[left, :, start : start + rows] = get(2 * left + image)[...].T
    at = 0
    sum_at = 0
    for right, (left, _) in enumerate(pairs):
        columns = sources[2 * (lefts + right)].shape[1]
        for image in range(2):
            start = image * space
            wide[start : start + rows, :columns] = get(2 * (lefts + right) + image)[...]
            wide[start + rows : start + space, :columns] = jnp.zeros((empty, columns), BF16)
        if summed[right]:
            sums_out[0:1, sum_at : sum_at + columns] = column_sum(wide[:, :columns].astype(F32))
            sum_at += columns
        for first in range(0, columns, step):
            found = dot_nn(turned[left], wide[:, first : first + step]).astype(BF16)
            for group in range(groups):
                held[group_place(group, top, order), :, at : at + step] = found[
                    group * block : (group + 1) * block
                ]
            sent = at // send_outs[0].shape[2]
            inner = at - sent * send_outs[0].shape[2]
            for half, out in (
                (0, keep_out.at[:, :, at : at + step]),
                (1, send_outs[sent].at[:, :, inner : inner + step]),
            ):
                copy = pltpu.make_async_copy(
                    held.at[half * groups // 2 : (half + 1) * groups // 2, :, at : at + step],
                    out,
                    sems.at[half, at // step],
                )
                copy.start()
                copies.append(copy)
            at += step
    for copy in copies:
        copy.wait()


def weight_grads(top, groups, order, pairs, lefts, rights, summed, pieces, far_ins, name, micros):
    width = lefts[0].shape[1]
    step = 512 if all(item.shape[1] % 512 == 0 for item in rights) else 384
    columns = sum(item.shape[1] for item in rights[::2])
    widest = max(item.shape[1] for item in rights)
    space = 2 * LANES
    summed_columns = sum(item.shape[1] for item, used in zip(rights[::2], summed) if used)
    outs = [
        shape((groups // 2, width // groups, columns), BF16),
        *[shape((groups // 2, width // groups, columns // pieces), BF16)] * pieces,
        shape((8, summed_columns), F32),
    ]
    count = 1 + max(left for left, _ in pairs)
    kept, *sent, sums = kernel_call(
        lambda *refs: grads_body(pairs, groups, order, step, summed, far_ins, refs),
        outs,
        [ANYWHERE] * (1 + pieces) + [IN_VMEM],
        (top, *lefts, *rights),
        [IN_SMEM] + [IN_HBM if is_far else IN_VMEM for is_far in far_ins],
        [
            pltpu.VMEM((groups, width // groups, columns), BF16),
            pltpu.VMEM((count, width, 2 * space), BF16),
            pltpu.VMEM((2 * space, widest), BF16),
            pltpu.SemaphoreType.DMA((2, columns // step)),
            *[
                pltpu.VMEM(item.shape, item.dtype)
                for item, is_far in zip((*lefts, *rights), far_ins)
                if is_far
            ],
            *([pltpu.SemaphoreType.DMA((sum(far_ins),))] if any(far_ins) else []),
        ],
        name,
        micros,
        (),
        20 * 1024 * 1024,
    )
    return kept, sent, sums


def swap(value):
    return lax.ppermute(value, "mp", [(0, 1), (1, 0)])


def trade(value, bit, size):
    return lax.ppermute(value, "dp", [(source, source ^ bit) for source in range(size)])


def fold_body(kept, *refs):
    *pieces, keep_out, send_out = refs
    half = keep_out.shape[0]
    at = 0
    for found in pieces:
        columns = slice(at, at + found.shape[2])
        at += found.shape[2]
        for start, out in ((0, keep_out), (half, send_out)):
            for block in range(half):
                total = kept[start + block, :, columns].astype(F32) + found[start + block].astype(F32)
                out[block, :, columns] = total.astype(BF16)


def fold(kept, found, name):
    half = shape((kept.shape[0] // 2, *kept.shape[1:]), BF16)
    return kernel_call(
        fold_body, [half, half], [IN_VMEM] * 2, (kept, *found), [IN_VMEM] * (1 + len(found)), [],
        name, 0.1,
    )


class Scatter:
    def __init__(self, kept, sent, order, size, name):
        self.kept, self.sent, self.order, self.size, self.name = kept, sent, order, size, name
        self.finer = size >> len(order)
        self.level = 0
        self.send()

    def send(self):
        self.found = [
            trade(item, self.finer << self.order[self.level], self.size) for item in self.sent
        ]

    def step(self):
        if self.level + 1 < len(self.order):
            self.kept, sent = fold(self.kept, self.found, f"{self.name}_{self.level}")
            self.sent = [sent]
            self.level += 1
            self.send()

    def finish(self):
        for _ in self.order:
            self.step()
        kept, finer = self.kept, self.finer
        found = jnp.concatenate(self.found, axis=2) if len(self.found) > 1 else self.found[0]
        rank = lax.axis_index("dp")
        while finer > 1:
            finer //= 2
            held = (kept.astype(F32) + found.astype(F32)).astype(BF16)
            halves = held.reshape((2, 1, held.shape[1] // 2, held.shape[2]))
            mine = (rank // finer) % 2
            kept = lax.dynamic_index_in_dim(halves, mine, 0, keepdims=False)
            found = trade(lax.dynamic_index_in_dim(halves, 1 - mine, 0, keepdims=False), finer, self.size)
        return kept, found

    def join(self):
        kept, found = self.finish()
        return (
            kernel_call(
                add_body, shape(kept.shape, F32), IN_VMEM, (kept, found), [IN_VMEM] * 2, [],
                f"{self.name}_end", 0.1,
            ),
        )


def add_body(left, right, out):
    out[...] = left[...].astype(F32) + right[...].astype(F32)


def some_bits(name, size):
    bits = range(size.bit_length() - 1)
    listed = [bit for bit in BIT_ORDER[name] if bit in bits]
    return tuple(listed + [bit for bit in bits if bit not in listed])


class Total:
    def __init__(self, value, size):
        self.value, self.size = value, size
        self.left = [1 << bit for bit in some_bits("total", size)]
        self.send()

    def send(self):
        self.found = trade(self.value, self.left.pop(0), self.size)

    def step(self):
        if self.left:
            self.value = kernel_call(
                add_body, shape(self.value.shape, F32), IN_VMEM, (self.value, self.found),
                [IN_VMEM] * 2, [], "total", 0.1,
            )
            self.send()

    def finish(self):
        while self.left:
            self.step()
        return self.value, self.found


def collect_body(counts, widths, refs):
    outs = refs[sum(counts) :]
    for layer, count in enumerate(counts):
        total = refs[0][0].astype(F32)
        if count == 2:
            total = total + refs[1][0].astype(F32)
        refs = refs[count:]
        at = 0
        for out, parts in zip(outs, widths):
            for part in range(parts):
                columns = out.shape[-1]
                if len(out.shape) == 4:
                    out[layer, part] = total[:, at : at + columns]
                else:
                    out[layer] = total[:, at : at + columns]
                at += columns


def collect(pairs, shapes, name):
    flat = [item for pair in pairs for item in pair]
    counts = [len(pair) for pair in pairs]
    return kernel_call(
        lambda *refs: collect_body(
            counts, [dims[1] if len(dims) == 4 else 1 for dims in shapes], refs
        ),
        [pltpu.HBM(dims, F32) for dims in shapes],
        [IN_VMEM] * len(shapes),
        flat,
        [IN_VMEM] * len(flat),
        [],
        name,
        0.1,
    )


def pack_body(width, layers, refs):
    sums_0, theirs_0, sums_low, sums_1, last = refs[:5]
    ups, mixes, tables = refs[5 : 5 + layers], refs[5 + layers : 5 + 2 * layers], refs[5 + 2 * layers : -1]
    out = refs[-1]
    out[...] = jnp.zeros(out.shape, F32)
    out[0:2] = sums_0[3:5] + theirs_0[3:5]
    out[2:3] = sums_0[2:3]
    out[3:5] = sums_0[0:2]
    out[5:6] = sums_low[2:3]
    out[6:8] = sums_low[0:2]
    out[8:9] = sums_1[2:3]
    out[9:11] = sums_1[0:2]
    out[11:12] = last[0:1]
    row = 6 * layers
    for item in ups:
        for start in range(0, item.shape[1], width):
            out[row : row + 1] = item[0:1, start : start + width]
            row += 1
    third = mixes[0].shape[1] // 3
    for item in mixes:
        out[row : row + 1, :third] = item[0:1, :third]
        out[row : row + 1, third : 2 * third] = item[0:1, 2 * third :]
        row += 1
    for item in tables:
        heads, offsets = item.shape
        for head in range(heads):
            lane = head * TURN % width
            out[row : row + 1, lane : lane + offsets] = item[head : head + 1]
            if (head + 1) * TURN % width == 0:
                row += 1


def unpack_body(refs):
    packed, found, vectors, up_bias, pair_bias, tables = refs
    width = packed.shape[1]
    layers, units = up_bias.shape
    total = packed[...] + found[...]
    for layer in range(layers):
        for member in range(6):
            vectors[member, layer : layer + 1] = total[6 * layer + member : 6 * layer + member + 1]
    row = 6 * layers
    for layer in range(layers):
        for start in range(0, units, width):
            up_bias[layer : layer + 1, start : start + width] = total[row : row + 1]
            row += 1
    third = pair_bias.shape[2]
    for layer in range(layers):
        for member in range(2):
            pair_bias[layer, member : member + 1] = total[
                row : row + 1, member * third : (member + 1) * third
            ]
        row += 1
    heads, _, offsets = tables.shape
    for layer in range(layers):
        for head in range(heads):
            lane = head * TURN % width
            tables[head, layer : layer + 1] = total[row : row + 1, lane : lane + offsets]
            if (head + 1) * TURN % width == 0:
                row += 1


def shards(
    tokens,
    keep_mask,
    cotangent,
    first_gain,
    first_shift,
    attention_in,
    query_value_bias,
    position_table,
    attention_out,
    attention_bias,
    second_gain,
    second_shift,
    expand_weight,
    expand_bias,
    reduce_weight,
    reduce_bias,
):
    LINE.clear()
    FETCHED.clear()
    size = lax.axis_size("dp")
    half = lax.axis_index("mp")
    groups = min(16, size)
    top = (lax.axis_index("dp") // (size // groups)).astype(jnp.int32).reshape(1)
    layers, width = first_gain.shape
    head_width = attention_out.shape[1]
    units = expand_weight.shape[2]
    heads = head_width // HEAD_DIM
    matrix_in = jnp.transpose(attention_in, (0, 2, 1, 3))
    own_half = half.astype(jnp.int32).reshape(1)
    bias, masks, (keep_columns, vectors, tokens, cotangent, up_bias, pair_bias) = make_tables(
        own_half, jnp.transpose(position_table, (1, 0, 2)), keep_mask,
        (tokens, cotangent, expand_bias, query_value_bias),
        (first_gain, first_shift, attention_bias, second_gain, second_shift, reduce_bias),
        ((matrix_in, 0), (attention_out, 0)), (top,),
    )
    heads_held = list(FETCHED)
    other_tokens = swap(tokens)
    other_cotangent = swap(cotangent)

    def attend(layer, image, streams, also=(), fetch=()):
        return attention_forward(
            layer, streams, vectors, pair_bias, bias[layer], masks[layer][image], *heads_held,
            also, fetch,
        )

    def feed(layer, image, streams, grad=None, prior_sums=None, fetch=()):
        return ffn_forward(
            layer, image, streams, vectors, up_bias, *units_held, grad, keep_columns, prior_sums,
            fetch,
        )

    att, ffn = [[None, None], [None, None]], [[None, None], [None, None]]
    att[0][0] = attend(0, 0, (tokens,))
    sent_own = swap(att[0][0][7])
    att[0][1] = attend(
        0, 1, (other_tokens,), (other_cotangent,), ((expand_weight, 0), (reduce_weight, 0))
    )
    units_held = list(FETCHED)
    sent_other = swap(att[0][1][7])
    ffn[0][1] = feed(
        0, 1, (att[0][1][0], att[0][1][7], sent_own), fetch=((matrix_in, 1), (attention_out, 1))
    )
    heads_held = list(FETCHED)
    sent_2 = swap(ffn[0][1][6])
    ffn[0][0] = feed(0, 0, (att[0][0][0], att[0][0][7], sent_other))
    sent_1 = swap(ffn[0][0][6])
    att[1][0] = attend(1, 0, (ffn[0][0][0], ffn[0][0][6], sent_2))
    sent_own = swap(att[1][0][7])
    att[1][1] = attend(
        1, 1, (ffn[0][1][0], ffn[0][1][6], sent_1), (), ((expand_weight, 1), (reduce_weight, 1))
    )
    units_held = list(FETCHED)
    sent_other = swap(att[1][1][7])

    far_ins = (True, True, False, False, False, False, True, True)

    def ffn_grads(layer, low, hidden, name):
        normed = [ffn[layer][image][1] for image in range(2)]
        active = [ffn[layer][image][4] for image in range(2)]
        order = some_bits(f"ffn_{layer}", groups)
        kept, sent, sums = weight_grads(
            top, groups, order, ((0, 0), (1, 1)), (*normed, *low), (*hidden, *active),
            (True, False), PIECES["ffn"], far_ins if layer in FAR_LAYERS else (False,) * 8, name, MICROS[name],
        )
        return Scatter(kept, sent, order, size, f"ffn_fold_{layer}"), sums

    def attention_grads(layer, low, mixed, name):
        normed = [att[layer][image][1] for image in range(2)]
        attended = [att[layer][image][6] for image in range(2)]
        order = some_bits(f"attention_{layer}", groups)
        kept, sent, sums = weight_grads(
            top, groups, order, ((0, 0), (1, 1)), (*normed, *low), (*mixed, *attended),
            (True, False), PIECES["attention"], far_ins if layer in FAR_LAYERS else (False,) * 8, name, MICROS[name],
        )
        return Scatter(kept, sent, order, size, f"attention_fold_{layer}"), sums

    def attend_back(layer, image, grads, prior=(), micros=5, fetch=()):
        held = att[layer][image]
        return attention_backward(
            layer, grads, ffn[layer][image][2], ffn[layer][image][3], vectors, held[2],
            held[4], held[5], *later["heads"], prior, micros, fetch,
        )

    def feed_back(image, grads, prior_sums=None, micros=4, fetch=()):
        held = att[1][image]
        return ffn_backward(
            0, grads, held[2], held[3], vectors, ffn[0][image][5], *later["units"],
            prior_sums, micros, fetch,
        )

    back, low = [[None, None], [None, None]], [None, None]
    later = {"heads": heads_held, "units": None}
    sent, sums, extra, outs = {}, {}, {}, {}
    rows = width // size

    def ffn_1_other():
        ffn[1][1] = feed(1, 1, (att[1][1][0], att[1][1][7], sent_own), other_cotangent)
        sent["ffn_1_other"] = swap(ffn[1][1][7])
        sent["block"] = swap(ffn[1][1][6])

    def ffn_1_own():
        ffn[1][0] = feed(1, 0, (att[1][0][0], att[1][0][7], sent_other), cotangent, ffn[1][1][8])
        sent["ffn_1_own"] = swap(ffn[1][0][7])

    def ffn_grads_1():
        sums["ffn_sum_1"], extra["up_1"] = ffn_grads(
            1, (ffn[1][0][9], ffn[1][1][9]), (ffn[1][0][5], ffn[1][1][5]), "ffn_grads_1"
        )

    def attention_back_1_own():
        back[1][0] = attend_back(
            1, 0, (ffn[1][0][9], ffn[1][0][7], sent["ffn_1_other"]), (),
            MICROS["attention_back_1_own"], ((expand_weight, 0), (reduce_weight, 0)),
        )
        later["units"] = list(FETCHED)
        sent["back_1_own"] = swap(back[1][0][3])

    def attention_back_1_other():
        back[1][1] = attend_back(
            1, 1, (ffn[1][1][9], ffn[1][1][7], sent["ffn_1_own"]), back[1][0][4:6],
            MICROS["attention_back_1_other"],
        )
        sent["back_1_other"] = swap(back[1][1][3])

    def attention_grads_1():
        sums["attention_sum_1"], extra["mixed_1"] = attention_grads(
            1, (back[1][0][1], back[1][1][1]), (back[1][0][2], back[1][1][2]), "attention_grads_1"
        )

    def ffn_back_0_other():
        low[1] = feed_back(
            1, (back[1][1][0], back[1][1][3], sent["back_1_own"]), None,
            MICROS["ffn_back_0_other"], ((matrix_in, 0), (attention_out, 0)),
        )
        later["heads"] = list(FETCHED)
        sent["low_other"] = swap(low[1][3])

    def ffn_back_0_own():
        low[0] = feed_back(
            0, (back[1][0][0], back[1][0][3], sent["back_1_other"]), low[1][4],
            MICROS["ffn_back_0_own"],
        )
        sent["low_own"] = swap(low[0][3])

    def ffn_grads_0():
        sums["ffn_sum_0"], extra["up_0"] = ffn_grads(
            0, (low[0][1], low[1][1]), (low[0][2], low[1][2]), "ffn_grads_0"
        )

    def attention_back_0_own():
        back[0][0] = attend_back(
            0, 0, (low[0][0], low[0][3], sent["low_other"]), (), MICROS["attention_back_0_own"]
        )

    def attention_back_0_other():
        back[0][1] = attend_back(
            0, 1, (low[1][0], low[1][3], sent["low_own"]), back[0][0][4:6],
            MICROS["attention_back_0_other"],
        )
        sent["last"] = swap(back[0][1][3])
        sent["sums"] = swap(back[0][1][4])

    def attention_grads_0():
        sums["attention_sum_0"], extra["mixed_0"] = attention_grads(
            0, (back[0][0][1], back[0][1][1]), (back[0][0][2], back[0][1][2]), "attention_grads_0"
        )

    def pack():
        pieces = (
            back[0][1][4], sent["sums"], low[0][4], back[1][1][4], ffn[1][0][8],
            extra["up_0"], extra["up_1"], extra["mixed_0"], extra["mixed_1"],
            back[0][1][5], back[1][1][5],
        )
        per_row = width // TURN
        count = layers * (6 + units // width + 1 + heads // per_row)
        packed = kernel_call(
            lambda *refs: pack_body(width, layers, refs),
            shape((-(-count // 8) * 8, width), F32),
            IN_VMEM,
            pieces,
            [IN_VMEM] * len(pieces),
            [],
            "pack",
            MICROS["pack"],
        )
        sums["total"] = Total(packed, size)

    def unpack():
        outs["small"] = kernel_call(
            lambda *refs: unpack_body(refs),
            [
                shape((6, layers, width), F32),
                shape((layers, units), F32),
                shape((layers, 2, head_width), F32),
                shape((heads, layers, SPAN * SPAN), F32),
            ],
            [IN_VMEM] * 4,
            sums["total"].finish(),
            [IN_VMEM] * 2,
            [],
            "unpack",
            0.1,
        )

    def tokens_grad():
        outs["tokens_grad"] = finish(
            finish_body, F32, "finish", 0.1,
            back[0][0][0], back[0][0][3], sent["last"], att[0][0][2], att[0][0][3], vectors,
        )

    def block_output():
        outs["block_output"] = finish(
            lambda *refs: output_body(1, *refs), BF16, "output", 0.1,
            ffn[1][0][0], ffn[1][0][6], sent["block"], vectors,
        )

    def attention_end_1():
        extra["attention_1"] = sums["attention_sum_1"].join()

    def ffn_end_1():
        extra["ffn_1"] = sums["ffn_sum_1"].join()

    def attention_outputs():
        outs["attention"] = collect(
            (sums["attention_sum_0"].finish(), extra["attention_1"]),
            [(layers, 3, rows, head_width), (layers, rows, head_width)],
            "attention_collect",
        )

    def ffn_outputs():
        outs["ffn"] = collect(
            (sums["ffn_sum_0"].finish(), extra["ffn_1"]), [(layers, rows, units)] * 2, "ffn_collect"
        )

    steps = {
        item.__name__: item
        for item in (
            ffn_1_other, ffn_1_own, ffn_grads_1, attention_back_1_own, attention_back_1_other,
            attention_grads_1, ffn_back_0_other, ffn_back_0_own, ffn_grads_0,
            attention_back_0_own, attention_back_0_other, attention_grads_0, pack, unpack,
            tokens_grad, block_output, attention_end_1, ffn_end_1, attention_outputs, ffn_outputs,
        )
    }
    for name in PLAN:
        if name in steps:
            steps[name]()
        else:
            sums[name].step()

    in_grad, out_grad = outs["attention"]
    up_grad, down_grad = outs["ffn"]
    vector_grads, expand_bias_grad, pair_grad, table_grad = outs["small"]
    return (
        outs["block_output"],
        outs["tokens_grad"],
        jnp.transpose(in_grad, (0, 2, 1, 3)),
        jnp.transpose(out_grad, (0, 2, 1)),
        up_grad,
        jnp.transpose(down_grad, (0, 2, 1)),
        pair_grad,
        expand_bias_grad,
        jnp.transpose(table_grad, (1, 0, 2)),
        jnp.transpose(vector_grads, (1, 0, 2)),
    )


def solution(mesh):
    return jax.shard_map(
        shards,
        mesh=mesh,
        in_specs=(
            P(("dp", "mp"), None),
            P("dp", None),
            P(("dp", "mp"), None),
            P(),
            P(),
            P(None, None, None, "mp"),
            P(None, None, "mp"),
            P(None, "mp", None),
            P(None, "mp", None),
            P(),
            P(),
            P(),
            P(None, None, "mp"),
            P(None, "mp"),
            P(None, "mp", None),
            P(),
        ),
        out_specs=(
            P(("dp", "mp"), None),
            P(("dp", "mp"), None),
            P(None, "dp", None, "mp"),
            P(None, "mp", "dp"),
            P(None, "dp", "mp"),
            P(None, "mp", "dp"),
            P(None, None, "mp"),
            P(None, "mp"),
            P(None, "mp", None),
            P(),
        ),
        check_vma=False,
    )
```

```python
import jax
import jax.numpy as jnp
import numpy as np
from jax import lax
from jax.experimental import pallas as pl
from jax.experimental.pallas import tpu as pltpu
from jax.sharding import PartitionSpec as P

HEAD_DIM = 32
GRID = 14
WIN = 7
SHIFT = 3
PATCHES = 196
BLOCK = 98
SLOT = 128
KEYS = 112
LANES = 128
SPAN = 2 * WIN - 1
TURN = 256

EPSILON = 1e-05
MASKED = -1e30
F32 = jnp.float32
BF16 = jnp.bfloat16
VMEM_LIMIT = 14 * 1024 * 1024

IN_VMEM = pl.BlockSpec(memory_space=pltpu.VMEM)
IN_SMEM = pl.BlockSpec(memory_space=pltpu.SMEM)
ANYWHERE = pl.BlockSpec(memory_space=pl.ANY)
IN_HBM = pl.BlockSpec(memory_space=pltpu.HBM)


def shape(dims, kind):
    return jax.ShapeDtypeStruct(dims, kind)


def far(dims, kind):
    return pltpu.HBM(dims, kind)


class Saver:
    def __init__(self, held, outs, sems):
        self.held, self.outs, self.sems = held, outs, sems
        self.copies = []

    def put(self, index, value):
        self.held[index][...] = value
        self.start(index)

    def start(self, index):
        copy = pltpu.make_async_copy(self.held[index], self.outs[index], self.sems.at[index])
        copy.start()
        self.copies.append(copy)

    def wait(self):
        for copy in self.copies:
            copy.wait()


class Near:
    def __init__(self, held):
        self.held = held

    def put(self, index, value):
        self.held[index][...] = value

    def get(self, index):
        return self.held[index]

    def start(self, index):
        pass

    def wait(self):
        pass


class Loader:
    def __init__(self, sources, held, sems):
        self.held = held
        self.copies = [
            pltpu.make_async_copy(source, target, sems.at[index])
            for index, (source, target) in enumerate(zip(sources, held))
        ]
        self.waiting = set(range(len(held)))
        for copy in self.copies:
            copy.start()

    def get(self, index):
        if index in self.waiting:
            self.waiting.remove(index)
            self.copies[index].wait()
        return self.held[index]


FETCHED = []
LINE = []
COST = 1.0e9
FAR_LAYERS = ()
PLAN = (
    "ffn_1_other",
    "ffn_1_own",
    "ffn_grads_1",
    "attention_back_1_own",
    "ffn_sum_1",
    "attention_back_1_other",
    "attention_grads_1",
    "ffn_back_0_other",
    "ffn_back_0_own",
    "ffn_grads_0",
    "attention_sum_1",
    "ffn_sum_1",
    "ffn_sum_0",
    "attention_back_0_own",
    "attention_sum_1",
    "attention_back_0_other",
    "attention_grads_0",
    "ffn_sum_1",
    "pack",
    "attention_sum_0",
    "ffn_sum_0",
    "ffn_end_1",
    "attention_sum_0",
    "attention_sum_1",
    "attention_sum_0",
    "tokens_grad",
    "ffn_sum_0",
    "total",
    "attention_end_1",
    "block_output",
    "attention_outputs",
    "total",
    "total",
    "ffn_outputs",
    "unpack",
)
MICROS = {
    "attention_back_1_own": 14.22,
    "attention_back_1_other": 0.06,
    "attention_grads_1": 0.81,
    "ffn_back_0_other": 1.81,
    "ffn_back_0_own": 0.26,
    "ffn_grads_0": 0.1,
    "attention_back_0_own": 0.36,
    "attention_back_0_other": 0.33,
    "attention_grads_0": 0.17,
    "pack": 0.44,
    "ffn_grads_1": 0.3,
}
PIECES = {"ffn": 3, "attention": 2}
BIT_ORDER = {
    "ffn_1": (0, 2, 1, 3),
    "attention_1": (0, 1, 2, 3),
    "ffn_0": (0, 2, 1, 3),
    "attention_0": (0, 1, 2, 3),
    "total": (0, 2, 1, 3),
}


def kernel_call(body, outs, out_specs, ins, in_specs, scratch, name, micros, also=(), limit=None, fetch=()
):
    behind = [item for item in (*LINE, *also) if not any(item is used for used in ins)]
    skipped = len(behind)
    ins = [
        pltpu.with_memory_space_constraint(item, pltpu.HBM) if spec is IN_HBM else item
        for item, spec in zip(ins, in_specs)
    ]
    flat = outs if isinstance(outs, list) else [outs]
    flat_specs = out_specs if isinstance(out_specs, list) else [out_specs]
    count, near_count = len(fetch), len(ins)

    def whole(*refs):
        refs = refs[skipped:]
        own_ins, sources, refs = refs[:near_count], refs[near_count : near_count + count], refs[near_count + count :]
        own_outs, targets, refs = refs[: len(flat)], refs[len(flat) : len(flat) + count], refs[len(flat) + count :]
        copies = []
        if count:
            refs, sems = refs[:-1], refs[-1]
            for index, (_, layer) in enumerate(fetch):
                copy = pltpu.make_async_copy(
                    sources[index].at[layer], targets[index], sems.at[index]
                )
                copy.start()
                copies.append(copy)
        body(*own_ins, *own_outs, *refs)
        for copy in copies:
            copy.wait()

    found = pl.pallas_call(
        whole,
        out_shape=flat + [shape(item.shape[1:], item.dtype) for item, _ in fetch],
        in_specs=[ANYWHERE] * skipped + in_specs + [IN_HBM] * count,
        out_specs=flat_specs + [IN_VMEM] * count,
        scratch_shapes=list(scratch) + ([pltpu.SemaphoreType.DMA((count,))] if count else []),
        compiler_params=pltpu.CompilerParams(vmem_limit_bytes=limit or VMEM_LIMIT),
        cost_estimate=pl.CostEstimate(
            flops=int(micros * COST), bytes_accessed=1024, transcendentals=0
        ),
        name=name,
    )(
        *behind,
        *ins,
        *[pltpu.with_memory_space_constraint(item, pltpu.HBM) for item, _ in fetch],
    )
    near = [item for item, kind in zip(found, flat) if isinstance(kind, jax.ShapeDtypeStruct)]
    if near:
        LINE[:] = [min(near, key=lambda item: item.size)]
    else:
        LINE[:] = [pltpu.with_memory_space_constraint(found[0], pltpu.HBM)]
    if count:
        found, FETCHED[:] = found[: len(flat)], found[len(flat) :]
    return found if isinstance(outs, list) else found[0]


def dot_nn(left, right):
    return lax.dot_general(left, right, (((1,), (0,)), ((), ())), preferred_element_type=F32)


def dot_nt(left, right):
    return lax.dot_general(left, right, (((1,), (1,)), ((), ())), preferred_element_type=F32)


def dot_tn(left, right):
    return lax.dot_general(left, right, (((0,), (0,)), ((), ())), preferred_element_type=F32)


def dot_tt(left, right):
    return lax.dot_general(left, right, (((0,), (1,)), ((), ())), preferred_element_type=F32)


def dot_full(left, right, contracted):
    return lax.dot_general(
        left,
        right,
        (contracted, ((), ())),
        preferred_element_type=F32,
        precision=lax.Precision.HIGHEST,
    )


def place_matrix(layer):
    row = lax.broadcasted_iota(jnp.int32, (2 * SLOT, PATCHES), 0)
    patch = lax.broadcasted_iota(jnp.int32, (2 * SLOT, PATCHES), 1)
    second = row >= SLOT
    within = jnp.where(second, row - SLOT, row)
    found = within + jnp.where(second, BLOCK, 0) + layer * SHIFT * GRID
    found = jnp.where(found >= PATCHES, found - PATCHES, found)
    return jnp.where((within < BLOCK) & (found == patch), 1.0, 0.0).astype(BF16)


def window_matrix(layer, block):
    def groups(place):
        turned_row = (place * 147) >> 11
        col = place - turned_row * GRID
        row = turned_row + block * WIN + layer * SHIFT
        row = jnp.where(row >= GRID, row - GRID, row)

        def group(position):
            moved = position + layer * (WIN - SHIFT)
            return jnp.where(moved >= 2 * WIN, 2, jnp.where(moved >= WIN, 1, 0))

        return group(row) * 4 + group(col)

    key = lax.broadcasted_iota(jnp.int32, (KEYS, LANES), 0)
    query = lax.broadcasted_iota(jnp.int32, (KEYS, LANES), 1)
    return (groups(key) == groups(query)) & (key < BLOCK) & (query < BLOCK)


def offset_matrix():
    offset = lax.broadcasted_iota(jnp.int32, (SPAN * SPAN, TURN), 0)
    lane = lax.broadcasted_iota(jnp.int32, (SPAN * SPAN, TURN), 1)
    row = (offset * 79) >> 10
    place = offset - row * SPAN + row * GRID - (WIN - 1) * (GRID + 1)
    return jnp.where(jnp.where(place < 0, place + TURN, place) == lane, 1.0, 0.0)


def heads_apart(value):
    rows = value.shape[0]
    parts = []
    for member in range(rows // HEAD_DIM):
        start = member * HEAD_DIM
        pieces = [value[start : start + HEAD_DIM]]
        if start:
            pieces.insert(0, jnp.zeros((start, value.shape[1]), value.dtype))
        if start + HEAD_DIM < rows:
            pieces.append(jnp.zeros((rows - start - HEAD_DIM, value.shape[1]), value.dtype))
        parts.append(jnp.concatenate(pieces, axis=0))
    return jnp.concatenate(parts, axis=1)


def heads_together(value):
    count = value.shape[0] // HEAD_DIM
    columns = value.shape[1] // count
    return jnp.concatenate(
        [
            value[
                member * HEAD_DIM : (member + 1) * HEAD_DIM,
                member * columns : (member + 1) * columns,
            ]
            for member in range(count)
        ],
        axis=0,
    )


def norm_rows(stream, gain, shift):
    center = stream - jnp.mean(stream, axis=-1, keepdims=True)
    spread = jnp.mean(center * center, axis=-1, keepdims=True)
    rstd = lax.rsqrt(spread + EPSILON)
    x_hat = center * rstd
    return x_hat, rstd, (x_hat * gain + shift).astype(BF16)


def norm_back(grad_normed, x_hat, rstd, gain):
    scaled = grad_normed * gain
    term = jnp.mean(scaled, axis=-1, keepdims=True)
    along = jnp.mean(scaled * x_hat, axis=-1, keepdims=True)
    return rstd * (scaled - term - x_hat * along)


def column_sum(value):
    return jnp.sum(value, axis=0, keepdims=True)


def put_sums(out, prior, sums):
    for row, found in enumerate(sums):
        out[row : row + 1] = found if prior is None else found + prior[row : row + 1]
    out[len(sums) :] = jnp.zeros((out.shape[0] - len(sums), out.shape[1]), F32)


FIRST_GAIN, FIRST_SHIFT, ATTENTION_BIAS, SECOND_GAIN, SECOND_SHIFT, REDUCE_BIAS = range(6)


def vector_row(vectors, member, layer):
    row = member * (vectors.shape[0] // 6) + layer
    return vectors[row : row + 1]


def head_lanes(rows, member):
    lane = lax.broadcasted_iota(jnp.int32, (rows, LANES), 1)
    return (lane >= member * HEAD_DIM) & (lane < (member + 1) * HEAD_DIM)


def head_rows(value):
    rows = value.shape[0]
    return jnp.concatenate(
        [
            jnp.where(head_lanes(rows, member), value, jnp.zeros_like(value))
            for member in range(LANES // HEAD_DIM)
        ],
        axis=0,
    )


def tables_body(heads, layers, refs):
    half = refs[0]
    in_hbm, refs = refs[1:13], refs[13:]
    biases, refs = refs[:layers], refs[layers:]
    masks, refs = refs[: 2 * layers], refs[2 * layers :]
    keep_out, vectors_out = refs[:2]
    held = [refs[6], refs[7], *refs[2:6], *refs[8:14]]
    sems = refs[14]
    copies = []
    for index, (source, target) in enumerate(zip(in_hbm, held)):
        copies.append(pltpu.make_async_copy(source, target, sems.at[index]))
        copies[-1].start()
    table, keep = held[:2]
    same = lax.broadcasted_iota(jnp.int32, (KEYS, LANES), 0) == lax.broadcasted_iota(
        jnp.int32, (KEYS, LANES), 1
    )
    offsets = offset_matrix()
    per_group = LANES // HEAD_DIM
    for copy in copies:
        copy.wait()
    own_first = half[0] == 0
    rows = [keep[image : image + 1].astype(F32) for image in range(2)]
    pair = jnp.concatenate(
        [jnp.where(own_first, rows[0], rows[1]), jnp.where(own_first, rows[1], rows[0])], axis=0
    ).astype(BF16)
    for layer in range(layers):
        line = dot_full(table[:, layer], offsets, ((1,), (0,)))
        for head in range(heads):
            wide = jnp.broadcast_to(line[head : head + 1], (KEYS, TURN))
            lanes = head % per_group * LANES
            biases[layer][head // per_group, :, lanes : lanes + LANES] = pltpu.roll(
                wide, 0, 1, stride=1, stride_axis=0
            )[:, :LANES]
        place = place_matrix(layer)
        kept = dot_nt(place, pair)
        for block in range(2):
            window = window_matrix(layer, block)
            for image in range(2):
                column = kept[block * SLOT : block * SLOT + KEYS, image : image + 1]
                fine = window & ((column > 0.5) | same)
                masks[layer * 2 + image][block] = jnp.where(fine, 0.0, MASKED)
        if layer == 0:
            keep_out[...] = dot_tn(place, kept.astype(BF16))
    for index, item in enumerate(held[6:]):
        vectors_out[index * layers : (index + 1) * layers] = item[...]


def make_tables(half, position_table, keep_mask, moved, vectors, fetch, also):
    heads, layers, _ = position_table.shape
    groups = heads * HEAD_DIM // LANES
    width = vectors[0].shape[1]
    ins = (position_table, keep_mask, *moved, *vectors)
    outs = [shape((groups, KEYS, 4 * LANES), F32)] * layers + [shape((2, KEYS, LANES), F32)] * (
        2 * layers
    )
    outs += [
        shape((PATCHES, 2), F32),
        shape((len(vectors) * layers, width), F32),
        *[shape(item.shape, item.dtype) for item in moved],
    ]
    found = kernel_call(
        lambda *refs: tables_body(heads, layers, refs),
        outs,
        [IN_VMEM] * len(outs),
        (half, *ins),
        [IN_SMEM] + [IN_HBM] * len(ins),
        [pltpu.VMEM(item.shape, item.dtype) for item in (*ins[:2], *vectors)]
        + [pltpu.SemaphoreType.DMA((len(ins),))],
        "tables",
        1.6,
        also,
        None,
        fetch,
    )
    masks = [found[layers + 2 * layer : layers + 2 * layer + 2] for layer in range(layers)]
    return found[:layers], masks, found[3 * layers :]


def attention_body(layer, heads, chained, refs):
    if chained:
        base, mine, theirs = refs[:3]
        refs = refs[3:]
    else:
        base, refs = refs[0], refs[1:]
    vectors, pair_bias, bias, mask, in_held, out_held = refs[:6]
    refs = refs[6:]
    if chained:
        stream_out, refs = refs[0], refs[1:]
    hat_out, rstd_out, partial_out = refs[1], refs[2], refs[6]
    far_outs = (refs[0], refs[3], refs[4], refs[5])
    turned = refs[7]
    save = Saver(refs[8:12], far_outs, refs[12]) if layer in FAR_LAYERS else Near(far_outs)
    qkv_out, weights_out = save.held[1:3]
    width = heads * HEAD_DIM
    stream = base[...].astype(F32)
    if chained:
        stream = (
            stream
            + (mine[...].astype(F32) + theirs[...].astype(F32))
            + vector_row(vectors, REDUCE_BIAS, layer - 1)
        )
        stream_out[...] = stream
    x_hat, rstd, normed = norm_rows(
        stream, vector_row(vectors, FIRST_GAIN, layer), vector_row(vectors, FIRST_SHIFT, layer)
    )
    save.put(0, normed)
    hat_out[...] = x_hat.astype(BF16)
    rstd_out[...] = rstd
    place = place_matrix(layer)
    parts = []
    for member in range(3):
        mixed = dot_nn(normed, in_held[member])
        if member != 1:
            mixed = mixed + pair_bias[layer, member // 2 : member // 2 + 1]
        parts.append(mixed.astype(BF16))
        qkv_out[:, member * width : (member + 1) * width] = parts[-1]
    save.start(1)
    queries = dot_tt(parts[0], place).astype(BF16)
    keys = dot_nn(place, parts[1]).astype(BF16)
    values = dot_tt(parts[2], place).astype(BF16)
    scale = HEAD_DIM ** (-0.5)
    groups = width // LANES
    for group in range(groups):
        lanes = slice(group * LANES, (group + 1) * LANES)
        for block in range(2):
            slots = slice(block * SLOT, (block + 1) * SLOT)
            own_keys = slice(block * SLOT, block * SLOT + KEYS)
            scores = dot_nn(keys[own_keys, lanes], heads_apart(queries[lanes, slots])) * scale
            scores = scores + bias[group] + jnp.concatenate([mask[block]] * 4, axis=1)
            raised = jnp.exp(scores - jnp.max(scores, axis=0, keepdims=True))
            weights = raised * (1.0 / jnp.sum(raised, axis=0, keepdims=True))
            weights = weights.astype(BF16)
            weights_out[group * 2 + block] = weights
            found = heads_together(dot_nn(values[lanes, own_keys], weights))
            turned[lanes, slots] = found.astype(BF16)
    attended = dot_tt(place, turned[...]).astype(BF16)
    save.start(2)
    save.put(3, attended)
    partial_out[...] = dot_nn(attended, out_held[...]).astype(BF16)
    save.wait()


def attention_forward(layer, streams, vectors, pair_bias, bias, mask, matrix_in, matrix_out, also=(), fetch=(), micros=4):
    chained = len(streams) > 1
    rows, width = streams[0].shape
    head_width = matrix_out.shape[0]
    put = far if layer in FAR_LAYERS else shape
    spec = IN_HBM if layer in FAR_LAYERS else IN_VMEM
    heads = head_width // HEAD_DIM
    saved = [
        (rows, width),
        (rows, 3 * head_width),
        (2 * head_width // LANES, KEYS, 4 * LANES),
        (rows, head_width),
    ]
    outs = [
        put(saved[0], BF16),
        shape((rows, width), BF16),
        shape((rows, 1), F32),
        *[put(dims, BF16) for dims in saved[1:]],
        shape((rows, width), BF16),
    ]
    out_specs = [spec, IN_VMEM, IN_VMEM, spec, spec, spec, IN_VMEM]
    if chained:
        outs = [shape((rows, width), F32)] + outs
        out_specs = [IN_VMEM] + out_specs
    ins = (*streams, vectors, pair_bias, bias, mask, matrix_in, matrix_out)
    found = kernel_call(
        lambda *refs: attention_body(layer, heads, chained, refs),
        outs,
        out_specs,
        ins,
        [IN_VMEM] * len(ins),
        [pltpu.VMEM((head_width, 2 * SLOT), BF16)]
        + (
            [*[pltpu.VMEM(dims, BF16) for dims in saved], pltpu.SemaphoreType.DMA((4,))]
            if layer in FAR_LAYERS
            else []
        ),
        f"attention_{layer}",
        micros,
        also,
        None,
        fetch,
    )
    return found if chained else [streams[0], *found]


def gelu_parts(hidden):
    below = 0.5 * (1.0 + lax.erf(hidden * (0.5**0.5)))
    density = jnp.exp(-0.5 * hidden * hidden) * (0.5 / np.pi) ** 0.5
    return hidden * below, below + hidden * density


def ffn_body(layer, both, image, joined, step, refs):
    base, mine, theirs, vectors, up_bias = refs[:5]
    refs = refs[5:]
    if both:
        grad, keep, refs = refs[0], refs[1], refs[2:]
    if joined:
        prior_sums, refs = refs[0], refs[1:]
    up_held, down_held, *refs = refs
    mid_out, hat_out, rstd_out, partial_out = refs[0], refs[2], refs[3], refs[6]
    far_outs = (refs[1], refs[4], refs[5])
    if both:
        back_out, sums_out, grad_out = refs[7:10]
    held = refs[7:]
    save = Saver(held[:3], far_outs, held[3]) if layer in FAR_LAYERS else Near(far_outs)
    active_out, slope_out = save.held[1:]
    mid = (
        base[...].astype(F32)
        + (mine[...].astype(F32) + theirs[...].astype(F32))
        + vector_row(vectors, ATTENTION_BIAS, layer)
    )
    mid_out[...] = mid
    x_hat, rstd, normed = norm_rows(
        mid, vector_row(vectors, SECOND_GAIN, layer), vector_row(vectors, SECOND_SHIFT, layer)
    )
    save.put(0, normed)
    hat_out[...] = x_hat.astype(BF16)
    rstd_out[...] = rstd
    if both:
        grad_rows = (grad[...].astype(F32) * keep[:, image : image + 1]).astype(BF16)
        grad_out[...] = grad_rows
        put_sums(sums_out, prior_sums if joined else None, [column_sum(grad_rows.astype(F32))])
    forward, backward = None, None
    for start in range(0, up_held.shape[1], step):
        part = slice(start, start + step)
        hidden = dot_nn(normed, up_held[:, part]) + up_bias[layer : layer + 1, part]
        active, slope = gelu_parts(hidden)
        active = active.astype(BF16)
        active_out[:, part] = active
        term = dot_nn(active, down_held[part])
        forward = term if forward is None else forward + term
        if both:
            grad_hidden = (slope * dot_nt(grad_rows, down_held[part])).astype(BF16)
            slope_out[:, part] = grad_hidden
            term = dot_nt(grad_hidden, up_held[:, part])
            backward = term if backward is None else backward + term
        else:
            slope_out[:, part] = slope.astype(BF16)
    save.start(1)
    save.start(2)
    partial_out[...] = forward.astype(BF16)
    if both:
        back_out[...] = backward.astype(BF16)
    save.wait()


def ffn_forward(layer, image, streams, vectors, up_bias, up, down, grad=None, keep=None, prior_sums=None, fetch=(), also=()):
    rows, width = streams[0].shape
    units = up.shape[1]
    both = grad is not None
    put = far if layer in FAR_LAYERS else shape
    saved = [(rows, width), (rows, units), (rows, units)]
    outs = [
        shape((rows, width), F32),
        put(saved[0], BF16),
        shape((rows, width), BF16),
        shape((rows, 1), F32),
        put(saved[1], BF16),
        put(saved[2], BF16),
        shape((rows, width), BF16),
    ]
    ins = [*streams, vectors, up_bias]
    if both:
        outs += [shape((rows, width), BF16), shape((8, width), F32), shape((rows, width), BF16)]
        ins += [grad, keep]
    joined = prior_sums is not None
    if joined:
        ins.append(prior_sums)
    specs = [IN_VMEM] * (len(ins) + 2)
    return kernel_call(
        lambda *refs: ffn_body(layer, both, image, joined, units // 3, refs),
        outs,
        [IN_VMEM if put is shape or index not in (1, 4, 5) else IN_HBM for index in range(len(outs))],
        (*ins, up, down),
        specs,
        []
        if put is shape
        else [*[pltpu.VMEM(dims, BF16) for dims in saved], pltpu.SemaphoreType.DMA((3,))],
        f"ffn_both_{layer}" if both else f"ffn_{layer}",
        4.6 if both else 3,
        also,
        None,
        fetch,
    )


def ffn_back_body(layer, joined, step, refs):
    base, mine, theirs, hat, rstd, vectors = refs[:6]
    refs = refs[6:]
    if joined:
        prior_sums, refs = refs[0], refs[1:]
    slope_hbm, up_held, down_held = refs[:3]
    grad_out, low_out, hidden_out, partial_out, sums_out = refs[3:8]
    slope, load = slope_hbm, Near([slope_hbm])
    if layer in FAR_LAYERS:
        slope = refs[8]
        load = Loader([slope_hbm], [slope], refs[9])
    grad_normed = mine[...].astype(F32) + theirs[...].astype(F32)
    x_hat = hat[...].astype(F32)
    grad = base[...] + norm_back(
        grad_normed, x_hat, rstd[...], vector_row(vectors, FIRST_GAIN, layer + 1)
    )
    grad_out[...] = grad
    low = grad.astype(BF16)
    low_out[...] = low
    sums = [column_sum(grad_normed * x_hat), column_sum(grad_normed), column_sum(grad)]
    put_sums(sums_out, prior_sums if joined else None, sums)
    backward = None
    load.get(0)
    for start in range(0, up_held.shape[1], step):
        part = slice(start, start + step)
        grad_hidden = (slope[:, part].astype(F32) * dot_nt(low, down_held[part])).astype(BF16)
        hidden_out[:, part] = grad_hidden
        term = dot_nt(grad_hidden, up_held[:, part])
        backward = term if backward is None else backward + term
    partial_out[...] = backward.astype(BF16)


def ffn_backward(layer, grads, hat, rstd, vectors, slope, up, down, prior_sums=None, micros=4, fetch=()):
    rows, width = grads[0].shape
    units = up.shape[1]
    outs = [
        shape((rows, width), F32),
        shape((rows, width), BF16),
        shape((rows, units), BF16),
        shape((rows, width), BF16),
        shape((8, width), F32),
    ]
    ins = [*grads, hat, rstd, vectors]
    joined = prior_sums is not None
    if joined:
        ins.append(prior_sums)
    return kernel_call(
        lambda *refs: ffn_back_body(layer, joined, units // 3, refs),
        outs,
        [IN_VMEM] * 5,
        (*ins, slope, up, down),
        [IN_VMEM] * len(ins) + [IN_HBM if layer in FAR_LAYERS else IN_VMEM] + [IN_VMEM] * 2,
        [pltpu.VMEM((rows, units), BF16), pltpu.SemaphoreType.DMA((1,))]
        if layer in FAR_LAYERS
        else [],
        f"ffn_back_{layer}",
        micros,
        (),
        None,
        fetch,
    )


def attention_back_body(layer, heads, joined, refs):
    base, mine, theirs, hat, rstd, vectors, first_hat = refs[:7]
    refs = refs[7:]
    if joined:
        prior_sums, prior_table = refs[:2]
        refs = refs[2:]
    qkv, weights, in_held, out_held = refs[:4]
    grad_out, low_out, mixed_out, partial_out, sums_out, table_out = refs[4:10]
    turned, merged, diagonals = refs[10:13]
    load = Near([qkv, weights])
    if layer in FAR_LAYERS:
        load = Loader([qkv, weights], refs[13:15], refs[15])
        qkv, weights = refs[13:15]
    width = heads * HEAD_DIM
    per_group = LANES // HEAD_DIM
    grad_normed = mine[...].astype(F32) + theirs[...].astype(F32)
    x_hat = hat[...].astype(F32)
    grad = base[...].astype(F32) + norm_back(
        grad_normed, x_hat, rstd[...], vector_row(vectors, SECOND_GAIN, layer)
    )
    grad_out[...] = grad
    low = grad.astype(BF16)
    low_out[...] = low
    sums = [column_sum(grad_normed * x_hat), column_sum(grad_normed), column_sum(grad)]
    place = place_matrix(layer)
    load.get(0)
    queries = dot_nn(place, qkv[:, :width]).astype(BF16)
    turned_keys = dot_tt(qkv[:, width : 2 * width], place).astype(BF16)
    values = dot_nn(place, qkv[:, 2 * width :]).astype(BF16)
    grad_attended = dot_nt(low, out_held[...]).astype(BF16)
    grad_slots = dot_nn(place, grad_attended).astype(BF16)
    grad_turned = dot_tt(grad_attended, place).astype(BF16)
    load.get(1)
    scale = HEAD_DIM ** (-0.5)
    empty = jnp.zeros((SLOT - KEYS, LANES), BF16)
    for group in range(width // LANES):
        lanes = slice(group * LANES, (group + 1) * LANES)
        total = None
        for block in range(2):
            top_row = block * SLOT
            slots = slice(top_row, top_row + SLOT)
            own_keys = slice(top_row, top_row + KEYS)
            low_weights = weights[group * 2 + block]
            full = low_weights.astype(F32)
            grad_weights = dot_nn(values[own_keys, lanes], heads_apart(grad_turned[lanes, slots]))
            spread = jnp.sum(full * grad_weights, axis=0, keepdims=True)
            grad_scores = full * (grad_weights - spread)
            total = grad_scores if total is None else total + grad_scores
            grad_raw = (grad_scores * scale).astype(BF16)
            grad_query = heads_together(dot_nn(turned_keys[lanes, own_keys], grad_raw))
            grad_key = dot_nn(grad_raw, head_rows(queries[slots, lanes]))
            grad_value = dot_nn(low_weights, head_rows(grad_slots[slots, lanes]))
            turned[lanes, slots] = grad_query.astype(BF16)
            for at, found in ((0, grad_key), (width, grad_value)):
                columns = slice(at + group * LANES, at + (group + 1) * LANES)
                merged[own_keys, columns] = found.astype(BF16)
                merged[top_row + KEYS : top_row + SLOT, columns] = empty
        for member in range(per_group):
            head = group * per_group + member
            own = total[:, member * LANES : (member + 1) * LANES]
            wide = jnp.concatenate([own, jnp.zeros_like(own)], axis=1)
            line = None
            for start in range(0, KEYS, 8):
                rows = wide[start : start + 8]
                if start:
                    rows = pltpu.roll(rows, TURN - start, 1)
                line = rows if line is None else line + rows
            diagonals[head * 8 : head * 8 + 8] = line
    mixed = [dot_tt(place, turned[...]).astype(BF16)]
    both = dot_tn(place, merged[...]).astype(BF16)
    mixed += [both[:, :width], both[:, width:]]
    mixed_out[:, :width] = mixed[0]
    mixed_out[:, width:] = both
    partial = dot_nt(mixed[0], in_held[0])
    partial = partial + dot_nt(mixed[1], in_held[1])
    partial = partial + dot_nt(mixed[2], in_held[2])
    partial_out[...] = partial.astype(BF16)
    sums += [column_sum(partial * first_hat[...].astype(F32)), column_sum(partial)]
    put_sums(sums_out, prior_sums if joined else None, sums)
    lines = diagonals[...]
    row = lax.broadcasted_iota(jnp.int32, lines.shape, 0)
    for bit in range(3):
        moved = pltpu.roll(lines, TURN - (1 << bit), 1)
        lines = jnp.where(((row >> bit) & 1) == 1, moved, lines)
    lines = jnp.sum(lines.reshape(heads, 8, TURN), axis=1)
    table = dot_full(lines, offset_matrix(), ((1,), (1,)))
    table_out[...] = table + prior_table[...] if joined else table


def attention_backward(
    layer, grads, hat, rstd, vectors, first_hat, qkv, weights, matrix_in, matrix_out,
    prior=(), micros=5, fetch=(),
):
    rows, width = grads[0].shape
    head_width = matrix_out.shape[0]
    heads = head_width // HEAD_DIM
    outs = [
        shape((rows, width), F32),
        shape((rows, width), BF16),
        shape((rows, 3 * head_width), BF16),
        shape((rows, width), BF16),
        shape((8, width), F32),
        shape((heads, SPAN * SPAN), F32),
    ]
    ins = (*grads, hat, rstd, vectors, first_hat, *prior)
    return kernel_call(
        lambda *refs: attention_back_body(layer, heads, bool(prior), refs),
        outs,
        [IN_VMEM] * 6,
        (*ins, qkv, weights, matrix_in, matrix_out),
        [IN_VMEM] * len(ins) + [IN_HBM if layer in FAR_LAYERS else IN_VMEM] * 2 + [IN_VMEM] * 2,
        [
            pltpu.VMEM((head_width, 2 * SLOT), BF16),
            pltpu.VMEM((2 * SLOT, 2 * head_width), BF16),
            pltpu.VMEM((heads * 8, TURN), F32),
        ]
        + (
            [
                pltpu.VMEM(qkv.shape, BF16),
                pltpu.VMEM(weights.shape, BF16),
                pltpu.SemaphoreType.DMA((2,)),
            ]
            if layer in FAR_LAYERS
            else []
        ),
        f"attention_back_{layer}",
        micros,
        (),
        None,
        fetch,
    )


def finish_body(base, mine, theirs, hat, rstd, vectors, out):
    grad_normed = mine[...].astype(F32) + theirs[...].astype(F32)
    out[...] = base[...] + norm_back(
        grad_normed, hat[...].astype(F32), rstd[...], vector_row(vectors, FIRST_GAIN, 0)
    )


def output_body(layer, base, mine, theirs, vectors, out):
    total = base[...] + (mine[...].astype(F32) + theirs[...].astype(F32))
    out[...] = (total + vector_row(vectors, REDUCE_BIAS, layer)).astype(BF16)


def finish(body, kind, name, micros, *ins):
    return kernel_call(
        body, pltpu.HBM(ins[0].shape, kind), IN_VMEM, ins, [IN_VMEM] * len(ins), [], name, micros
    )


def group_place(group, top, order):
    place = 0
    for step, bit in enumerate(order):
        place = place + ((((group >> bit) & 1) ^ ((top >> bit) & 1)) << (len(order) - 1 - step))
    return place


def grads_body(pairs, groups, order, step, summed, far_ins, refs):
    top = refs[0][0]
    lefts = 1 + max(left for left, _ in pairs)
    rights = len(pairs)
    refs = refs[1:]
    total = 2 * (lefts + rights)
    sources, refs = refs[:total], refs[total:]
    held_ins = list(sources)
    far_count = sum(far_ins)
    if far_count:
        scratch, sems, refs = refs[-far_count - 1 : -1], refs[-1], refs[: -far_count - 1]
        loader = Loader([item for item, is_far in zip(sources, far_ins) if is_far], scratch, sems)
        places = [index for index, is_far in enumerate(far_ins) if is_far]

    def get(index):
        return loader.get(places.index(index)) if far_ins[index] else held_ins[index]

    keep_out, sums_out, held, turned, wide, sems = (refs[0], *refs[-5:])
    send_outs = refs[1:-5]
    rows = sources[0].shape[0]
    space = wide.shape[0] // 2
    empty = space - rows
    block = keep_out.shape[1]
    copies = []
    for left in range(lefts):
        for image in range(2):
            start = image * space
            turned[left, :, start + LANES : start + space] = jnp.zeros(
                (turned.shape[1], space - LANES), BF16
            )
            turned[left, :, start : start + rows] = get(2 * left + image)[...].T
    at = 0
    sum_at = 0
    for right, (left, _) in enumerate(pairs):
        columns = sources[2 * (lefts + right)].shape[1]
        for image in range(2):
            start = image * space
            wide[start : start + rows, :columns] = get(2 * (lefts + right) + image)[...]
            wide[start + rows : start + space, :columns] = jnp.zeros((empty, columns), BF16)
        if summed[right]:
            sums_out[0:1, sum_at : sum_at + columns] = column_sum(wide[:, :columns].astype(F32))
            sum_at += columns
        for first in range(0, columns, step):
            found = dot_nn(turned[left], wide[:, first : first + step]).astype(BF16)
            for group in range(groups):
                held[group_place(group, top, order), :, at : at + step] = found[
                    group * block : (group + 1) * block
                ]
            sent = at // send_outs[0].shape[2]
            inner = at - sent * send_outs[0].shape[2]
            for half, out in (
                (0, keep_out.at[:, :, at : at + step]),
                (1, send_outs[sent].at[:, :, inner : inner + step]),
            ):
                copy = pltpu.make_async_copy(
                    held.at[half * groups // 2 : (half + 1) * groups // 2, :, at : at + step],
                    out,
                    sems.at[half, at // step],
                )
                copy.start()
                copies.append(copy)
            at += step
    for copy in copies:
        copy.wait()


def weight_grads(top, groups, order, pairs, lefts, rights, summed, pieces, far_ins, name, micros):
    width = lefts[0].shape[1]
    step = 512 if all(item.shape[1] % 512 == 0 for item in rights) else 384
    columns = sum(item.shape[1] for item in rights[::2])
    widest = max(item.shape[1] for item in rights)
    space = 2 * LANES
    summed_columns = sum(item.shape[1] for item, used in zip(rights[::2], summed) if used)
    outs = [
        shape((groups // 2, width // groups, columns), BF16),
        *[shape((groups // 2, width // groups, columns // pieces), BF16)] * pieces,
        shape((8, summed_columns), F32),
    ]
    count = 1 + max(left for left, _ in pairs)
    kept, *sent, sums = kernel_call(
        lambda *refs: grads_body(pairs, groups, order, step, summed, far_ins, refs),
        outs,
        [ANYWHERE] * (1 + pieces) + [IN_VMEM],
        (top, *lefts, *rights),
        [IN_SMEM] + [IN_HBM if is_far else IN_VMEM for is_far in far_ins],
        [
            pltpu.VMEM((groups, width // groups, columns), BF16),
            pltpu.VMEM((count, width, 2 * space), BF16),
            pltpu.VMEM((2 * space, widest), BF16),
            pltpu.SemaphoreType.DMA((2, columns // step)),
            *[
                pltpu.VMEM(item.shape, item.dtype)
                for item, is_far in zip((*lefts, *rights), far_ins)
                if is_far
            ],
            *([pltpu.SemaphoreType.DMA((sum(far_ins),))] if any(far_ins) else []),
        ],
        name,
        micros,
        (),
        20 * 1024 * 1024,
    )
    return kept, sent, sums


def swap(value):
    return lax.ppermute(value, "mp", [(0, 1), (1, 0)])


def trade(value, bit, size):
    return lax.ppermute(value, "dp", [(source, source ^ bit) for source in range(size)])


def fold_body(kept, *refs):
    *pieces, keep_out, send_out = refs
    half = keep_out.shape[0]
    at = 0
    for found in pieces:
        columns = slice(at, at + found.shape[2])
        at += found.shape[2]
        for start, out in ((0, keep_out), (half, send_out)):
            for block in range(half):
                total = kept[start + block, :, columns].astype(F32) + found[start + block].astype(F32)
                out[block, :, columns] = total.astype(BF16)


def fold(kept, found, name):
    half = shape((kept.shape[0] // 2, *kept.shape[1:]), BF16)
    return kernel_call(
        fold_body, [half, half], [IN_VMEM] * 2, (kept, *found), [IN_VMEM] * (1 + len(found)), [],
        name, 0.1,
    )


class Scatter:
    def __init__(self, kept, sent, order, size, name):
        self.kept, self.sent, self.order, self.size, self.name = kept, sent, order, size, name
        self.finer = size >> len(order)
        self.level = 0
        self.send()

    def send(self):
        self.found = [
            trade(item, self.finer << self.order[self.level], self.size) for item in self.sent
        ]

    def step(self):
        if self.level + 1 < len(self.order):
            self.kept, sent = fold(self.kept, self.found, f"{self.name}_{self.level}")
            self.sent = [sent]
            self.level += 1
            self.send()

    def finish(self):
        for _ in self.order:
            self.step()
        kept, finer = self.kept, self.finer
        found = jnp.concatenate(self.found, axis=2) if len(self.found) > 1 else self.found[0]
        rank = lax.axis_index("dp")
        while finer > 1:
            finer //= 2
            held = (kept.astype(F32) + found.astype(F32)).astype(BF16)
            halves = held.reshape((2, 1, held.shape[1] // 2, held.shape[2]))
            mine = (rank // finer) % 2
            kept = lax.dynamic_index_in_dim(halves, mine, 0, keepdims=False)
            found = trade(lax.dynamic_index_in_dim(halves, 1 - mine, 0, keepdims=False), finer, self.size)
        return kept, found

    def join(self):
        kept, found = self.finish()
        return (
            kernel_call(
                add_body, shape(kept.shape, F32), IN_VMEM, (kept, found), [IN_VMEM] * 2, [],
                f"{self.name}_end", 0.1,
            ),
        )


def add_body(left, right, out):
    out[...] = left[...].astype(F32) + right[...].astype(F32)


def some_bits(name, size):
    bits = range(size.bit_length() - 1)
    listed = [bit for bit in BIT_ORDER[name] if bit in bits]
    return tuple(listed + [bit for bit in bits if bit not in listed])


class Total:
    def __init__(self, value, size):
        self.value, self.size = value, size
        self.left = [1 << bit for bit in some_bits("total", size)]
        self.send()

    def send(self):
        self.found = trade(self.value, self.left.pop(0), self.size)

    def step(self):
        if self.left:
            self.value = kernel_call(
                add_body, shape(self.value.shape, F32), IN_VMEM, (self.value, self.found),
                [IN_VMEM] * 2, [], "total", 0.1,
            )
            self.send()

    def finish(self):
        while self.left:
            self.step()
        return self.value, self.found


def collect_body(counts, widths, refs):
    outs = refs[sum(counts) :]
    for layer, count in enumerate(counts):
        total = refs[0][0].astype(F32)
        if count == 2:
            total = total + refs[1][0].astype(F32)
        refs = refs[count:]
        at = 0
        for out, parts in zip(outs, widths):
            for part in range(parts):
                columns = out.shape[-1]
                if len(out.shape) == 4:
                    out[layer, part] = total[:, at : at + columns]
                else:
                    out[layer] = total[:, at : at + columns]
                at += columns


def collect(pairs, shapes, name):
    flat = [item for pair in pairs for item in pair]
    counts = [len(pair) for pair in pairs]
    return kernel_call(
        lambda *refs: collect_body(
            counts, [dims[1] if len(dims) == 4 else 1 for dims in shapes], refs
        ),
        [pltpu.HBM(dims, F32) for dims in shapes],
        [IN_VMEM] * len(shapes),
        flat,
        [IN_VMEM] * len(flat),
        [],
        name,
        0.1,
    )


def pack_body(width, layers, refs):
    sums_0, theirs_0, sums_low, sums_1, last = refs[:5]
    ups, mixes, tables = refs[5 : 5 + layers], refs[5 + layers : 5 + 2 * layers], refs[5 + 2 * layers : -1]
    out = refs[-1]
    out[...] = jnp.zeros(out.shape, F32)
    out[0:2] = sums_0[3:5] + theirs_0[3:5]
    out[2:3] = sums_0[2:3]
    out[3:5] = sums_0[0:2]
    out[5:6] = sums_low[2:3]
    out[6:8] = sums_low[0:2]
    out[8:9] = sums_1[2:3]
    out[9:11] = sums_1[0:2]
    out[11:12] = last[0:1]
    row = 6 * layers
    for item in ups:
        for start in range(0, item.shape[1], width):
            out[row : row + 1] = item[0:1, start : start + width]
            row += 1
    third = mixes[0].shape[1] // 3
    for item in mixes:
        out[row : row + 1, :third] = item[0:1, :third]
        out[row : row + 1, third : 2 * third] = item[0:1, 2 * third :]
        row += 1
    for item in tables:
        heads, offsets = item.shape
        for head in range(heads):
            lane = head * TURN % width
            out[row : row + 1, lane : lane + offsets] = item[head : head + 1]
            if (head + 1) * TURN % width == 0:
                row += 1


def unpack_body(refs):
    packed, found, vectors, up_bias, pair_bias, tables = refs
    width = packed.shape[1]
    layers, units = up_bias.shape
    total = packed[...] + found[...]
    for layer in range(layers):
        for member in range(6):
            vectors[member, layer : layer + 1] = total[6 * layer + member : 6 * layer + member + 1]
    row = 6 * layers
    for layer in range(layers):
        for start in range(0, units, width):
            up_bias[layer : layer + 1, start : start + width] = total[row : row + 1]
            row += 1
    third = pair_bias.shape[2]
    for layer in range(layers):
        for member in range(2):
            pair_bias[layer, member : member + 1] = total[
                row : row + 1, member * third : (member + 1) * third
            ]
        row += 1
    heads, _, offsets = tables.shape
    for layer in range(layers):
        for head in range(heads):
            lane = head * TURN % width
            tables[head, layer : layer + 1] = total[row : row + 1, lane : lane + offsets]
            if (head + 1) * TURN % width == 0:
                row += 1


def shards(
    tokens,
    keep_mask,
    cotangent,
    first_gain,
    first_shift,
    attention_in,
    query_value_bias,
    position_table,
    attention_out,
    attention_bias,
    second_gain,
    second_shift,
    expand_weight,
    expand_bias,
    reduce_weight,
    reduce_bias,
):
    LINE.clear()
    FETCHED.clear()
    size = lax.axis_size("dp")
    half = lax.axis_index("mp")
    groups = min(16, size)
    top = (lax.axis_index("dp") // (size // groups)).astype(jnp.int32).reshape(1)
    layers, width = first_gain.shape
    head_width = attention_out.shape[1]
    units = expand_weight.shape[2]
    heads = head_width // HEAD_DIM
    matrix_in = jnp.transpose(attention_in, (0, 2, 1, 3))
    own_half = half.astype(jnp.int32).reshape(1)
    other_tokens = swap(tokens)
    other_cotangent = swap(cotangent)
    bias, masks, (keep_columns, vectors, tokens, cotangent, up_bias, pair_bias) = make_tables(
        own_half, jnp.transpose(position_table, (1, 0, 2)), keep_mask,
        (tokens, cotangent, expand_bias, query_value_bias),
        (first_gain, first_shift, attention_bias, second_gain, second_shift, reduce_bias),
        ((matrix_in, 0), (attention_out, 0)), (top,),
    )
    heads_held = list(FETCHED)
    def attend(layer, image, streams, also=(), fetch=(), micros=4):
        return attention_forward(
            layer, streams, vectors, pair_bias, bias[layer], masks[layer][image], *heads_held,
            also, fetch, micros,
        )

    def feed(layer, image, streams, grad=None, prior_sums=None, fetch=(), also=()):
        return ffn_forward(
            layer, image, streams, vectors, up_bias, *units_held, grad, keep_columns, prior_sums,
            fetch, also,
        )

    att, ffn = [[None, None], [None, None]], [[None, None], [None, None]]
    att[0][0] = attend(0, 0, (tokens,), micros=0.3)
    sent_own = swap(att[0][0][7])
    att[0][1] = attend(
        0, 1, (other_tokens,), (), ((expand_weight, 0), (reduce_weight, 0))
    )
    units_held = list(FETCHED)
    sent_other = swap(att[0][1][7])
    ffn[0][1] = feed(
        0, 1, (att[0][1][0], att[0][1][7], sent_own), also=(other_cotangent,),
        fetch=((matrix_in, 1), (attention_out, 1)),
    )
    heads_held = list(FETCHED)
    sent_2 = swap(ffn[0][1][6])
    ffn[0][0] = feed(0, 0, (att[0][0][0], att[0][0][7], sent_other))
    sent_1 = swap(ffn[0][0][6])
    att[1][0] = attend(1, 0, (ffn[0][0][0], ffn[0][0][6], sent_2))
    sent_own = swap(att[1][0][7])
    att[1][1] = attend(
        1, 1, (ffn[0][1][0], ffn[0][1][6], sent_1), (), ((expand_weight, 1), (reduce_weight, 1))
    )
    units_held = list(FETCHED)
    sent_other = swap(att[1][1][7])

    far_ins = (True, True, False, False, False, False, True, True)

    def ffn_grads(layer, low, hidden, name):
        normed = [ffn[layer][image][1] for image in range(2)]
        active = [ffn[layer][image][4] for image in range(2)]
        order = some_bits(f"ffn_{layer}", groups)
        kept, sent, sums = weight_grads(
            top, groups, order, ((0, 0), (1, 1)), (*normed, *low), (*hidden, *active),
            (True, False), PIECES["ffn"], far_ins if layer in FAR_LAYERS else (False,) * 8, name, MICROS[name],
        )
        return Scatter(kept, sent, order, size, f"ffn_fold_{layer}"), sums

    def attention_grads(layer, low, mixed, name):
        normed = [att[layer][image][1] for image in range(2)]
        attended = [att[layer][image][6] for image in range(2)]
        order = some_bits(f"attention_{layer}", groups)
        kept, sent, sums = weight_grads(
            top, groups, order, ((0, 0), (1, 1)), (*normed, *low), (*mixed, *attended),
            (True, False), PIECES["attention"], far_ins if layer in FAR_LAYERS else (False,) * 8, name, MICROS[name],
        )
        return Scatter(kept, sent, order, size, f"attention_fold_{layer}"), sums

    def attend_back(layer, image, grads, prior=(), micros=5, fetch=()):
        held = att[layer][image]
        return attention_backward(
            layer, grads, ffn[layer][image][2], ffn[layer][image][3], vectors, held[2],
            held[4], held[5], *later["heads"], prior, micros, fetch,
        )

    def feed_back(image, grads, prior_sums=None, micros=4, fetch=()):
        held = att[1][image]
        return ffn_backward(
            0, grads, held[2], held[3], vectors, ffn[0][image][5], *later["units"],
            prior_sums, micros, fetch,
        )

    back, low = [[None, None], [None, None]], [None, None]
    later = {"heads": heads_held, "units": None}
    sent, sums, extra, outs = {}, {}, {}, {}
    rows = width // size

    def ffn_1_other():
        ffn[1][1] = feed(1, 1, (att[1][1][0], att[1][1][7], sent_own), other_cotangent)
        sent["ffn_1_other"] = swap(ffn[1][1][7])
        sent["block"] = swap(ffn[1][1][6])

    def ffn_1_own():
        ffn[1][0] = feed(1, 0, (att[1][0][0], att[1][0][7], sent_other), cotangent, ffn[1][1][8])
        sent["ffn_1_own"] = swap(ffn[1][0][7])

    def ffn_grads_1():
        sums["ffn_sum_1"], extra["up_1"] = ffn_grads(
            1, (ffn[1][0][9], ffn[1][1][9]), (ffn[1][0][5], ffn[1][1][5]), "ffn_grads_1"
        )

    def attention_back_1_own():
        back[1][0] = attend_back(
            1, 0, (ffn[1][0][9], ffn[1][0][7], sent["ffn_1_other"]), (),
            MICROS["attention_back_1_own"], ((expand_weight, 0), (reduce_weight, 0)),
        )
        later["units"] = list(FETCHED)
        sent["back_1_own"] = swap(back[1][0][3])

    def attention_back_1_other():
        back[1][1] = attend_back(
            1, 1, (ffn[1][1][9], ffn[1][1][7], sent["ffn_1_own"]), back[1][0][4:6],
            MICROS["attention_back_1_other"],
        )
        sent["back_1_other"] = swap(back[1][1][3])

    def attention_grads_1():
        sums["attention_sum_1"], extra["mixed_1"] = attention_grads(
            1, (back[1][0][1], back[1][1][1]), (back[1][0][2], back[1][1][2]), "attention_grads_1"
        )

    def ffn_back_0_other():
        low[1] = feed_back(
            1, (back[1][1][0], back[1][1][3], sent["back_1_own"]), None,
            MICROS["ffn_back_0_other"], ((matrix_in, 0), (attention_out, 0)),
        )
        later["heads"] = list(FETCHED)
        sent["low_other"] = swap(low[1][3])

    def ffn_back_0_own():
        low[0] = feed_back(
            0, (back[1][0][0], back[1][0][3], sent["back_1_other"]), low[1][4],
            MICROS["ffn_back_0_own"],
        )
        sent["low_own"] = swap(low[0][3])

    def ffn_grads_0():
        sums["ffn_sum_0"], extra["up_0"] = ffn_grads(
            0, (low[0][1], low[1][1]), (low[0][2], low[1][2]), "ffn_grads_0"
        )

    def attention_back_0_own():
        back[0][0] = attend_back(
            0, 0, (low[0][0], low[0][3], sent["low_other"]), (), MICROS["attention_back_0_own"]
        )

    def attention_back_0_other():
        back[0][1] = attend_back(
            0, 1, (low[1][0], low[1][3], sent["low_own"]), back[0][0][4:6],
            MICROS["attention_back_0_other"],
        )
        sent["last"] = swap(back[0][1][3])
        sent["sums"] = swap(back[0][1][4])

    def attention_grads_0():
        sums["attention_sum_0"], extra["mixed_0"] = attention_grads(
            0, (back[0][0][1], back[0][1][1]), (back[0][0][2], back[0][1][2]), "attention_grads_0"
        )

    def pack():
        pieces = (
            back[0][1][4], sent["sums"], low[0][4], back[1][1][4], ffn[1][0][8],
            extra["up_0"], extra["up_1"], extra["mixed_0"], extra["mixed_1"],
            back[0][1][5], back[1][1][5],
        )
        per_row = width // TURN
        count = layers * (6 + units // width + 1 + heads // per_row)
        packed = kernel_call(
            lambda *refs: pack_body(width, layers, refs),
            shape((-(-count // 8) * 8, width), F32),
            IN_VMEM,
            pieces,
            [IN_VMEM] * len(pieces),
            [],
            "pack",
            MICROS["pack"],
        )
        sums["total"] = Total(packed, size)

    def unpack():
        outs["small"] = kernel_call(
            lambda *refs: unpack_body(refs),
            [
                shape((6, layers, width), F32),
                shape((layers, units), F32),
                shape((layers, 2, head_width), F32),
                shape((heads, layers, SPAN * SPAN), F32),
            ],
            [IN_VMEM] * 4,
            sums["total"].finish(),
            [IN_VMEM] * 2,
            [],
            "unpack",
            0.1,
        )

    def tokens_grad():
        outs["tokens_grad"] = finish(
            finish_body, F32, "finish", 0.1,
            back[0][0][0], back[0][0][3], sent["last"], att[0][0][2], att[0][0][3], vectors,
        )

    def block_output():
        outs["block_output"] = finish(
            lambda *refs: output_body(1, *refs), BF16, "output", 0.1,
            ffn[1][0][0], ffn[1][0][6], sent["block"], vectors,
        )

    def attention_end_1():
        extra["attention_1"] = sums["attention_sum_1"].join()

    def ffn_end_1():
        extra["ffn_1"] = sums["ffn_sum_1"].join()

    def attention_outputs():
        outs["attention"] = collect(
            (sums["attention_sum_0"].finish(), extra["attention_1"]),
            [(layers, 3, rows, head_width), (layers, rows, head_width)],
            "attention_collect",
        )

    def ffn_outputs():
        outs["ffn"] = collect(
            (sums["ffn_sum_0"].finish(), extra["ffn_1"]), [(layers, rows, units)] * 2, "ffn_collect"
        )

    steps = {
        item.__name__: item
        for item in (
            ffn_1_other, ffn_1_own, ffn_grads_1, attention_back_1_own, attention_back_1_other,
            attention_grads_1, ffn_back_0_other, ffn_back_0_own, ffn_grads_0,
            attention_back_0_own, attention_back_0_other, attention_grads_0, pack, unpack,
            tokens_grad, block_output, attention_end_1, ffn_end_1, attention_outputs, ffn_outputs,
        )
    }
    for name in PLAN:
        if name in steps:
            steps[name]()
        else:
            sums[name].step()

    in_grad, out_grad = outs["attention"]
    up_grad, down_grad = outs["ffn"]
    vector_grads, expand_bias_grad, pair_grad, table_grad = outs["small"]
    return (
        outs["block_output"],
        outs["tokens_grad"],
        jnp.transpose(in_grad, (0, 2, 1, 3)),
        jnp.transpose(out_grad, (0, 2, 1)),
        up_grad,
        jnp.transpose(down_grad, (0, 2, 1)),
        pair_grad,
        expand_bias_grad,
        jnp.transpose(table_grad, (1, 0, 2)),
        jnp.transpose(vector_grads, (1, 0, 2)),
    )


def solution(mesh):
    return jax.shard_map(
        shards,
        mesh=mesh,
        in_specs=(
            P(("dp", "mp"), None),
            P("dp", None),
            P(("dp", "mp"), None),
            P(),
            P(),
            P(None, None, None, "mp"),
            P(None, None, "mp"),
            P(None, "mp", None),
            P(None, "mp", None),
            P(),
            P(),
            P(),
            P(None, None, "mp"),
            P(None, "mp"),
            P(None, "mp", None),
            P(),
        ),
        out_specs=(
            P(("dp", "mp"), None),
            P(("dp", "mp"), None),
            P(None, "dp", None, "mp"),
            P(None, "mp", "dp"),
            P(None, "dp", "mp"),
            P(None, "mp", "dp"),
            P(None, None, "mp"),
            P(None, "mp"),
            P(None, "mp", None),
            P(),
        ),
        check_vma=False,
    )
```

```python
import jax
import jax.numpy as jnp
import numpy as np
from jax import lax
from jax.experimental import pallas as pl
from jax.experimental.pallas import tpu as pltpu
from jax.sharding import PartitionSpec as P

HEAD_DIM = 32
GRID = 14
WIN = 7
SHIFT = 3
PATCHES = 196
BLOCK = 98
SLOT = 128
KEYS = 112
LANES = 128
SPAN = 2 * WIN - 1
TURN = 256

EPSILON = 1e-05
MASKED = -1e30
F32 = jnp.float32
BF16 = jnp.bfloat16
VMEM_LIMIT = 14 * 1024 * 1024

IN_VMEM = pl.BlockSpec(memory_space=pltpu.VMEM)
IN_SMEM = pl.BlockSpec(memory_space=pltpu.SMEM)
ANYWHERE = pl.BlockSpec(memory_space=pl.ANY)
IN_HBM = pl.BlockSpec(memory_space=pltpu.HBM)


def shape(dims, kind):
    return jax.ShapeDtypeStruct(dims, kind)


def far(dims, kind):
    return pltpu.HBM(dims, kind)


class Saver:
    def __init__(self, held, outs, sems):
        self.held, self.outs, self.sems = held, outs, sems
        self.copies = []

    def put(self, index, value):
        self.held[index][...] = value
        self.start(index)

    def start(self, index):
        copy = pltpu.make_async_copy(self.held[index], self.outs[index], self.sems.at[index])
        copy.start()
        self.copies.append(copy)

    def wait(self):
        for copy in self.copies:
            copy.wait()


class Near:
    def __init__(self, held):
        self.held = held

    def put(self, index, value):
        self.held[index][...] = value

    def get(self, index):
        return self.held[index]

    def start(self, index):
        pass

    def wait(self):
        pass


class Loader:
    def __init__(self, sources, held, sems):
        self.held = held
        self.copies = [
            pltpu.make_async_copy(source, target, sems.at[index])
            for index, (source, target) in enumerate(zip(sources, held))
        ]
        self.waiting = set(range(len(held)))
        for copy in self.copies:
            copy.start()

    def get(self, index):
        if index in self.waiting:
            self.waiting.remove(index)
            self.copies[index].wait()
        return self.held[index]


FETCHED = []
LINE = []
COST = 1.0e9
FAR_LAYERS = ()
PLAN = (
    "ffn_1_other",
    "ffn_1_own",
    "ffn_grads_1",
    "attention_back_1_own",
    "ffn_sum_1",
    "attention_back_1_other",
    "attention_grads_1",
    "ffn_back_0_other",
    "ffn_back_0_own",
    "ffn_grads_0",
    "attention_sum_1",
    "ffn_sum_1",
    "ffn_sum_0",
    "attention_sum_1",
    "attention_back_0_own",
    "attention_back_0_other",
    "attention_grads_0",
    "ffn_sum_1",
    "attention_sum_0",
    "pack",
    "ffn_sum_0",
    "attention_sum_0",
    "ffn_sum_0",
    "attention_sum_1",
    "block_output",
    "ffn_end_1",
    "attention_sum_0",
    "total",
    "tokens_grad",
    "attention_end_1",
    "attention_outputs",
    "total",
    "total",
    "ffn_outputs",
    "unpack",
)
MICROS = {
    "attention_back_1_own": 14.22,
    "attention_back_1_other": 0.06,
    "attention_grads_1": 0.81,
    "ffn_back_0_other": 1.81,
    "ffn_back_0_own": 0.26,
    "ffn_grads_0": 0.05,
    "attention_back_0_own": 0.36,
    "attention_back_0_other": 0.05,
    "attention_grads_0": 0.05,
    "pack": 2.09,
    "ffn_grads_1": 0.3,
}
PIECES = {"ffn": 2, "attention": 2}
BIT_ORDER = {
    "ffn_1": (0, 2, 1, 3),
    "attention_1": (0, 1, 2, 3),
    "ffn_0": (0, 2, 1, 3),
    "attention_0": (0, 1, 2, 3),
    "total": (0, 2, 1, 3),
}


def kernel_call(body, outs, out_specs, ins, in_specs, scratch, name, micros, also=(), limit=None, fetch=()
):
    behind = [item for item in (*LINE, *also) if not any(item is used for used in ins)]
    skipped = len(behind)
    ins = [
        pltpu.with_memory_space_constraint(item, pltpu.HBM) if spec is IN_HBM else item
        for item, spec in zip(ins, in_specs)
    ]
    flat = outs if isinstance(outs, list) else [outs]
    flat_specs = out_specs if isinstance(out_specs, list) else [out_specs]
    count, near_count = len(fetch), len(ins)

    def whole(*refs):
        refs = refs[skipped:]
        own_ins, sources, refs = refs[:near_count], refs[near_count : near_count + count], refs[near_count + count :]
        own_outs, targets, refs = refs[: len(flat)], refs[len(flat) : len(flat) + count], refs[len(flat) + count :]
        copies = []
        if count:
            refs, sems = refs[:-1], refs[-1]
            for index, (_, layer) in enumerate(fetch):
                copy = pltpu.make_async_copy(
                    sources[index].at[layer], targets[index], sems.at[index]
                )
                copy.start()
                copies.append(copy)
        body(*own_ins, *own_outs, *refs)
        for copy in copies:
            copy.wait()

    found = pl.pallas_call(
        whole,
        out_shape=flat + [shape(item.shape[1:], item.dtype) for item, _ in fetch],
        in_specs=[ANYWHERE] * skipped + in_specs + [IN_HBM] * count,
        out_specs=flat_specs + [IN_VMEM] * count,
        scratch_shapes=list(scratch) + ([pltpu.SemaphoreType.DMA((count,))] if count else []),
        compiler_params=pltpu.CompilerParams(vmem_limit_bytes=limit or VMEM_LIMIT),
        cost_estimate=pl.CostEstimate(
            flops=int(micros * COST), bytes_accessed=1024, transcendentals=0
        ),
        name=name,
    )(
        *behind,
        *ins,
        *[pltpu.with_memory_space_constraint(item, pltpu.HBM) for item, _ in fetch],
    )
    near = [item for item, kind in zip(found, flat) if isinstance(kind, jax.ShapeDtypeStruct)]
    if near:
        LINE[:] = [min(near, key=lambda item: item.size)]
    else:
        LINE[:] = [pltpu.with_memory_space_constraint(found[0], pltpu.HBM)]
    if count:
        found, FETCHED[:] = found[: len(flat)], found[len(flat) :]
    return found if isinstance(outs, list) else found[0]


def dot_nn(left, right):
    return lax.dot_general(left, right, (((1,), (0,)), ((), ())), preferred_element_type=F32)


def dot_nt(left, right):
    return lax.dot_general(left, right, (((1,), (1,)), ((), ())), preferred_element_type=F32)


def dot_tn(left, right):
    return lax.dot_general(left, right, (((0,), (0,)), ((), ())), preferred_element_type=F32)


def dot_tt(left, right):
    return lax.dot_general(left, right, (((0,), (1,)), ((), ())), preferred_element_type=F32)


def dot_full(left, right, contracted):
    return lax.dot_general(
        left,
        right,
        (contracted, ((), ())),
        preferred_element_type=F32,
        precision=lax.Precision.HIGHEST,
    )


def place_matrix(layer):
    row = lax.broadcasted_iota(jnp.int32, (2 * SLOT, PATCHES), 0)
    patch = lax.broadcasted_iota(jnp.int32, (2 * SLOT, PATCHES), 1)
    second = row >= SLOT
    within = jnp.where(second, row - SLOT, row)
    found = within + jnp.where(second, BLOCK, 0) + layer * SHIFT * GRID
    found = jnp.where(found >= PATCHES, found - PATCHES, found)
    return jnp.where((within < BLOCK) & (found == patch), 1.0, 0.0).astype(BF16)


def window_matrix(layer, block):
    def groups(place):
        turned_row = (place * 147) >> 11
        col = place - turned_row * GRID
        row = turned_row + block * WIN + layer * SHIFT
        row = jnp.where(row >= GRID, row - GRID, row)

        def group(position):
            moved = position + layer * (WIN - SHIFT)
            return jnp.where(moved >= 2 * WIN, 2, jnp.where(moved >= WIN, 1, 0))

        return group(row) * 4 + group(col)

    key = lax.broadcasted_iota(jnp.int32, (KEYS, LANES), 0)
    query = lax.broadcasted_iota(jnp.int32, (KEYS, LANES), 1)
    return (groups(key) == groups(query)) & (key < BLOCK) & (query < BLOCK)


def offset_matrix():
    offset = lax.broadcasted_iota(jnp.int32, (SPAN * SPAN, TURN), 0)
    lane = lax.broadcasted_iota(jnp.int32, (SPAN * SPAN, TURN), 1)
    row = (offset * 79) >> 10
    place = offset - row * SPAN + row * GRID - (WIN - 1) * (GRID + 1)
    return jnp.where(jnp.where(place < 0, place + TURN, place) == lane, 1.0, 0.0)


def heads_apart(value):
    rows = value.shape[0]
    parts = []
    for member in range(rows // HEAD_DIM):
        start = member * HEAD_DIM
        pieces = [value[start : start + HEAD_DIM]]
        if start:
            pieces.insert(0, jnp.zeros((start, value.shape[1]), value.dtype))
        if start + HEAD_DIM < rows:
            pieces.append(jnp.zeros((rows - start - HEAD_DIM, value.shape[1]), value.dtype))
        parts.append(jnp.concatenate(pieces, axis=0))
    return jnp.concatenate(parts, axis=1)


def heads_together(value):
    count = value.shape[0] // HEAD_DIM
    columns = value.shape[1] // count
    return jnp.concatenate(
        [
            value[
                member * HEAD_DIM : (member + 1) * HEAD_DIM,
                member * columns : (member + 1) * columns,
            ]
            for member in range(count)
        ],
        axis=0,
    )


def norm_rows(stream, gain, shift):
    center = stream - jnp.mean(stream, axis=-1, keepdims=True)
    spread = jnp.mean(center * center, axis=-1, keepdims=True)
    rstd = lax.rsqrt(spread + EPSILON)
    x_hat = center * rstd
    return x_hat, rstd, (x_hat * gain + shift).astype(BF16)


def norm_back(grad_normed, x_hat, rstd, gain):
    scaled = grad_normed * gain
    term = jnp.mean(scaled, axis=-1, keepdims=True)
    along = jnp.mean(scaled * x_hat, axis=-1, keepdims=True)
    return rstd * (scaled - term - x_hat * along)


def column_sum(value):
    return jnp.sum(value, axis=0, keepdims=True)


def put_sums(out, prior, sums):
    for row, found in enumerate(sums):
        out[row : row + 1] = found if prior is None else found + prior[row : row + 1]
    out[len(sums) :] = jnp.zeros((out.shape[0] - len(sums), out.shape[1]), F32)


FIRST_GAIN, FIRST_SHIFT, ATTENTION_BIAS, SECOND_GAIN, SECOND_SHIFT, REDUCE_BIAS = range(6)


def vector_row(vectors, member, layer):
    row = member * (vectors.shape[0] // 6) + layer
    return vectors[row : row + 1]


def head_lanes(rows, member):
    lane = lax.broadcasted_iota(jnp.int32, (rows, LANES), 1)
    return (lane >= member * HEAD_DIM) & (lane < (member + 1) * HEAD_DIM)


def head_rows(value):
    rows = value.shape[0]
    return jnp.concatenate(
        [
            jnp.where(head_lanes(rows, member), value, jnp.zeros_like(value))
            for member in range(LANES // HEAD_DIM)
        ],
        axis=0,
    )


def tables_body(heads, layers, refs):
    half = refs[0]
    in_hbm, refs = refs[1:13], refs[13:]
    biases, refs = refs[:layers], refs[layers:]
    masks, refs = refs[: 2 * layers], refs[2 * layers :]
    keep_out, vectors_out = refs[:2]
    held = [refs[6], refs[7], *refs[2:6], *refs[8:14]]
    sems = refs[14]
    copies = []
    for index, (source, target) in enumerate(zip(in_hbm, held)):
        copies.append(pltpu.make_async_copy(source, target, sems.at[index]))
        copies[-1].start()
    table, keep = held[:2]
    same = lax.broadcasted_iota(jnp.int32, (KEYS, LANES), 0) == lax.broadcasted_iota(
        jnp.int32, (KEYS, LANES), 1
    )
    offsets = offset_matrix()
    per_group = LANES // HEAD_DIM
    for copy in copies:
        copy.wait()
    own_first = half[0] == 0
    rows = [keep[image : image + 1].astype(F32) for image in range(2)]
    pair = jnp.concatenate(
        [jnp.where(own_first, rows[0], rows[1]), jnp.where(own_first, rows[1], rows[0])], axis=0
    ).astype(BF16)
    for layer in range(layers):
        line = dot_full(table[:, layer], offsets, ((1,), (0,)))
        for head in range(heads):
            wide = jnp.broadcast_to(line[head : head + 1], (KEYS, TURN))
            lanes = head % per_group * LANES
            biases[layer][head // per_group, :, lanes : lanes + LANES] = pltpu.roll(
                wide, 0, 1, stride=1, stride_axis=0
            )[:, :LANES]
        place = place_matrix(layer)
        kept = dot_nt(place, pair)
        for block in range(2):
            window = window_matrix(layer, block)
            for image in range(2):
                column = kept[block * SLOT : block * SLOT + KEYS, image : image + 1]
                fine = window & ((column > 0.5) | same)
                masks[layer * 2 + image][block] = jnp.where(fine, 0.0, MASKED)
        if layer == 0:
            keep_out[...] = dot_tn(place, kept.astype(BF16))
    for index, item in enumerate(held[6:]):
        vectors_out[index * layers : (index + 1) * layers] = item[...]


def make_tables(half, position_table, keep_mask, moved, vectors, fetch, also):
    heads, layers, _ = position_table.shape
    groups = heads * HEAD_DIM // LANES
    width = vectors[0].shape[1]
    ins = (position_table, keep_mask, *moved, *vectors)
    outs = [shape((groups, KEYS, 4 * LANES), F32)] * layers + [shape((2, KEYS, LANES), F32)] * (
        2 * layers
    )
    outs += [
        shape((PATCHES, 2), F32),
        shape((len(vectors) * layers, width), F32),
        *[shape(item.shape, item.dtype) for item in moved],
    ]
    found = kernel_call(
        lambda *refs: tables_body(heads, layers, refs),
        outs,
        [IN_VMEM] * len(outs),
        (half, *ins),
        [IN_SMEM] + [IN_HBM] * len(ins),
        [pltpu.VMEM(item.shape, item.dtype) for item in (*ins[:2], *vectors)]
        + [pltpu.SemaphoreType.DMA((len(ins),))],
        "tables",
        1.6,
        also,
        None,
        fetch,
    )
    masks = [found[layers + 2 * layer : layers + 2 * layer + 2] for layer in range(layers)]
    return found[:layers], masks, found[3 * layers :]


def attention_body(layer, heads, chained, refs):
    if chained:
        base, mine, theirs = refs[:3]
        refs = refs[3:]
    else:
        base, refs = refs[0], refs[1:]
    vectors, pair_bias, bias, mask, in_held, out_held = refs[:6]
    refs = refs[6:]
    if chained:
        stream_out, refs = refs[0], refs[1:]
    hat_out, rstd_out, partial_out = refs[1], refs[2], refs[6]
    far_outs = (refs[0], refs[3], refs[4], refs[5])
    turned = refs[7]
    save = Saver(refs[8:12], far_outs, refs[12]) if layer in FAR_LAYERS else Near(far_outs)
    qkv_out, weights_out = save.held[1:3]
    width = heads * HEAD_DIM
    stream = base[...].astype(F32)
    if chained:
        stream = (
            stream
            + (mine[...].astype(F32) + theirs[...].astype(F32))
            + vector_row(vectors, REDUCE_BIAS, layer - 1)
        )
        stream_out[...] = stream
    x_hat, rstd, normed = norm_rows(
        stream, vector_row(vectors, FIRST_GAIN, layer), vector_row(vectors, FIRST_SHIFT, layer)
    )
    save.put(0, normed)
    hat_out[...] = x_hat.astype(BF16)
    rstd_out[...] = rstd
    place = place_matrix(layer)
    parts = []
    for member in range(3):
        mixed = dot_nn(normed, in_held[member])
        if member != 1:
            mixed = mixed + pair_bias[layer, member // 2 : member // 2 + 1]
        parts.append(mixed.astype(BF16))
        qkv_out[:, member * width : (member + 1) * width] = parts[-1]
    save.start(1)
    queries = dot_tt(parts[0], place).astype(BF16)
    keys = dot_nn(place, parts[1]).astype(BF16)
    values = dot_tt(parts[2], place).astype(BF16)
    scale = HEAD_DIM ** (-0.5)
    groups = width // LANES
    for group in range(groups):
        lanes = slice(group * LANES, (group + 1) * LANES)
        for block in range(2):
            slots = slice(block * SLOT, (block + 1) * SLOT)
            own_keys = slice(block * SLOT, block * SLOT + KEYS)
            scores = dot_nn(keys[own_keys, lanes], heads_apart(queries[lanes, slots])) * scale
            scores = scores + bias[group] + jnp.concatenate([mask[block]] * 4, axis=1)
            raised = jnp.exp(scores - jnp.max(scores, axis=0, keepdims=True))
            weights = raised * (1.0 / jnp.sum(raised, axis=0, keepdims=True))
            weights = weights.astype(BF16)
            weights_out[group * 2 + block] = weights
            found = heads_together(dot_nn(values[lanes, own_keys], weights))
            turned[lanes, slots] = found.astype(BF16)
    attended = dot_tt(place, turned[...]).astype(BF16)
    save.start(2)
    save.put(3, attended)
    partial_out[...] = dot_nn(attended, out_held[...]).astype(BF16)
    save.wait()


def attention_forward(layer, streams, vectors, pair_bias, bias, mask, matrix_in, matrix_out, also=(), fetch=(), micros=4):
    chained = len(streams) > 1
    rows, width = streams[0].shape
    head_width = matrix_out.shape[0]
    put = far if layer in FAR_LAYERS else shape
    spec = IN_HBM if layer in FAR_LAYERS else IN_VMEM
    heads = head_width // HEAD_DIM
    saved = [
        (rows, width),
        (rows, 3 * head_width),
        (2 * head_width // LANES, KEYS, 4 * LANES),
        (rows, head_width),
    ]
    outs = [
        put(saved[0], BF16),
        shape((rows, width), BF16),
        shape((rows, 1), F32),
        *[put(dims, BF16) for dims in saved[1:]],
        shape((rows, width), BF16),
    ]
    out_specs = [spec, IN_VMEM, IN_VMEM, spec, spec, spec, IN_VMEM]
    if chained:
        outs = [shape((rows, width), F32)] + outs
        out_specs = [IN_VMEM] + out_specs
    ins = (*streams, vectors, pair_bias, bias, mask, matrix_in, matrix_out)
    found = kernel_call(
        lambda *refs: attention_body(layer, heads, chained, refs),
        outs,
        out_specs,
        ins,
        [IN_VMEM] * len(ins),
        [pltpu.VMEM((head_width, 2 * SLOT), BF16)]
        + (
            [*[pltpu.VMEM(dims, BF16) for dims in saved], pltpu.SemaphoreType.DMA((4,))]
            if layer in FAR_LAYERS
            else []
        ),
        f"attention_{layer}",
        micros,
        also,
        None,
        fetch,
    )
    return found if chained else [streams[0], *found]


def gelu_parts(hidden):
    below = 0.5 * (1.0 + lax.erf(hidden * (0.5**0.5)))
    density = jnp.exp(-0.5 * hidden * hidden) * (0.5 / np.pi) ** 0.5
    return hidden * below, below + hidden * density


def ffn_body(layer, both, image, joined, step, refs):
    base, mine, theirs, vectors, up_bias = refs[:5]
    refs = refs[5:]
    if both:
        grad, keep, refs = refs[0], refs[1], refs[2:]
    if joined:
        prior_sums, refs = refs[0], refs[1:]
    up_held, down_held, *refs = refs
    mid_out, hat_out, rstd_out, partial_out = refs[0], refs[2], refs[3], refs[6]
    far_outs = (refs[1], refs[4], refs[5])
    if both:
        back_out, sums_out, grad_out = refs[7:10]
    held = refs[7:]
    save = Saver(held[:3], far_outs, held[3]) if layer in FAR_LAYERS else Near(far_outs)
    active_out, slope_out = save.held[1:]
    mid = (
        base[...].astype(F32)
        + (mine[...].astype(F32) + theirs[...].astype(F32))
        + vector_row(vectors, ATTENTION_BIAS, layer)
    )
    mid_out[...] = mid
    x_hat, rstd, normed = norm_rows(
        mid, vector_row(vectors, SECOND_GAIN, layer), vector_row(vectors, SECOND_SHIFT, layer)
    )
    save.put(0, normed)
    hat_out[...] = x_hat.astype(BF16)
    rstd_out[...] = rstd
    if both:
        grad_rows = (grad[...].astype(F32) * keep[:, image : image + 1]).astype(BF16)
        grad_out[...] = grad_rows
        put_sums(sums_out, prior_sums if joined else None, [column_sum(grad_rows.astype(F32))])
    forward, backward = None, None
    for start in range(0, up_held.shape[1], step):
        part = slice(start, start + step)
        hidden = dot_nn(normed, up_held[:, part]) + up_bias[layer : layer + 1, part]
        active, slope = gelu_parts(hidden)
        active = active.astype(BF16)
        active_out[:, part] = active
        term = dot_nn(active, down_held[part])
        forward = term if forward is None else forward + term
        if both:
            grad_hidden = (slope * dot_nt(grad_rows, down_held[part])).astype(BF16)
            slope_out[:, part] = grad_hidden
            term = dot_nt(grad_hidden, up_held[:, part])
            backward = term if backward is None else backward + term
        else:
            slope_out[:, part] = slope.astype(BF16)
    save.start(1)
    save.start(2)
    partial_out[...] = forward.astype(BF16)
    if both:
        back_out[...] = backward.astype(BF16)
    save.wait()


def ffn_forward(layer, image, streams, vectors, up_bias, up, down, grad=None, keep=None, prior_sums=None, fetch=(), also=()):
    rows, width = streams[0].shape
    units = up.shape[1]
    both = grad is not None
    put = far if layer in FAR_LAYERS else shape
    saved = [(rows, width), (rows, units), (rows, units)]
    outs = [
        shape((rows, width), F32),
        put(saved[0], BF16),
        shape((rows, width), BF16),
        shape((rows, 1), F32),
        put(saved[1], BF16),
        put(saved[2], BF16),
        shape((rows, width), BF16),
    ]
    ins = [*streams, vectors, up_bias]
    if both:
        outs += [shape((rows, width), BF16), shape((8, width), F32), shape((rows, width), BF16)]
        ins += [grad, keep]
    joined = prior_sums is not None
    if joined:
        ins.append(prior_sums)
    specs = [IN_VMEM] * (len(ins) + 2)
    return kernel_call(
        lambda *refs: ffn_body(layer, both, image, joined, units // 3, refs),
        outs,
        [IN_VMEM if put is shape or index not in (1, 4, 5) else IN_HBM for index in range(len(outs))],
        (*ins, up, down),
        specs,
        []
        if put is shape
        else [*[pltpu.VMEM(dims, BF16) for dims in saved], pltpu.SemaphoreType.DMA((3,))],
        f"ffn_both_{layer}" if both else f"ffn_{layer}",
        4.6 if both else 3,
        also,
        None,
        fetch,
    )


def ffn_back_body(layer, joined, step, refs):
    base, mine, theirs, hat, rstd, vectors = refs[:6]
    refs = refs[6:]
    if joined:
        prior_sums, refs = refs[0], refs[1:]
    slope_hbm, up_held, down_held = refs[:3]
    grad_out, low_out, hidden_out, partial_out, sums_out = refs[3:8]
    slope, load = slope_hbm, Near([slope_hbm])
    if layer in FAR_LAYERS:
        slope = refs[8]
        load = Loader([slope_hbm], [slope], refs[9])
    grad_normed = mine[...].astype(F32) + theirs[...].astype(F32)
    x_hat = hat[...].astype(F32)
    grad = base[...] + norm_back(
        grad_normed, x_hat, rstd[...], vector_row(vectors, FIRST_GAIN, layer + 1)
    )
    grad_out[...] = grad
    low = grad.astype(BF16)
    low_out[...] = low
    sums = [column_sum(grad_normed * x_hat), column_sum(grad_normed), column_sum(grad)]
    put_sums(sums_out, prior_sums if joined else None, sums)
    backward = None
    load.get(0)
    for start in range(0, up_held.shape[1], step):
        part = slice(start, start + step)
        grad_hidden = (slope[:, part].astype(F32) * dot_nt(low, down_held[part])).astype(BF16)
        hidden_out[:, part] = grad_hidden
        term = dot_nt(grad_hidden, up_held[:, part])
        backward = term if backward is None else backward + term
    partial_out[...] = backward.astype(BF16)


def ffn_backward(layer, grads, hat, rstd, vectors, slope, up, down, prior_sums=None, micros=4, fetch=()):
    rows, width = grads[0].shape
    units = up.shape[1]
    outs = [
        shape((rows, width), F32),
        shape((rows, width), BF16),
        shape((rows, units), BF16),
        shape((rows, width), BF16),
        shape((8, width), F32),
    ]
    ins = [*grads, hat, rstd, vectors]
    joined = prior_sums is not None
    if joined:
        ins.append(prior_sums)
    return kernel_call(
        lambda *refs: ffn_back_body(layer, joined, units // 3, refs),
        outs,
        [IN_VMEM] * 5,
        (*ins, slope, up, down),
        [IN_VMEM] * len(ins) + [IN_HBM if layer in FAR_LAYERS else IN_VMEM] + [IN_VMEM] * 2,
        [pltpu.VMEM((rows, units), BF16), pltpu.SemaphoreType.DMA((1,))]
        if layer in FAR_LAYERS
        else [],
        f"ffn_back_{layer}",
        micros,
        (),
        None,
        fetch,
    )


def attention_back_body(layer, heads, joined, refs):
    base, mine, theirs, hat, rstd, vectors, first_hat = refs[:7]
    refs = refs[7:]
    if joined:
        prior_sums, prior_table = refs[:2]
        refs = refs[2:]
    qkv, weights, in_held, out_held = refs[:4]
    grad_out, low_out, mixed_out, partial_out, sums_out, table_out = refs[4:10]
    turned, merged, diagonals = refs[10:13]
    load = Near([qkv, weights])
    if layer in FAR_LAYERS:
        load = Loader([qkv, weights], refs[13:15], refs[15])
        qkv, weights = refs[13:15]
    width = heads * HEAD_DIM
    per_group = LANES // HEAD_DIM
    grad_normed = mine[...].astype(F32) + theirs[...].astype(F32)
    x_hat = hat[...].astype(F32)
    grad = base[...].astype(F32) + norm_back(
        grad_normed, x_hat, rstd[...], vector_row(vectors, SECOND_GAIN, layer)
    )
    grad_out[...] = grad
    low = grad.astype(BF16)
    low_out[...] = low
    sums = [column_sum(grad_normed * x_hat), column_sum(grad_normed), column_sum(grad)]
    place = place_matrix(layer)
    load.get(0)
    queries = dot_nn(place, qkv[:, :width]).astype(BF16)
    turned_keys = dot_tt(qkv[:, width : 2 * width], place).astype(BF16)
    values = dot_nn(place, qkv[:, 2 * width :]).astype(BF16)
    grad_attended = dot_nt(low, out_held[...]).astype(BF16)
    grad_slots = dot_nn(place, grad_attended).astype(BF16)
    grad_turned = dot_tt(grad_attended, place).astype(BF16)
    load.get(1)
    scale = HEAD_DIM ** (-0.5)
    empty = jnp.zeros((SLOT - KEYS, LANES), BF16)
    for group in range(width // LANES):
        lanes = slice(group * LANES, (group + 1) * LANES)
        total = None
        for block in range(2):
            top_row = block * SLOT
            slots = slice(top_row, top_row + SLOT)
            own_keys = slice(top_row, top_row + KEYS)
            low_weights = weights[group * 2 + block]
            full = low_weights.astype(F32)
            grad_weights = dot_nn(values[own_keys, lanes], heads_apart(grad_turned[lanes, slots]))
            spread = jnp.sum(full * grad_weights, axis=0, keepdims=True)
            grad_scores = full * (grad_weights - spread)
            total = grad_scores if total is None else total + grad_scores
            grad_raw = (grad_scores * scale).astype(BF16)
            grad_query = heads_together(dot_nn(turned_keys[lanes, own_keys], grad_raw))
            grad_key = dot_nn(grad_raw, head_rows(queries[slots, lanes]))
            grad_value = dot_nn(low_weights, head_rows(grad_slots[slots, lanes]))
            turned[lanes, slots] = grad_query.astype(BF16)
            for at, found in ((0, grad_key), (width, grad_value)):
                columns = slice(at + group * LANES, at + (group + 1) * LANES)
                merged[own_keys, columns] = found.astype(BF16)
                merged[top_row + KEYS : top_row + SLOT, columns] = empty
        for member in range(per_group):
            head = group * per_group + member
            own = total[:, member * LANES : (member + 1) * LANES]
            wide = jnp.concatenate([own, jnp.zeros_like(own)], axis=1)
            line = None
            for start in range(0, KEYS, 8):
                rows = wide[start : start + 8]
                if start:
                    rows = pltpu.roll(rows, TURN - start, 1)
                line = rows if line is None else line + rows
            diagonals[head * 8 : head * 8 + 8] = line
    mixed = [dot_tt(place, turned[...]).astype(BF16)]
    both = dot_tn(place, merged[...]).astype(BF16)
    mixed += [both[:, :width], both[:, width:]]
    mixed_out[:, :width] = mixed[0]
    mixed_out[:, width:] = both
    partial = dot_nt(mixed[0], in_held[0])
    partial = partial + dot_nt(mixed[1], in_held[1])
    partial = partial + dot_nt(mixed[2], in_held[2])
    partial_out[...] = partial.astype(BF16)
    sums += [column_sum(partial * first_hat[...].astype(F32)), column_sum(partial)]
    put_sums(sums_out, prior_sums if joined else None, sums)
    lines = diagonals[...]
    row = lax.broadcasted_iota(jnp.int32, lines.shape, 0)
    for bit in range(3):
        moved = pltpu.roll(lines, TURN - (1 << bit), 1)
        lines = jnp.where(((row >> bit) & 1) == 1, moved, lines)
    lines = jnp.sum(lines.reshape(heads, 8, TURN), axis=1)
    table = dot_full(lines, offset_matrix(), ((1,), (1,)))
    table_out[...] = table + prior_table[...] if joined else table


def attention_backward(
    layer, grads, hat, rstd, vectors, first_hat, qkv, weights, matrix_in, matrix_out,
    prior=(), micros=5, fetch=(),
):
    rows, width = grads[0].shape
    head_width = matrix_out.shape[0]
    heads = head_width // HEAD_DIM
    outs = [
        shape((rows, width), F32),
        shape((rows, width), BF16),
        shape((rows, 3 * head_width), BF16),
        shape((rows, width), BF16),
        shape((8, width), F32),
        shape((heads, SPAN * SPAN), F32),
    ]
    ins = (*grads, hat, rstd, vectors, first_hat, *prior)
    return kernel_call(
        lambda *refs: attention_back_body(layer, heads, bool(prior), refs),
        outs,
        [IN_VMEM] * 6,
        (*ins, qkv, weights, matrix_in, matrix_out),
        [IN_VMEM] * len(ins) + [IN_HBM if layer in FAR_LAYERS else IN_VMEM] * 2 + [IN_VMEM] * 2,
        [
            pltpu.VMEM((head_width, 2 * SLOT), BF16),
            pltpu.VMEM((2 * SLOT, 2 * head_width), BF16),
            pltpu.VMEM((heads * 8, TURN), F32),
        ]
        + (
            [
                pltpu.VMEM(qkv.shape, BF16),
                pltpu.VMEM(weights.shape, BF16),
                pltpu.SemaphoreType.DMA((2,)),
            ]
            if layer in FAR_LAYERS
            else []
        ),
        f"attention_back_{layer}",
        micros,
        (),
        None,
        fetch,
    )


def finish_body(base, mine, theirs, hat, rstd, vectors, out):
    grad_normed = mine[...].astype(F32) + theirs[...].astype(F32)
    out[...] = base[...] + norm_back(
        grad_normed, hat[...].astype(F32), rstd[...], vector_row(vectors, FIRST_GAIN, 0)
    )


def output_body(layer, base, mine, theirs, vectors, out):
    total = base[...] + (mine[...].astype(F32) + theirs[...].astype(F32))
    out[...] = (total + vector_row(vectors, REDUCE_BIAS, layer)).astype(BF16)


def finish(body, kind, name, micros, *ins):
    return kernel_call(
        body, pltpu.HBM(ins[0].shape, kind), IN_VMEM, ins, [IN_VMEM] * len(ins), [], name, micros
    )


def group_place(group, top, order):
    place = 0
    for step, bit in enumerate(order):
        place = place + ((((group >> bit) & 1) ^ ((top >> bit) & 1)) << (len(order) - 1 - step))
    return place


def grads_body(pairs, groups, order, step, summed, far_ins, refs):
    top = refs[0][0]
    lefts = 1 + max(left for left, _ in pairs)
    rights = len(pairs)
    refs = refs[1:]
    total = 2 * (lefts + rights)
    sources, refs = refs[:total], refs[total:]
    held_ins = list(sources)
    far_count = sum(far_ins)
    if far_count:
        scratch, sems, refs = refs[-far_count - 1 : -1], refs[-1], refs[: -far_count - 1]
        loader = Loader([item for item, is_far in zip(sources, far_ins) if is_far], scratch, sems)
        places = [index for index, is_far in enumerate(far_ins) if is_far]

    def get(index):
        return loader.get(places.index(index)) if far_ins[index] else held_ins[index]

    keep_out, sums_out, held, turned, wide, sems = (refs[0], *refs[-5:])
    send_outs = refs[1:-5]
    rows = sources[0].shape[0]
    space = wide.shape[0] // 2
    empty = space - rows
    block = keep_out.shape[1]
    copies = []
    for left in range(lefts):
        for image in range(2):
            start = image * space
            turned[left, :, start + LANES : start + space] = jnp.zeros(
                (turned.shape[1], space - LANES), BF16
            )
            turned[left, :, start : start + rows] = get(2 * left + image)[...].T
    at = 0
    sum_at = 0
    for right, (left, _) in enumerate(pairs):
        columns = sources[2 * (lefts + right)].shape[1]
        for image in range(2):
            start = image * space
            wide[start : start + rows, :columns] = get(2 * (lefts + right) + image)[...]
            wide[start + rows : start + space, :columns] = jnp.zeros((empty, columns), BF16)
        if summed[right]:
            sums_out[0:1, sum_at : sum_at + columns] = column_sum(wide[:, :columns].astype(F32))
            sum_at += columns
        for first in range(0, columns, step):
            found = dot_nn(turned[left], wide[:, first : first + step]).astype(BF16)
            for group in range(groups):
                held[group_place(group, top, order), :, at : at + step] = found[
                    group * block : (group + 1) * block
                ]
            sent = at // send_outs[0].shape[2]
            inner = at - sent * send_outs[0].shape[2]
            for half, out in (
                (0, keep_out.at[:, :, at : at + step]),
                (1, send_outs[sent].at[:, :, inner : inner + step]),
            ):
                copy = pltpu.make_async_copy(
                    held.at[half * groups // 2 : (half + 1) * groups // 2, :, at : at + step],
                    out,
                    sems.at[half, at // step],
                )
                copy.start()
                copies.append(copy)
            at += step
    for copy in copies:
        copy.wait()


def weight_grads(top, groups, order, pairs, lefts, rights, summed, pieces, far_ins, name, micros):
    width = lefts[0].shape[1]
    step = 512 if all(item.shape[1] % 512 == 0 for item in rights) else 384
    columns = sum(item.shape[1] for item in rights[::2])
    widest = max(item.shape[1] for item in rights)
    space = 2 * LANES
    summed_columns = sum(item.shape[1] for item, used in zip(rights[::2], summed) if used)
    outs = [
        shape((groups // 2, width // groups, columns), BF16),
        *[shape((groups // 2, width // groups, columns // pieces), BF16)] * pieces,
        shape((8, summed_columns), F32),
    ]
    count = 1 + max(left for left, _ in pairs)
    kept, *sent, sums = kernel_call(
        lambda *refs: grads_body(pairs, groups, order, step, summed, far_ins, refs),
        outs,
        [ANYWHERE] * (1 + pieces) + [IN_VMEM],
        (top, *lefts, *rights),
        [IN_SMEM] + [IN_HBM if is_far else IN_VMEM for is_far in far_ins],
        [
            pltpu.VMEM((groups, width // groups, columns), BF16),
            pltpu.VMEM((count, width, 2 * space), BF16),
            pltpu.VMEM((2 * space, widest), BF16),
            pltpu.SemaphoreType.DMA((2, columns // step)),
            *[
                pltpu.VMEM(item.shape, item.dtype)
                for item, is_far in zip((*lefts, *rights), far_ins)
                if is_far
            ],
            *([pltpu.SemaphoreType.DMA((sum(far_ins),))] if any(far_ins) else []),
        ],
        name,
        micros,
        (),
        20 * 1024 * 1024,
    )
    return kept, sent, sums


def swap(value):
    return lax.ppermute(value, "mp", [(0, 1), (1, 0)])


def trade(value, bit, size):
    return lax.ppermute(value, "dp", [(source, source ^ bit) for source in range(size)])


def fold_body(kept, *refs):
    *pieces, keep_out, send_out = refs
    half = keep_out.shape[0]
    at = 0
    for found in pieces:
        columns = slice(at, at + found.shape[2])
        at += found.shape[2]
        for start, out in ((0, keep_out), (half, send_out)):
            for block in range(half):
                total = kept[start + block, :, columns].astype(F32) + found[start + block].astype(F32)
                out[block, :, columns] = total.astype(BF16)


def fold(kept, found, name):
    half = shape((kept.shape[0] // 2, *kept.shape[1:]), BF16)
    return kernel_call(
        fold_body, [half, half], [IN_VMEM] * 2, (kept, *found), [IN_VMEM] * (1 + len(found)), [],
        name, 0.1,
    )


class Scatter:
    def __init__(self, kept, sent, order, size, name):
        self.kept, self.sent, self.order, self.size, self.name = kept, sent, order, size, name
        self.finer = size >> len(order)
        self.level = 0
        self.send()

    def send(self):
        self.found = [
            trade(item, self.finer << self.order[self.level], self.size) for item in self.sent
        ]

    def step(self):
        if self.level + 1 < len(self.order):
            self.kept, sent = fold(self.kept, self.found, f"{self.name}_{self.level}")
            self.sent = [sent]
            self.level += 1
            self.send()

    def finish(self):
        for _ in self.order:
            self.step()
        kept, finer = self.kept, self.finer
        found = jnp.concatenate(self.found, axis=2) if len(self.found) > 1 else self.found[0]
        rank = lax.axis_index("dp")
        while finer > 1:
            finer //= 2
            held = (kept.astype(F32) + found.astype(F32)).astype(BF16)
            halves = held.reshape((2, 1, held.shape[1] // 2, held.shape[2]))
            mine = (rank // finer) % 2
            kept = lax.dynamic_index_in_dim(halves, mine, 0, keepdims=False)
            found = trade(lax.dynamic_index_in_dim(halves, 1 - mine, 0, keepdims=False), finer, self.size)
        return kept, found

    def join(self):
        kept, found = self.finish()
        return (
            kernel_call(
                add_body, shape(kept.shape, F32), IN_VMEM, (kept, found), [IN_VMEM] * 2, [],
                f"{self.name}_end", 0.1,
            ),
        )


def add_body(left, right, out):
    out[...] = left[...].astype(F32) + right[...].astype(F32)


def some_bits(name, size):
    bits = range(size.bit_length() - 1)
    listed = [bit for bit in BIT_ORDER[name] if bit in bits]
    return tuple(listed + [bit for bit in bits if bit not in listed])


class Total:
    def __init__(self, value, size):
        self.value, self.size = value, size
        self.left = [1 << bit for bit in some_bits("total", size)]
        self.send()

    def send(self):
        self.found = trade(self.value, self.left.pop(0), self.size)

    def step(self):
        if self.left:
            self.value = kernel_call(
                add_body, shape(self.value.shape, F32), IN_VMEM, (self.value, self.found),
                [IN_VMEM] * 2, [], "total", 0.1,
            )
            self.send()

    def finish(self):
        while self.left:
            self.step()
        return self.value, self.found


def collect_body(counts, widths, refs):
    outs = refs[sum(counts) :]
    for layer, count in enumerate(counts):
        total = refs[0][0].astype(F32)
        if count == 2:
            total = total + refs[1][0].astype(F32)
        refs = refs[count:]
        at = 0
        for out, parts in zip(outs, widths):
            for part in range(parts):
                columns = out.shape[-1]
                if len(out.shape) == 4:
                    out[layer, part] = total[:, at : at + columns]
                else:
                    out[layer] = total[:, at : at + columns]
                at += columns


def collect(pairs, shapes, name):
    flat = [item for pair in pairs for item in pair]
    counts = [len(pair) for pair in pairs]
    return kernel_call(
        lambda *refs: collect_body(
            counts, [dims[1] if len(dims) == 4 else 1 for dims in shapes], refs
        ),
        [pltpu.HBM(dims, F32) for dims in shapes],
        [IN_VMEM] * len(shapes),
        flat,
        [IN_VMEM] * len(flat),
        [],
        name,
        0.1,
    )


def pack_body(width, layers, refs):
    sums_0, theirs_0, sums_low, sums_1, last = refs[:5]
    ups, mixes, tables = refs[5 : 5 + layers], refs[5 + layers : 5 + 2 * layers], refs[5 + 2 * layers : -1]
    out = refs[-1]
    out[...] = jnp.zeros(out.shape, F32)
    out[0:2] = sums_0[3:5] + theirs_0[3:5]
    out[2:3] = sums_0[2:3]
    out[3:5] = sums_0[0:2]
    out[5:6] = sums_low[2:3]
    out[6:8] = sums_low[0:2]
    out[8:9] = sums_1[2:3]
    out[9:11] = sums_1[0:2]
    out[11:12] = last[0:1]
    row = 6 * layers
    for item in ups:
        for start in range(0, item.shape[1], width):
            out[row : row + 1] = item[0:1, start : start + width]
            row += 1
    third = mixes[0].shape[1] // 3
    for item in mixes:
        out[row : row + 1, :third] = item[0:1, :third]
        out[row : row + 1, third : 2 * third] = item[0:1, 2 * third :]
        row += 1
    for item in tables:
        heads, offsets = item.shape
        for head in range(heads):
            lane = head * TURN % width
            out[row : row + 1, lane : lane + offsets] = item[head : head + 1]
            if (head + 1) * TURN % width == 0:
                row += 1


def unpack_body(refs):
    packed, found, vectors, up_bias, pair_bias, tables = refs
    width = packed.shape[1]
    layers, units = up_bias.shape
    total = packed[...] + found[...]
    for layer in range(layers):
        for member in range(6):
            vectors[member, layer : layer + 1] = total[6 * layer + member : 6 * layer + member + 1]
    row = 6 * layers
    for layer in range(layers):
        for start in range(0, units, width):
            up_bias[layer : layer + 1, start : start + width] = total[row : row + 1]
            row += 1
    third = pair_bias.shape[2]
    for layer in range(layers):
        for member in range(2):
            pair_bias[layer, member : member + 1] = total[
                row : row + 1, member * third : (member + 1) * third
            ]
        row += 1
    heads, _, offsets = tables.shape
    for layer in range(layers):
        for head in range(heads):
            lane = head * TURN % width
            tables[head, layer : layer + 1] = total[row : row + 1, lane : lane + offsets]
            if (head + 1) * TURN % width == 0:
                row += 1


def shards(
    tokens,
    keep_mask,
    cotangent,
    first_gain,
    first_shift,
    attention_in,
    query_value_bias,
    position_table,
    attention_out,
    attention_bias,
    second_gain,
    second_shift,
    expand_weight,
    expand_bias,
    reduce_weight,
    reduce_bias,
):
    LINE.clear()
    FETCHED.clear()
    size = lax.axis_size("dp")
    half = lax.axis_index("mp")
    groups = min(16, size)
    top = (lax.axis_index("dp") // (size // groups)).astype(jnp.int32).reshape(1)
    layers, width = first_gain.shape
    head_width = attention_out.shape[1]
    units = expand_weight.shape[2]
    heads = head_width // HEAD_DIM
    matrix_in = jnp.transpose(attention_in, (0, 2, 1, 3))
    own_half = half.astype(jnp.int32).reshape(1)
    other_tokens = swap(tokens)
    other_cotangent = swap(cotangent)
    bias, masks, (keep_columns, vectors, tokens, cotangent, up_bias, pair_bias) = make_tables(
        own_half, jnp.transpose(position_table, (1, 0, 2)), keep_mask,
        (tokens, cotangent, expand_bias, query_value_bias),
        (first_gain, first_shift, attention_bias, second_gain, second_shift, reduce_bias),
        ((matrix_in, 0), (attention_out, 0)), (top,),
    )
    heads_held = list(FETCHED)
    def attend(layer, image, streams, also=(), fetch=(), micros=4):
        return attention_forward(
            layer, streams, vectors, pair_bias, bias[layer], masks[layer][image], *heads_held,
            also, fetch, micros,
        )

    def feed(layer, image, streams, grad=None, prior_sums=None, fetch=(), also=()):
        return ffn_forward(
            layer, image, streams, vectors, up_bias, *units_held, grad, keep_columns, prior_sums,
            fetch, also,
        )

    att, ffn = [[None, None], [None, None]], [[None, None], [None, None]]
    att[0][0] = attend(0, 0, (tokens,), micros=0.3)
    sent_own = swap(att[0][0][7])
    att[0][1] = attend(
        0, 1, (other_tokens,), (), ((expand_weight, 0), (reduce_weight, 0))
    )
    units_held = list(FETCHED)
    sent_other = swap(att[0][1][7])
    ffn[0][1] = feed(
        0, 1, (att[0][1][0], att[0][1][7], sent_own), also=(other_cotangent,),
        fetch=((matrix_in, 1), (attention_out, 1)),
    )
    heads_held = list(FETCHED)
    sent_2 = swap(ffn[0][1][6])
    ffn[0][0] = feed(0, 0, (att[0][0][0], att[0][0][7], sent_other))
    sent_1 = swap(ffn[0][0][6])
    att[1][0] = attend(1, 0, (ffn[0][0][0], ffn[0][0][6], sent_2))
    sent_own = swap(att[1][0][7])
    att[1][1] = attend(
        1, 1, (ffn[0][1][0], ffn[0][1][6], sent_1), (), ((expand_weight, 1), (reduce_weight, 1))
    )
    units_held = list(FETCHED)
    sent_other = swap(att[1][1][7])

    far_ins = (True, True, False, False, False, False, True, True)

    def ffn_grads(layer, low, hidden, name):
        normed = [ffn[layer][image][1] for image in range(2)]
        active = [ffn[layer][image][4] for image in range(2)]
        order = some_bits(f"ffn_{layer}", groups)
        kept, sent, sums = weight_grads(
            top, groups, order, ((0, 0), (1, 1)), (*normed, *low), (*hidden, *active),
            (True, False), PIECES["ffn"], far_ins if layer in FAR_LAYERS else (False,) * 8, name, MICROS[name],
        )
        return Scatter(kept, sent, order, size, f"ffn_fold_{layer}"), sums

    def attention_grads(layer, low, mixed, name):
        normed = [att[layer][image][1] for image in range(2)]
        attended = [att[layer][image][6] for image in range(2)]
        order = some_bits(f"attention_{layer}", groups)
        kept, sent, sums = weight_grads(
            top, groups, order, ((0, 0), (1, 1)), (*normed, *low), (*mixed, *attended),
            (True, False), PIECES["attention"], far_ins if layer in FAR_LAYERS else (False,) * 8, name, MICROS[name],
        )
        return Scatter(kept, sent, order, size, f"attention_fold_{layer}"), sums

    def attend_back(layer, image, grads, prior=(), micros=5, fetch=()):
        held = att[layer][image]
        return attention_backward(
            layer, grads, ffn[layer][image][2], ffn[layer][image][3], vectors, held[2],
            held[4], held[5], *later["heads"], prior, micros, fetch,
        )

    def feed_back(image, grads, prior_sums=None, micros=4, fetch=()):
        held = att[1][image]
        return ffn_backward(
            0, grads, held[2], held[3], vectors, ffn[0][image][5], *later["units"],
            prior_sums, micros, fetch,
        )

    back, low = [[None, None], [None, None]], [None, None]
    later = {"heads": heads_held, "units": None}
    sent, sums, extra, outs = {}, {}, {}, {}
    rows = width // size

    def ffn_1_other():
        ffn[1][1] = feed(1, 1, (att[1][1][0], att[1][1][7], sent_own), other_cotangent)
        sent["ffn_1_other"] = swap(ffn[1][1][7])
        sent["block"] = swap(ffn[1][1][6])

    def ffn_1_own():
        ffn[1][0] = feed(1, 0, (att[1][0][0], att[1][0][7], sent_other), cotangent, ffn[1][1][8])
        sent["ffn_1_own"] = swap(ffn[1][0][7])

    def ffn_grads_1():
        sums["ffn_sum_1"], extra["up_1"] = ffn_grads(
            1, (ffn[1][0][9], ffn[1][1][9]), (ffn[1][0][5], ffn[1][1][5]), "ffn_grads_1"
        )

    def attention_back_1_own():
        back[1][0] = attend_back(
            1, 0, (ffn[1][0][9], ffn[1][0][7], sent["ffn_1_other"]), (),
            MICROS["attention_back_1_own"], ((expand_weight, 0), (reduce_weight, 0)),
        )
        later["units"] = list(FETCHED)
        sent["back_1_own"] = swap(back[1][0][3])

    def attention_back_1_other():
        back[1][1] = attend_back(
            1, 1, (ffn[1][1][9], ffn[1][1][7], sent["ffn_1_own"]), back[1][0][4:6],
            MICROS["attention_back_1_other"],
        )
        sent["back_1_other"] = swap(back[1][1][3])

    def attention_grads_1():
        sums["attention_sum_1"], extra["mixed_1"] = attention_grads(
            1, (back[1][0][1], back[1][1][1]), (back[1][0][2], back[1][1][2]), "attention_grads_1"
        )

    def ffn_back_0_other():
        low[1] = feed_back(
            1, (back[1][1][0], back[1][1][3], sent["back_1_own"]), None,
            MICROS["ffn_back_0_other"], ((matrix_in, 0), (attention_out, 0)),
        )
        later["heads"] = list(FETCHED)
        sent["low_other"] = swap(low[1][3])

    def ffn_back_0_own():
        low[0] = feed_back(
            0, (back[1][0][0], back[1][0][3], sent["back_1_other"]), low[1][4],
            MICROS["ffn_back_0_own"],
        )
        sent["low_own"] = swap(low[0][3])

    def ffn_grads_0():
        sums["ffn_sum_0"], extra["up_0"] = ffn_grads(
            0, (low[0][1], low[1][1]), (low[0][2], low[1][2]), "ffn_grads_0"
        )

    def attention_back_0_own():
        back[0][0] = attend_back(
            0, 0, (low[0][0], low[0][3], sent["low_other"]), (), MICROS["attention_back_0_own"]
        )

    def attention_back_0_other():
        back[0][1] = attend_back(
            0, 1, (low[1][0], low[1][3], sent["low_own"]), back[0][0][4:6],
            MICROS["attention_back_0_other"],
        )
        sent["last"] = swap(back[0][1][3])
        sent["sums"] = swap(back[0][1][4])

    def attention_grads_0():
        sums["attention_sum_0"], extra["mixed_0"] = attention_grads(
            0, (back[0][0][1], back[0][1][1]), (back[0][0][2], back[0][1][2]), "attention_grads_0"
        )

    def pack():
        pieces = (
            back[0][1][4], sent["sums"], low[0][4], back[1][1][4], ffn[1][0][8],
            extra["up_0"], extra["up_1"], extra["mixed_0"], extra["mixed_1"],
            back[0][1][5], back[1][1][5],
        )
        per_row = width // TURN
        count = layers * (6 + units // width + 1 + heads // per_row)
        packed = kernel_call(
            lambda *refs: pack_body(width, layers, refs),
            shape((-(-count // 8) * 8, width), F32),
            IN_VMEM,
            pieces,
            [IN_VMEM] * len(pieces),
            [],
            "pack",
            MICROS["pack"],
        )
        sums["total"] = Total(packed, size)

    def unpack():
        outs["small"] = kernel_call(
            lambda *refs: unpack_body(refs),
            [
                shape((6, layers, width), F32),
                shape((layers, units), F32),
                shape((layers, 2, head_width), F32),
                shape((heads, layers, SPAN * SPAN), F32),
            ],
            [IN_VMEM] * 4,
            sums["total"].finish(),
            [IN_VMEM] * 2,
            [],
            "unpack",
            0.1,
        )

    def tokens_grad():
        outs["tokens_grad"] = finish(
            finish_body, F32, "finish", 0.1,
            back[0][0][0], back[0][0][3], sent["last"], att[0][0][2], att[0][0][3], vectors,
        )

    def block_output():
        outs["block_output"] = finish(
            lambda *refs: output_body(1, *refs), BF16, "output", 0.1,
            ffn[1][0][0], ffn[1][0][6], sent["block"], vectors,
        )

    def attention_end_1():
        extra["attention_1"] = sums["attention_sum_1"].join()

    def ffn_end_1():
        extra["ffn_1"] = sums["ffn_sum_1"].join()

    def attention_outputs():
        outs["attention"] = collect(
            (sums["attention_sum_0"].finish(), extra["attention_1"]),
            [(layers, 3, rows, head_width), (layers, rows, head_width)],
            "attention_collect",
        )

    def ffn_outputs():
        outs["ffn"] = collect(
            (sums["ffn_sum_0"].finish(), extra["ffn_1"]), [(layers, rows, units)] * 2, "ffn_collect"
        )

    steps = {
        item.__name__: item
        for item in (
            ffn_1_other, ffn_1_own, ffn_grads_1, attention_back_1_own, attention_back_1_other,
            attention_grads_1, ffn_back_0_other, ffn_back_0_own, ffn_grads_0,
            attention_back_0_own, attention_back_0_other, attention_grads_0, pack, unpack,
            tokens_grad, block_output, attention_end_1, ffn_end_1, attention_outputs, ffn_outputs,
        )
    }
    for name in PLAN:
        if name in steps:
            steps[name]()
        else:
            sums[name].step()

    in_grad, out_grad = outs["attention"]
    up_grad, down_grad = outs["ffn"]
    vector_grads, expand_bias_grad, pair_grad, table_grad = outs["small"]
    return (
        outs["block_output"],
        outs["tokens_grad"],
        jnp.transpose(in_grad, (0, 2, 1, 3)),
        jnp.transpose(out_grad, (0, 2, 1)),
        up_grad,
        jnp.transpose(down_grad, (0, 2, 1)),
        pair_grad,
        expand_bias_grad,
        jnp.transpose(table_grad, (1, 0, 2)),
        jnp.transpose(vector_grads, (1, 0, 2)),
    )


def solution(mesh):
    return jax.shard_map(
        shards,
        mesh=mesh,
        in_specs=(
            P(("dp", "mp"), None),
            P("dp", None),
            P(("dp", "mp"), None),
            P(),
            P(),
            P(None, None, None, "mp"),
            P(None, None, "mp"),
            P(None, "mp", None),
            P(None, "mp", None),
            P(),
            P(),
            P(),
            P(None, None, "mp"),
            P(None, "mp"),
            P(None, "mp", None),
            P(),
        ),
        out_specs=(
            P(("dp", "mp"), None),
            P(("dp", "mp"), None),
            P(None, "dp", None, "mp"),
            P(None, "mp", "dp"),
            P(None, "dp", "mp"),
            P(None, "mp", "dp"),
            P(None, None, "mp"),
            P(None, "mp"),
            P(None, "mp", None),
            P(),
        ),
        check_vma=False,
    )
```

```python
import jax
import jax.numpy as jnp
import numpy as np
from jax import lax
from jax.experimental import pallas as pl
from jax.experimental.pallas import tpu as pltpu
from jax.sharding import PartitionSpec as P

HEAD_DIM = 32
GRID = 14
WIN = 7
SHIFT = 3
PATCHES = 196
BLOCK = 98
SLOT = 128
KEYS = 112
LANES = 128
SPAN = 2 * WIN - 1
TURN = 256

EPSILON = 1e-05
MASKED = -1e30
F32 = jnp.float32
BF16 = jnp.bfloat16
VMEM_LIMIT = 14 * 1024 * 1024

IN_VMEM = pl.BlockSpec(memory_space=pltpu.VMEM)
IN_SMEM = pl.BlockSpec(memory_space=pltpu.SMEM)
ANYWHERE = pl.BlockSpec(memory_space=pl.ANY)
IN_HBM = pl.BlockSpec(memory_space=pltpu.HBM)


def shape(dims, kind):
    return jax.ShapeDtypeStruct(dims, kind)


def far(dims, kind):
    return pltpu.HBM(dims, kind)


class Saver:
    def __init__(self, held, outs, sems):
        self.held, self.outs, self.sems = held, outs, sems
        self.copies = []

    def put(self, index, value):
        self.held[index][...] = value
        self.start(index)

    def start(self, index):
        copy = pltpu.make_async_copy(self.held[index], self.outs[index], self.sems.at[index])
        copy.start()
        self.copies.append(copy)

    def wait(self):
        for copy in self.copies:
            copy.wait()


class Near:
    def __init__(self, held):
        self.held = held

    def put(self, index, value):
        self.held[index][...] = value

    def get(self, index):
        return self.held[index]

    def start(self, index):
        pass

    def wait(self):
        pass


class Loader:
    def __init__(self, sources, held, sems):
        self.held = held
        self.copies = [
            pltpu.make_async_copy(source, target, sems.at[index])
            for index, (source, target) in enumerate(zip(sources, held))
        ]
        self.waiting = set(range(len(held)))
        for copy in self.copies:
            copy.start()

    def get(self, index):
        if index in self.waiting:
            self.waiting.remove(index)
            self.copies[index].wait()
        return self.held[index]


FETCHED = []
LINE = []
COST = 1.0e9
FAR_LAYERS = ()
PLAN = (
    "ffn_1_other",
    "ffn_1_own",
    "ffn_grads_1",
    "attention_back_1_own",
    "ffn_sum_1",
    "attention_back_1_other",
    "attention_grads_1",
    "ffn_back_0_other",
    "ffn_back_0_own",
    "ffn_grads_0",
    "attention_sum_1",
    "ffn_sum_1",
    "ffn_sum_0",
    "attention_back_0_own",
    "attention_sum_1",
    "attention_back_0_other",
    "attention_grads_0",
    "ffn_sum_1",
    "pack",
    "attention_sum_0",
    "ffn_sum_0",
    "ffn_end_1",
    "attention_sum_0",
    "attention_sum_1",
    "attention_sum_0",
    "tokens_grad",
    "ffn_sum_0",
    "total",
    "attention_end_1",
    "block_output",
    "attention_outputs",
    "total",
    "total",
    "ffn_outputs",
    "unpack",
)
MICROS = {
    "attention_back_1_own": 14.22,
    "attention_back_1_other": 0.06,
    "attention_grads_1": 0.81,
    "ffn_back_0_other": 1.81,
    "ffn_back_0_own": 0.26,
    "ffn_grads_0": 0.1,
    "attention_back_0_own": 0.36,
    "attention_back_0_other": 0.33,
    "attention_grads_0": 0.17,
    "pack": 0.44,
    "ffn_grads_1": 0.3,
}
PIECES = {"ffn": 3, "attention": 2}
BIT_ORDER = {
    "ffn_1": (0, 2, 1, 3),
    "attention_1": (0, 1, 3, 2),
    "ffn_0": (0, 2, 1, 3),
    "attention_0": (0, 1, 2, 3),
    "total": (0, 2, 1, 3),
}


def kernel_call(body, outs, out_specs, ins, in_specs, scratch, name, micros, also=(), limit=None, fetch=()
):
    behind = [item for item in (*LINE, *also) if not any(item is used for used in ins)]
    skipped = len(behind)
    ins = [
        pltpu.with_memory_space_constraint(item, pltpu.HBM) if spec is IN_HBM else item
        for item, spec in zip(ins, in_specs)
    ]
    flat = outs if isinstance(outs, list) else [outs]
    flat_specs = out_specs if isinstance(out_specs, list) else [out_specs]
    count, near_count = len(fetch), len(ins)

    def whole(*refs):
        refs = refs[skipped:]
        own_ins, sources, refs = refs[:near_count], refs[near_count : near_count + count], refs[near_count + count :]
        own_outs, targets, refs = refs[: len(flat)], refs[len(flat) : len(flat) + count], refs[len(flat) + count :]
        copies = []
        if count:
            refs, sems = refs[:-1], refs[-1]
            for index, (_, layer) in enumerate(fetch):
                copy = pltpu.make_async_copy(
                    sources[index].at[layer], targets[index], sems.at[index]
                )
                copy.start()
                copies.append(copy)
        body(*own_ins, *own_outs, *refs)
        for copy in copies:
            copy.wait()

    found = pl.pallas_call(
        whole,
        out_shape=flat + [shape(item.shape[1:], item.dtype) for item, _ in fetch],
        in_specs=[ANYWHERE] * skipped + in_specs + [IN_HBM] * count,
        out_specs=flat_specs + [IN_VMEM] * count,
        scratch_shapes=list(scratch) + ([pltpu.SemaphoreType.DMA((count,))] if count else []),
        compiler_params=pltpu.CompilerParams(vmem_limit_bytes=limit or VMEM_LIMIT),
        cost_estimate=pl.CostEstimate(
            flops=int(micros * COST), bytes_accessed=1024, transcendentals=0
        ),
        name=name,
    )(
        *behind,
        *ins,
        *[pltpu.with_memory_space_constraint(item, pltpu.HBM) for item, _ in fetch],
    )
    near = [item for item, kind in zip(found, flat) if isinstance(kind, jax.ShapeDtypeStruct)]
    if near:
        LINE[:] = [min(near, key=lambda item: item.size)]
    else:
        LINE[:] = [pltpu.with_memory_space_constraint(found[0], pltpu.HBM)]
    if count:
        found, FETCHED[:] = found[: len(flat)], found[len(flat) :]
    return found if isinstance(outs, list) else found[0]


def dot_nn(left, right):
    return lax.dot_general(left, right, (((1,), (0,)), ((), ())), preferred_element_type=F32)


def dot_nt(left, right):
    return lax.dot_general(left, right, (((1,), (1,)), ((), ())), preferred_element_type=F32)


def dot_tn(left, right):
    return lax.dot_general(left, right, (((0,), (0,)), ((), ())), preferred_element_type=F32)


def dot_tt(left, right):
    return lax.dot_general(left, right, (((0,), (1,)), ((), ())), preferred_element_type=F32)


def dot_full(left, right, contracted):
    return lax.dot_general(
        left,
        right,
        (contracted, ((), ())),
        preferred_element_type=F32,
        precision=lax.Precision.HIGHEST,
    )


def place_matrix(layer):
    row = lax.broadcasted_iota(jnp.int32, (2 * SLOT, PATCHES), 0)
    patch = lax.broadcasted_iota(jnp.int32, (2 * SLOT, PATCHES), 1)
    second = row >= SLOT
    within = jnp.where(second, row - SLOT, row)
    found = within + jnp.where(second, BLOCK, 0) + layer * SHIFT * GRID
    found = jnp.where(found >= PATCHES, found - PATCHES, found)
    return jnp.where((within < BLOCK) & (found == patch), 1.0, 0.0).astype(BF16)


def window_matrix(layer, block):
    def groups(place):
        turned_row = (place * 147) >> 11
        col = place - turned_row * GRID
        row = turned_row + block * WIN + layer * SHIFT
        row = jnp.where(row >= GRID, row - GRID, row)

        def group(position):
            moved = position + layer * (WIN - SHIFT)
            return jnp.where(moved >= 2 * WIN, 2, jnp.where(moved >= WIN, 1, 0))

        return group(row) * 4 + group(col)

    key = lax.broadcasted_iota(jnp.int32, (KEYS, LANES), 0)
    query = lax.broadcasted_iota(jnp.int32, (KEYS, LANES), 1)
    return (groups(key) == groups(query)) & (key < BLOCK) & (query < BLOCK)


def offset_matrix():
    offset = lax.broadcasted_iota(jnp.int32, (SPAN * SPAN, TURN), 0)
    lane = lax.broadcasted_iota(jnp.int32, (SPAN * SPAN, TURN), 1)
    row = (offset * 79) >> 10
    place = offset - row * SPAN + row * GRID - (WIN - 1) * (GRID + 1)
    return jnp.where(jnp.where(place < 0, place + TURN, place) == lane, 1.0, 0.0)


def heads_apart(value):
    rows = value.shape[0]
    parts = []
    for member in range(rows // HEAD_DIM):
        start = member * HEAD_DIM
        pieces = [value[start : start + HEAD_DIM]]
        if start:
            pieces.insert(0, jnp.zeros((start, value.shape[1]), value.dtype))
        if start + HEAD_DIM < rows:
            pieces.append(jnp.zeros((rows - start - HEAD_DIM, value.shape[1]), value.dtype))
        parts.append(jnp.concatenate(pieces, axis=0))
    return jnp.concatenate(parts, axis=1)


def heads_together(value):
    count = value.shape[0] // HEAD_DIM
    columns = value.shape[1] // count
    return jnp.concatenate(
        [
            value[
                member * HEAD_DIM : (member + 1) * HEAD_DIM,
                member * columns : (member + 1) * columns,
            ]
            for member in range(count)
        ],
        axis=0,
    )


def norm_rows(stream, gain, shift):
    center = stream - jnp.mean(stream, axis=-1, keepdims=True)
    spread = jnp.mean(center * center, axis=-1, keepdims=True)
    rstd = lax.rsqrt(spread + EPSILON)
    x_hat = center * rstd
    return x_hat, rstd, (x_hat * gain + shift).astype(BF16)


def norm_back(grad_normed, x_hat, rstd, gain):
    scaled = grad_normed * gain
    term = jnp.mean(scaled, axis=-1, keepdims=True)
    along = jnp.mean(scaled * x_hat, axis=-1, keepdims=True)
    return rstd * (scaled - term - x_hat * along)


def column_sum(value):
    return jnp.sum(value, axis=0, keepdims=True)


def put_sums(out, prior, sums):
    for row, found in enumerate(sums):
        out[row : row + 1] = found if prior is None else found + prior[row : row + 1]
    out[len(sums) :] = jnp.zeros((out.shape[0] - len(sums), out.shape[1]), F32)


FIRST_GAIN, FIRST_SHIFT, ATTENTION_BIAS, SECOND_GAIN, SECOND_SHIFT, REDUCE_BIAS = range(6)


def vector_row(vectors, member, layer):
    row = member * (vectors.shape[0] // 6) + layer
    return vectors[row : row + 1]


def head_lanes(rows, member):
    lane = lax.broadcasted_iota(jnp.int32, (rows, LANES), 1)
    return (lane >= member * HEAD_DIM) & (lane < (member + 1) * HEAD_DIM)


def head_rows(value):
    rows = value.shape[0]
    return jnp.concatenate(
        [
            jnp.where(head_lanes(rows, member), value, jnp.zeros_like(value))
            for member in range(LANES // HEAD_DIM)
        ],
        axis=0,
    )


def tables_body(heads, layers, refs):
    half = refs[0]
    in_hbm, refs = refs[1:13], refs[13:]
    biases, refs = refs[:layers], refs[layers:]
    masks, refs = refs[: 2 * layers], refs[2 * layers :]
    keep_out, vectors_out = refs[:2]
    held = [refs[6], refs[7], *refs[2:6], *refs[8:14]]
    sems = refs[14]
    copies = []
    for index, (source, target) in enumerate(zip(in_hbm, held)):
        copies.append(pltpu.make_async_copy(source, target, sems.at[index]))
        copies[-1].start()
    table, keep = held[:2]
    same = lax.broadcasted_iota(jnp.int32, (KEYS, LANES), 0) == lax.broadcasted_iota(
        jnp.int32, (KEYS, LANES), 1
    )
    offsets = offset_matrix()
    per_group = LANES // HEAD_DIM
    for copy in copies:
        copy.wait()
    own_first = half[0] == 0
    rows = [keep[image : image + 1].astype(F32) for image in range(2)]
    pair = jnp.concatenate(
        [jnp.where(own_first, rows[0], rows[1]), jnp.where(own_first, rows[1], rows[0])], axis=0
    ).astype(BF16)
    for layer in range(layers):
        line = dot_full(table[:, layer], offsets, ((1,), (0,)))
        for head in range(heads):
            wide = jnp.broadcast_to(line[head : head + 1], (KEYS, TURN))
            lanes = head % per_group * LANES
            biases[layer][head // per_group, :, lanes : lanes + LANES] = pltpu.roll(
                wide, 0, 1, stride=1, stride_axis=0
            )[:, :LANES]
        place = place_matrix(layer)
        kept = dot_nt(place, pair)
        for block in range(2):
            window = window_matrix(layer, block)
            for image in range(2):
                column = kept[block * SLOT : block * SLOT + KEYS, image : image + 1]
                fine = window & ((column > 0.5) | same)
                masks[layer * 2 + image][block] = jnp.where(fine, 0.0, MASKED)
        if layer == 0:
            keep_out[...] = dot_tn(place, kept.astype(BF16))
    for index, item in enumerate(held[6:]):
        vectors_out[index * layers : (index + 1) * layers] = item[...]


def make_tables(half, position_table, keep_mask, moved, vectors, fetch, also):
    heads, layers, _ = position_table.shape
    groups = heads * HEAD_DIM // LANES
    width = vectors[0].shape[1]
    ins = (position_table, keep_mask, *moved, *vectors)
    outs = [shape((groups, KEYS, 4 * LANES), F32)] * layers + [shape((2, KEYS, LANES), F32)] * (
        2 * layers
    )
    outs += [
        shape((PATCHES, 2), F32),
        shape((len(vectors) * layers, width), F32),
        *[shape(item.shape, item.dtype) for item in moved],
    ]
    found = kernel_call(
        lambda *refs: tables_body(heads, layers, refs),
        outs,
        [IN_VMEM] * len(outs),
        (half, *ins),
        [IN_SMEM] + [IN_HBM] * len(ins),
        [pltpu.VMEM(item.shape, item.dtype) for item in (*ins[:2], *vectors)]
        + [pltpu.SemaphoreType.DMA((len(ins),))],
        "tables",
        1.6,
        also,
        None,
        fetch,
    )
    masks = [found[layers + 2 * layer : layers + 2 * layer + 2] for layer in range(layers)]
    return found[:layers], masks, found[3 * layers :]


def attention_body(layer, heads, chained, refs):
    if chained:
        base, mine, theirs = refs[:3]
        refs = refs[3:]
    else:
        base, refs = refs[0], refs[1:]
    vectors, pair_bias, bias, mask, in_held, out_held = refs[:6]
    refs = refs[6:]
    if chained:
        stream_out, refs = refs[0], refs[1:]
    hat_out, rstd_out, partial_out = refs[1], refs[2], refs[6]
    far_outs = (refs[0], refs[3], refs[4], refs[5])
    turned = refs[7]
    save = Saver(refs[8:12], far_outs, refs[12]) if layer in FAR_LAYERS else Near(far_outs)
    qkv_out, weights_out = save.held[1:3]
    width = heads * HEAD_DIM
    stream = base[...].astype(F32)
    if chained:
        stream = (
            stream
            + (mine[...].astype(F32) + theirs[...].astype(F32))
            + vector_row(vectors, REDUCE_BIAS, layer - 1)
        )
        stream_out[...] = stream
    x_hat, rstd, normed = norm_rows(
        stream, vector_row(vectors, FIRST_GAIN, layer), vector_row(vectors, FIRST_SHIFT, layer)
    )
    save.put(0, normed)
    hat_out[...] = x_hat.astype(BF16)
    rstd_out[...] = rstd
    place = place_matrix(layer)
    parts = []
    for member in range(3):
        mixed = dot_nn(normed, in_held[member])
        if member != 1:
            mixed = mixed + pair_bias[layer, member // 2 : member // 2 + 1]
        parts.append(mixed.astype(BF16))
        qkv_out[:, member * width : (member + 1) * width] = parts[-1]
    save.start(1)
    queries = dot_tt(parts[0], place).astype(BF16)
    keys = dot_nn(place, parts[1]).astype(BF16)
    values = dot_tt(parts[2], place).astype(BF16)
    scale = HEAD_DIM ** (-0.5)
    groups = width // LANES
    for group in range(groups):
        lanes = slice(group * LANES, (group + 1) * LANES)
        for block in range(2):
            slots = slice(block * SLOT, (block + 1) * SLOT)
            own_keys = slice(block * SLOT, block * SLOT + KEYS)
            scores = dot_nn(keys[own_keys, lanes], heads_apart(queries[lanes, slots])) * scale
            scores = scores + bias[group] + jnp.concatenate([mask[block]] * 4, axis=1)
            raised = jnp.exp(scores - jnp.max(scores, axis=0, keepdims=True))
            weights = raised * (1.0 / jnp.sum(raised, axis=0, keepdims=True))
            weights = weights.astype(BF16)
            weights_out[group * 2 + block] = weights
            found = heads_together(dot_nn(values[lanes, own_keys], weights))
            turned[lanes, slots] = found.astype(BF16)
    attended = dot_tt(place, turned[...]).astype(BF16)
    save.start(2)
    save.put(3, attended)
    partial_out[...] = dot_nn(attended, out_held[...]).astype(BF16)
    save.wait()


def attention_forward(layer, streams, vectors, pair_bias, bias, mask, matrix_in, matrix_out, also=(), fetch=(), micros=4):
    chained = len(streams) > 1
    rows, width = streams[0].shape
    head_width = matrix_out.shape[0]
    put = far if layer in FAR_LAYERS else shape
    spec = IN_HBM if layer in FAR_LAYERS else IN_VMEM
    heads = head_width // HEAD_DIM
    saved = [
        (rows, width),
        (rows, 3 * head_width),
        (2 * head_width // LANES, KEYS, 4 * LANES),
        (rows, head_width),
    ]
    outs = [
        put(saved[0], BF16),
        shape((rows, width), BF16),
        shape((rows, 1), F32),
        *[put(dims, BF16) for dims in saved[1:]],
        shape((rows, width), BF16),
    ]
    out_specs = [spec, IN_VMEM, IN_VMEM, spec, spec, spec, IN_VMEM]
    if chained:
        outs = [shape((rows, width), F32)] + outs
        out_specs = [IN_VMEM] + out_specs
    ins = (*streams, vectors, pair_bias, bias, mask, matrix_in, matrix_out)
    found = kernel_call(
        lambda *refs: attention_body(layer, heads, chained, refs),
        outs,
        out_specs,
        ins,
        [IN_VMEM] * len(ins),
        [pltpu.VMEM((head_width, 2 * SLOT), BF16)]
        + (
            [*[pltpu.VMEM(dims, BF16) for dims in saved], pltpu.SemaphoreType.DMA((4,))]
            if layer in FAR_LAYERS
            else []
        ),
        f"attention_{layer}",
        micros,
        also,
        None,
        fetch,
    )
    return found if chained else [streams[0], *found]


def gelu_parts(hidden):
    below = 0.5 * (1.0 + lax.erf(hidden * (0.5**0.5)))
    density = jnp.exp(-0.5 * hidden * hidden) * (0.5 / np.pi) ** 0.5
    return hidden * below, below + hidden * density


def ffn_body(layer, both, image, joined, step, refs):
    base, mine, theirs, vectors, up_bias = refs[:5]
    refs = refs[5:]
    if both:
        grad, keep, refs = refs[0], refs[1], refs[2:]
    if joined:
        prior_sums, refs = refs[0], refs[1:]
    up_held, down_held, *refs = refs
    mid_out, hat_out, rstd_out, partial_out = refs[0], refs[2], refs[3], refs[6]
    far_outs = (refs[1], refs[4], refs[5])
    if both:
        back_out, sums_out, grad_out = refs[7:10]
    held = refs[7:]
    save = Saver(held[:3], far_outs, held[3]) if layer in FAR_LAYERS else Near(far_outs)
    active_out, slope_out = save.held[1:]
    mid = (
        base[...].astype(F32)
        + (mine[...].astype(F32) + theirs[...].astype(F32))
        + vector_row(vectors, ATTENTION_BIAS, layer)
    )
    mid_out[...] = mid
    x_hat, rstd, normed = norm_rows(
        mid, vector_row(vectors, SECOND_GAIN, layer), vector_row(vectors, SECOND_SHIFT, layer)
    )
    save.put(0, normed)
    hat_out[...] = x_hat.astype(BF16)
    rstd_out[...] = rstd
    if both:
        grad_rows = (grad[...].astype(F32) * keep[:, image : image + 1]).astype(BF16)
        grad_out[...] = grad_rows
        put_sums(sums_out, prior_sums if joined else None, [column_sum(grad_rows.astype(F32))])
    forward, backward = None, None
    for start in range(0, up_held.shape[1], step):
        part = slice(start, start + step)
        hidden = dot_nn(normed, up_held[:, part]) + up_bias[layer : layer + 1, part]
        active, slope = gelu_parts(hidden)
        active = active.astype(BF16)
        active_out[:, part] = active
        term = dot_nn(active, down_held[part])
        forward = term if forward is None else forward + term
        if both:
            grad_hidden = (slope * dot_nt(grad_rows, down_held[part])).astype(BF16)
            slope_out[:, part] = grad_hidden
            term = dot_nt(grad_hidden, up_held[:, part])
            backward = term if backward is None else backward + term
        else:
            slope_out[:, part] = slope.astype(BF16)
    save.start(1)
    save.start(2)
    partial_out[...] = forward.astype(BF16)
    if both:
        back_out[...] = backward.astype(BF16)
    save.wait()


def ffn_forward(layer, image, streams, vectors, up_bias, up, down, grad=None, keep=None, prior_sums=None, fetch=(), also=()):
    rows, width = streams[0].shape
    units = up.shape[1]
    both = grad is not None
    put = far if layer in FAR_LAYERS else shape
    saved = [(rows, width), (rows, units), (rows, units)]
    outs = [
        shape((rows, width), F32),
        put(saved[0], BF16),
        shape((rows, width), BF16),
        shape((rows, 1), F32),
        put(saved[1], BF16),
        put(saved[2], BF16),
        shape((rows, width), BF16),
    ]
    ins = [*streams, vectors, up_bias]
    if both:
        outs += [shape((rows, width), BF16), shape((8, width), F32), shape((rows, width), BF16)]
        ins += [grad, keep]
    joined = prior_sums is not None
    if joined:
        ins.append(prior_sums)
    specs = [IN_VMEM] * (len(ins) + 2)
    return kernel_call(
        lambda *refs: ffn_body(layer, both, image, joined, units // 3, refs),
        outs,
        [IN_VMEM if put is shape or index not in (1, 4, 5) else IN_HBM for index in range(len(outs))],
        (*ins, up, down),
        specs,
        []
        if put is shape
        else [*[pltpu.VMEM(dims, BF16) for dims in saved], pltpu.SemaphoreType.DMA((3,))],
        f"ffn_both_{layer}" if both else f"ffn_{layer}",
        4.6 if both else 3,
        also,
        None,
        fetch,
    )


def ffn_back_body(layer, joined, step, refs):
    base, mine, theirs, hat, rstd, vectors = refs[:6]
    refs = refs[6:]
    if joined:
        prior_sums, refs = refs[0], refs[1:]
    slope_hbm, up_held, down_held = refs[:3]
    grad_out, low_out, hidden_out, partial_out, sums_out = refs[3:8]
    slope, load = slope_hbm, Near([slope_hbm])
    if layer in FAR_LAYERS:
        slope = refs[8]
        load = Loader([slope_hbm], [slope], refs[9])
    grad_normed = mine[...].astype(F32) + theirs[...].astype(F32)
    x_hat = hat[...].astype(F32)
    grad = base[...] + norm_back(
        grad_normed, x_hat, rstd[...], vector_row(vectors, FIRST_GAIN, layer + 1)
    )
    grad_out[...] = grad
    low = grad.astype(BF16)
    low_out[...] = low
    sums = [column_sum(grad_normed * x_hat), column_sum(grad_normed), column_sum(grad)]
    put_sums(sums_out, prior_sums if joined else None, sums)
    backward = None
    load.get(0)
    for start in range(0, up_held.shape[1], step):
        part = slice(start, start + step)
        grad_hidden = (slope[:, part].astype(F32) * dot_nt(low, down_held[part])).astype(BF16)
        hidden_out[:, part] = grad_hidden
        term = dot_nt(grad_hidden, up_held[:, part])
        backward = term if backward is None else backward + term
    partial_out[...] = backward.astype(BF16)


def ffn_backward(layer, grads, hat, rstd, vectors, slope, up, down, prior_sums=None, micros=4, fetch=()):
    rows, width = grads[0].shape
    units = up.shape[1]
    outs = [
        shape((rows, width), F32),
        shape((rows, width), BF16),
        shape((rows, units), BF16),
        shape((rows, width), BF16),
        shape((8, width), F32),
    ]
    ins = [*grads, hat, rstd, vectors]
    joined = prior_sums is not None
    if joined:
        ins.append(prior_sums)
    return kernel_call(
        lambda *refs: ffn_back_body(layer, joined, units // 3, refs),
        outs,
        [IN_VMEM] * 5,
        (*ins, slope, up, down),
        [IN_VMEM] * len(ins) + [IN_HBM if layer in FAR_LAYERS else IN_VMEM] + [IN_VMEM] * 2,
        [pltpu.VMEM((rows, units), BF16), pltpu.SemaphoreType.DMA((1,))]
        if layer in FAR_LAYERS
        else [],
        f"ffn_back_{layer}",
        micros,
        (),
        None,
        fetch,
    )


def attention_back_body(layer, heads, joined, refs):
    base, mine, theirs, hat, rstd, vectors, first_hat = refs[:7]
    refs = refs[7:]
    if joined:
        prior_sums, prior_table = refs[:2]
        refs = refs[2:]
    qkv, weights, in_held, out_held = refs[:4]
    grad_out, low_out, mixed_out, partial_out, sums_out, table_out = refs[4:10]
    turned, merged, diagonals = refs[10:13]
    load = Near([qkv, weights])
    if layer in FAR_LAYERS:
        load = Loader([qkv, weights], refs[13:15], refs[15])
        qkv, weights = refs[13:15]
    width = heads * HEAD_DIM
    per_group = LANES // HEAD_DIM
    grad_normed = mine[...].astype(F32) + theirs[...].astype(F32)
    x_hat = hat[...].astype(F32)
    grad = base[...].astype(F32) + norm_back(
        grad_normed, x_hat, rstd[...], vector_row(vectors, SECOND_GAIN, layer)
    )
    grad_out[...] = grad
    low = grad.astype(BF16)
    low_out[...] = low
    sums = [column_sum(grad_normed * x_hat), column_sum(grad_normed), column_sum(grad)]
    place = place_matrix(layer)
    load.get(0)
    queries = dot_nn(place, qkv[:, :width]).astype(BF16)
    turned_keys = dot_tt(qkv[:, width : 2 * width], place).astype(BF16)
    values = dot_nn(place, qkv[:, 2 * width :]).astype(BF16)
    grad_attended = dot_nt(low, out_held[...]).astype(BF16)
    grad_slots = dot_nn(place, grad_attended).astype(BF16)
    grad_turned = dot_tt(grad_attended, place).astype(BF16)
    load.get(1)
    scale = HEAD_DIM ** (-0.5)
    empty = jnp.zeros((SLOT - KEYS, LANES), BF16)
    for group in range(width // LANES):
        lanes = slice(group * LANES, (group + 1) * LANES)
        total = None
        for block in range(2):
            top_row = block * SLOT
            slots = slice(top_row, top_row + SLOT)
            own_keys = slice(top_row, top_row + KEYS)
            low_weights = weights[group * 2 + block]
            full = low_weights.astype(F32)
            grad_weights = dot_nn(values[own_keys, lanes], heads_apart(grad_turned[lanes, slots]))
            spread = jnp.sum(full * grad_weights, axis=0, keepdims=True)
            grad_scores = full * (grad_weights - spread)
            total = grad_scores if total is None else total + grad_scores
            grad_raw = (grad_scores * scale).astype(BF16)
            grad_query = heads_together(dot_nn(turned_keys[lanes, own_keys], grad_raw))
            grad_key = dot_nn(grad_raw, head_rows(queries[slots, lanes]))
            grad_value = dot_nn(low_weights, head_rows(grad_slots[slots, lanes]))
            turned[lanes, slots] = grad_query.astype(BF16)
            for at, found in ((0, grad_key), (width, grad_value)):
                columns = slice(at + group * LANES, at + (group + 1) * LANES)
                merged[own_keys, columns] = found.astype(BF16)
                merged[top_row + KEYS : top_row + SLOT, columns] = empty
        for member in range(per_group):
            head = group * per_group + member
            own = total[:, member * LANES : (member + 1) * LANES]
            wide = jnp.concatenate([own, jnp.zeros_like(own)], axis=1)
            line = None
            for start in range(0, KEYS, 8):
                rows = wide[start : start + 8]
                if start:
                    rows = pltpu.roll(rows, TURN - start, 1)
                line = rows if line is None else line + rows
            diagonals[head * 8 : head * 8 + 8] = line
    mixed = [dot_tt(place, turned[...]).astype(BF16)]
    both = dot_tn(place, merged[...]).astype(BF16)
    mixed += [both[:, :width], both[:, width:]]
    mixed_out[:, :width] = mixed[0]
    mixed_out[:, width:] = both
    partial = dot_nt(mixed[0], in_held[0])
    partial = partial + dot_nt(mixed[1], in_held[1])
    partial = partial + dot_nt(mixed[2], in_held[2])
    partial_out[...] = partial.astype(BF16)
    sums += [column_sum(partial * first_hat[...].astype(F32)), column_sum(partial)]
    put_sums(sums_out, prior_sums if joined else None, sums)
    lines = diagonals[...]
    row = lax.broadcasted_iota(jnp.int32, lines.shape, 0)
    for bit in range(3):
        moved = pltpu.roll(lines, TURN - (1 << bit), 1)
        lines = jnp.where(((row >> bit) & 1) == 1, moved, lines)
    lines = jnp.sum(lines.reshape(heads, 8, TURN), axis=1)
    table = dot_full(lines, offset_matrix(), ((1,), (1,)))
    table_out[...] = table + prior_table[...] if joined else table


def attention_backward(
    layer, grads, hat, rstd, vectors, first_hat, qkv, weights, matrix_in, matrix_out,
    prior=(), micros=5, fetch=(),
):
    rows, width = grads[0].shape
    head_width = matrix_out.shape[0]
    heads = head_width // HEAD_DIM
    outs = [
        shape((rows, width), F32),
        shape((rows, width), BF16),
        shape((rows, 3 * head_width), BF16),
        shape((rows, width), BF16),
        shape((8, width), F32),
        shape((heads, SPAN * SPAN), F32),
    ]
    ins = (*grads, hat, rstd, vectors, first_hat, *prior)
    return kernel_call(
        lambda *refs: attention_back_body(layer, heads, bool(prior), refs),
        outs,
        [IN_VMEM] * 6,
        (*ins, qkv, weights, matrix_in, matrix_out),
        [IN_VMEM] * len(ins) + [IN_HBM if layer in FAR_LAYERS else IN_VMEM] * 2 + [IN_VMEM] * 2,
        [
            pltpu.VMEM((head_width, 2 * SLOT), BF16),
            pltpu.VMEM((2 * SLOT, 2 * head_width), BF16),
            pltpu.VMEM((heads * 8, TURN), F32),
        ]
        + (
            [
                pltpu.VMEM(qkv.shape, BF16),
                pltpu.VMEM(weights.shape, BF16),
                pltpu.SemaphoreType.DMA((2,)),
            ]
            if layer in FAR_LAYERS
            else []
        ),
        f"attention_back_{layer}",
        micros,
        (),
        None,
        fetch,
    )


def finish_body(base, mine, theirs, hat, rstd, vectors, out):
    grad_normed = mine[...].astype(F32) + theirs[...].astype(F32)
    out[...] = base[...] + norm_back(
        grad_normed, hat[...].astype(F32), rstd[...], vector_row(vectors, FIRST_GAIN, 0)
    )


def output_body(layer, base, mine, theirs, vectors, out):
    total = base[...] + (mine[...].astype(F32) + theirs[...].astype(F32))
    out[...] = (total + vector_row(vectors, REDUCE_BIAS, layer)).astype(BF16)


def finish(body, kind, name, micros, *ins):
    return kernel_call(
        body, pltpu.HBM(ins[0].shape, kind), IN_VMEM, ins, [IN_VMEM] * len(ins), [], name, micros
    )


def group_place(group, top, order):
    place = 0
    for step, bit in enumerate(order):
        place = place + ((((group >> bit) & 1) ^ ((top >> bit) & 1)) << (len(order) - 1 - step))
    return place


def grads_body(pairs, groups, order, step, summed, far_ins, refs):
    top = refs[0][0]
    lefts = 1 + max(left for left, _ in pairs)
    rights = len(pairs)
    refs = refs[1:]
    total = 2 * (lefts + rights)
    sources, refs = refs[:total], refs[total:]
    held_ins = list(sources)
    far_count = sum(far_ins)
    if far_count:
        scratch, sems, refs = refs[-far_count - 1 : -1], refs[-1], refs[: -far_count - 1]
        loader = Loader([item for item, is_far in zip(sources, far_ins) if is_far], scratch, sems)
        places = [index for index, is_far in enumerate(far_ins) if is_far]

    def get(index):
        return loader.get(places.index(index)) if far_ins[index] else held_ins[index]

    keep_out, sums_out, held, turned, wide, sems = (refs[0], *refs[-5:])
    send_outs = refs[1:-5]
    rows = sources[0].shape[0]
    space = wide.shape[0] // 2
    empty = space - rows
    block = keep_out.shape[1]
    copies = []
    for left in range(lefts):
        for image in range(2):
            start = image * space
            turned[left, :, start + LANES : start + space] = jnp.zeros(
                (turned.shape[1], space - LANES), BF16
            )
            turned[left, :, start : start + rows] = get(2 * left + image)[...].T
    at = 0
    sum_at = 0
    for right, (left, _) in enumerate(pairs):
        columns = sources[2 * (lefts + right)].shape[1]
        for image in range(2):
            start = image * space
            wide[start : start + rows, :columns] = get(2 * (lefts + right) + image)[...]
            wide[start + rows : start + space, :columns] = jnp.zeros((empty, columns), BF16)
        if summed[right]:
            sums_out[0:1, sum_at : sum_at + columns] = column_sum(wide[:, :columns].astype(F32))
            sum_at += columns
        for first in range(0, columns, step):
            found = dot_nn(turned[left], wide[:, first : first + step]).astype(BF16)
            for group in range(groups):
                held[group_place(group, top, order), :, at : at + step] = found[
                    group * block : (group + 1) * block
                ]
            sent = at // send_outs[0].shape[2]
            inner = at - sent * send_outs[0].shape[2]
            for half, out in (
                (0, keep_out.at[:, :, at : at + step]),
                (1, send_outs[sent].at[:, :, inner : inner + step]),
            ):
                copy = pltpu.make_async_copy(
                    held.at[half * groups // 2 : (half + 1) * groups // 2, :, at : at + step],
                    out,
                    sems.at[half, at // step],
                )
                copy.start()
                copies.append(copy)
            at += step
    for copy in copies:
        copy.wait()


def weight_grads(top, groups, order, pairs, lefts, rights, summed, pieces, far_ins, name, micros):
    width = lefts[0].shape[1]
    step = 512 if all(item.shape[1] % 512 == 0 for item in rights) else 384
    columns = sum(item.shape[1] for item in rights[::2])
    widest = max(item.shape[1] for item in rights)
    space = 2 * LANES
    summed_columns = sum(item.shape[1] for item, used in zip(rights[::2], summed) if used)
    outs = [
        shape((groups // 2, width // groups, columns), BF16),
        *[shape((groups // 2, width // groups, columns // pieces), BF16)] * pieces,
        shape((8, summed_columns), F32),
    ]
    count = 1 + max(left for left, _ in pairs)
    kept, *sent, sums = kernel_call(
        lambda *refs: grads_body(pairs, groups, order, step, summed, far_ins, refs),
        outs,
        [ANYWHERE] * (1 + pieces) + [IN_VMEM],
        (top, *lefts, *rights),
        [IN_SMEM] + [IN_HBM if is_far else IN_VMEM for is_far in far_ins],
        [
            pltpu.VMEM((groups, width // groups, columns), BF16),
            pltpu.VMEM((count, width, 2 * space), BF16),
            pltpu.VMEM((2 * space, widest), BF16),
            pltpu.SemaphoreType.DMA((2, columns // step)),
            *[
                pltpu.VMEM(item.shape, item.dtype)
                for item, is_far in zip((*lefts, *rights), far_ins)
                if is_far
            ],
            *([pltpu.SemaphoreType.DMA((sum(far_ins),))] if any(far_ins) else []),
        ],
        name,
        micros,
        (),
        20 * 1024 * 1024,
    )
    return kept, sent, sums


def swap(value):
    return lax.ppermute(value, "mp", [(0, 1), (1, 0)])


def trade(value, bit, size):
    return lax.ppermute(value, "dp", [(source, source ^ bit) for source in range(size)])


def fold_body(kept, *refs):
    *pieces, keep_out, send_out = refs
    half = keep_out.shape[0]
    at = 0
    for found in pieces:
        columns = slice(at, at + found.shape[2])
        at += found.shape[2]
        for start, out in ((0, keep_out), (half, send_out)):
            for block in range(half):
                total = kept[start + block, :, columns].astype(F32) + found[start + block].astype(F32)
                out[block, :, columns] = total.astype(BF16)


def fold(kept, found, name):
    half = shape((kept.shape[0] // 2, *kept.shape[1:]), BF16)
    return kernel_call(
        fold_body, [half, half], [IN_VMEM] * 2, (kept, *found), [IN_VMEM] * (1 + len(found)), [],
        name, 0.1,
    )


class Scatter:
    def __init__(self, kept, sent, order, size, name):
        self.kept, self.sent, self.order, self.size, self.name = kept, sent, order, size, name
        self.finer = size >> len(order)
        self.level = 0
        self.send()

    def send(self):
        self.found = [
            trade(item, self.finer << self.order[self.level], self.size) for item in self.sent
        ]

    def step(self):
        if self.level + 1 < len(self.order):
            self.kept, sent = fold(self.kept, self.found, f"{self.name}_{self.level}")
            self.sent = [sent]
            self.level += 1
            self.send()

    def finish(self):
        for _ in self.order:
            self.step()
        kept, finer = self.kept, self.finer
        found = jnp.concatenate(self.found, axis=2) if len(self.found) > 1 else self.found[0]
        rank = lax.axis_index("dp")
        while finer > 1:
            finer //= 2
            held = (kept.astype(F32) + found.astype(F32)).astype(BF16)
            halves = held.reshape((2, 1, held.shape[1] // 2, held.shape[2]))
            mine = (rank // finer) % 2
            kept = lax.dynamic_index_in_dim(halves, mine, 0, keepdims=False)
            found = trade(lax.dynamic_index_in_dim(halves, 1 - mine, 0, keepdims=False), finer, self.size)
        return kept, found

    def join(self):
        kept, found = self.finish()
        return (
            kernel_call(
                add_body, shape(kept.shape, F32), IN_VMEM, (kept, found), [IN_VMEM] * 2, [],
                f"{self.name}_end", 0.1,
            ),
        )


def add_body(left, right, out):
    out[...] = left[...].astype(F32) + right[...].astype(F32)


def some_bits(name, size):
    bits = range(size.bit_length() - 1)
    listed = [bit for bit in BIT_ORDER[name] if bit in bits]
    return tuple(listed + [bit for bit in bits if bit not in listed])


class Total:
    def __init__(self, value, size):
        self.value, self.size = value, size
        self.left = [1 << bit for bit in some_bits("total", size)]
        self.send()

    def send(self):
        self.found = trade(self.value, self.left.pop(0), self.size)

    def step(self):
        if self.left:
            self.value = kernel_call(
                add_body, shape(self.value.shape, F32), IN_VMEM, (self.value, self.found),
                [IN_VMEM] * 2, [], "total", 0.1,
            )
            self.send()

    def finish(self):
        while self.left:
            self.step()
        return self.value, self.found


def collect_body(counts, widths, refs):
    outs = refs[sum(counts) :]
    for layer, count in enumerate(counts):
        total = refs[0][0].astype(F32)
        if count == 2:
            total = total + refs[1][0].astype(F32)
        refs = refs[count:]
        at = 0
        for out, parts in zip(outs, widths):
            for part in range(parts):
                columns = out.shape[-1]
                if len(out.shape) == 4:
                    out[layer, part] = total[:, at : at + columns]
                else:
                    out[layer] = total[:, at : at + columns]
                at += columns


def collect(pairs, shapes, name):
    flat = [item for pair in pairs for item in pair]
    counts = [len(pair) for pair in pairs]
    return kernel_call(
        lambda *refs: collect_body(
            counts, [dims[1] if len(dims) == 4 else 1 for dims in shapes], refs
        ),
        [pltpu.HBM(dims, F32) for dims in shapes],
        [IN_VMEM] * len(shapes),
        flat,
        [IN_VMEM] * len(flat),
        [],
        name,
        0.1,
    )


def pack_body(width, layers, refs):
    sums_0, theirs_0, sums_low, sums_1, last = refs[:5]
    ups, mixes, tables = refs[5 : 5 + layers], refs[5 + layers : 5 + 2 * layers], refs[5 + 2 * layers : -1]
    out = refs[-1]
    out[...] = jnp.zeros(out.shape, F32)
    out[0:2] = sums_0[3:5] + theirs_0[3:5]
    out[2:3] = sums_0[2:3]
    out[3:5] = sums_0[0:2]
    out[5:6] = sums_low[2:3]
    out[6:8] = sums_low[0:2]
    out[8:9] = sums_1[2:3]
    out[9:11] = sums_1[0:2]
    out[11:12] = last[0:1]
    row = 6 * layers
    for item in ups:
        for start in range(0, item.shape[1], width):
            out[row : row + 1] = item[0:1, start : start + width]
            row += 1
    third = mixes[0].shape[1] // 3
    for item in mixes:
        out[row : row + 1, :third] = item[0:1, :third]
        out[row : row + 1, third : 2 * third] = item[0:1, 2 * third :]
        row += 1
    for item in tables:
        heads, offsets = item.shape
        for head in range(heads):
            lane = head * TURN % width
            out[row : row + 1, lane : lane + offsets] = item[head : head + 1]
            if (head + 1) * TURN % width == 0:
                row += 1


def unpack_body(refs):
    packed, found, vectors, up_bias, pair_bias, tables = refs
    width = packed.shape[1]
    layers, units = up_bias.shape
    total = packed[...] + found[...]
    for layer in range(layers):
        for member in range(6):
            vectors[member, layer : layer + 1] = total[6 * layer + member : 6 * layer + member + 1]
    row = 6 * layers
    for layer in range(layers):
        for start in range(0, units, width):
            up_bias[layer : layer + 1, start : start + width] = total[row : row + 1]
            row += 1
    third = pair_bias.shape[2]
    for layer in range(layers):
        for member in range(2):
            pair_bias[layer, member : member + 1] = total[
                row : row + 1, member * third : (member + 1) * third
            ]
        row += 1
    heads, _, offsets = tables.shape
    for layer in range(layers):
        for head in range(heads):
            lane = head * TURN % width
            tables[head, layer : layer + 1] = total[row : row + 1, lane : lane + offsets]
            if (head + 1) * TURN % width == 0:
                row += 1


def shards(
    tokens,
    keep_mask,
    cotangent,
    first_gain,
    first_shift,
    attention_in,
    query_value_bias,
    position_table,
    attention_out,
    attention_bias,
    second_gain,
    second_shift,
    expand_weight,
    expand_bias,
    reduce_weight,
    reduce_bias,
):
    LINE.clear()
    FETCHED.clear()
    size = lax.axis_size("dp")
    half = lax.axis_index("mp")
    groups = min(16, size)
    top = (lax.axis_index("dp") // (size // groups)).astype(jnp.int32).reshape(1)
    layers, width = first_gain.shape
    head_width = attention_out.shape[1]
    units = expand_weight.shape[2]
    heads = head_width // HEAD_DIM
    matrix_in = jnp.transpose(attention_in, (0, 2, 1, 3))
    own_half = half.astype(jnp.int32).reshape(1)
    other_tokens = swap(tokens)
    other_cotangent = swap(cotangent)
    bias, masks, (keep_columns, vectors, tokens, cotangent, up_bias, pair_bias) = make_tables(
        own_half, jnp.transpose(position_table, (1, 0, 2)), keep_mask,
        (tokens, cotangent, expand_bias, query_value_bias),
        (first_gain, first_shift, attention_bias, second_gain, second_shift, reduce_bias),
        ((matrix_in, 0), (attention_out, 0)), (top,),
    )
    heads_held = list(FETCHED)
    def attend(layer, image, streams, also=(), fetch=(), micros=4):
        return attention_forward(
            layer, streams, vectors, pair_bias, bias[layer], masks[layer][image], *heads_held,
            also, fetch, micros,
        )

    def feed(layer, image, streams, grad=None, prior_sums=None, fetch=(), also=()):
        return ffn_forward(
            layer, image, streams, vectors, up_bias, *units_held, grad, keep_columns, prior_sums,
            fetch, also,
        )

    att, ffn = [[None, None], [None, None]], [[None, None], [None, None]]
    att[0][0] = attend(0, 0, (tokens,), micros=0.3)
    sent_own = swap(att[0][0][7])
    att[0][1] = attend(
        0, 1, (other_tokens,), (), ((expand_weight, 0), (reduce_weight, 0))
    )
    units_held = list(FETCHED)
    sent_other = swap(att[0][1][7])
    ffn[0][1] = feed(
        0, 1, (att[0][1][0], att[0][1][7], sent_own), also=(other_cotangent,),
        fetch=((matrix_in, 1), (attention_out, 1)),
    )
    heads_held = list(FETCHED)
    sent_2 = swap(ffn[0][1][6])
    ffn[0][0] = feed(0, 0, (att[0][0][0], att[0][0][7], sent_other))
    sent_1 = swap(ffn[0][0][6])
    att[1][0] = attend(1, 0, (ffn[0][0][0], ffn[0][0][6], sent_2))
    sent_own = swap(att[1][0][7])
    att[1][1] = attend(
        1, 1, (ffn[0][1][0], ffn[0][1][6], sent_1), (), ((expand_weight, 1), (reduce_weight, 1))
    )
    units_held = list(FETCHED)
    sent_other = swap(att[1][1][7])

    far_ins = (True, True, False, False, False, False, True, True)

    def ffn_grads(layer, low, hidden, name):
        normed = [ffn[layer][image][1] for image in range(2)]
        active = [ffn[layer][image][4] for image in range(2)]
        order = some_bits(f"ffn_{layer}", groups)
        kept, sent, sums = weight_grads(
            top, groups, order, ((0, 0), (1, 1)), (*normed, *low), (*hidden, *active),
            (True, False), PIECES["ffn"], far_ins if layer in FAR_LAYERS else (False,) * 8, name, MICROS[name],
        )
        return Scatter(kept, sent, order, size, f"ffn_fold_{layer}"), sums

    def attention_grads(layer, low, mixed, name):
        normed = [att[layer][image][1] for image in range(2)]
        attended = [att[layer][image][6] for image in range(2)]
        order = some_bits(f"attention_{layer}", groups)
        kept, sent, sums = weight_grads(
            top, groups, order, ((0, 0), (1, 1)), (*normed, *low), (*mixed, *attended),
            (True, False), PIECES["attention"], far_ins if layer in FAR_LAYERS else (False,) * 8, name, MICROS[name],
        )
        return Scatter(kept, sent, order, size, f"attention_fold_{layer}"), sums

    def attend_back(layer, image, grads, prior=(), micros=5, fetch=()):
        held = att[layer][image]
        return attention_backward(
            layer, grads, ffn[layer][image][2], ffn[layer][image][3], vectors, held[2],
            held[4], held[5], *later["heads"], prior, micros, fetch,
        )

    def feed_back(image, grads, prior_sums=None, micros=4, fetch=()):
        held = att[1][image]
        return ffn_backward(
            0, grads, held[2], held[3], vectors, ffn[0][image][5], *later["units"],
            prior_sums, micros, fetch,
        )

    back, low = [[None, None], [None, None]], [None, None]
    later = {"heads": heads_held, "units": None}
    sent, sums, extra, outs = {}, {}, {}, {}
    rows = width // size

    def ffn_1_other():
        ffn[1][1] = feed(1, 1, (att[1][1][0], att[1][1][7], sent_own), other_cotangent)
        sent["ffn_1_other"] = swap(ffn[1][1][7])
        sent["block"] = swap(ffn[1][1][6])

    def ffn_1_own():
        ffn[1][0] = feed(1, 0, (att[1][0][0], att[1][0][7], sent_other), cotangent, ffn[1][1][8])
        sent["ffn_1_own"] = swap(ffn[1][0][7])

    def ffn_grads_1():
        sums["ffn_sum_1"], extra["up_1"] = ffn_grads(
            1, (ffn[1][0][9], ffn[1][1][9]), (ffn[1][0][5], ffn[1][1][5]), "ffn_grads_1"
        )

    def attention_back_1_own():
        back[1][0] = attend_back(
            1, 0, (ffn[1][0][9], ffn[1][0][7], sent["ffn_1_other"]), (),
            MICROS["attention_back_1_own"], ((expand_weight, 0), (reduce_weight, 0)),
        )
        later["units"] = list(FETCHED)
        sent["back_1_own"] = swap(back[1][0][3])

    def attention_back_1_other():
        back[1][1] = attend_back(
            1, 1, (ffn[1][1][9], ffn[1][1][7], sent["ffn_1_own"]), back[1][0][4:6],
            MICROS["attention_back_1_other"],
        )
        sent["back_1_other"] = swap(back[1][1][3])

    def attention_grads_1():
        sums["attention_sum_1"], extra["mixed_1"] = attention_grads(
            1, (back[1][0][1], back[1][1][1]), (back[1][0][2], back[1][1][2]), "attention_grads_1"
        )

    def ffn_back_0_other():
        low[1] = feed_back(
            1, (back[1][1][0], back[1][1][3], sent["back_1_own"]), None,
            MICROS["ffn_back_0_other"], ((matrix_in, 0), (attention_out, 0)),
        )
        later["heads"] = list(FETCHED)
        sent["low_other"] = swap(low[1][3])

    def ffn_back_0_own():
        low[0] = feed_back(
            0, (back[1][0][0], back[1][0][3], sent["back_1_other"]), low[1][4],
            MICROS["ffn_back_0_own"],
        )
        sent["low_own"] = swap(low[0][3])

    def ffn_grads_0():
        sums["ffn_sum_0"], extra["up_0"] = ffn_grads(
            0, (low[0][1], low[1][1]), (low[0][2], low[1][2]), "ffn_grads_0"
        )

    def attention_back_0_own():
        back[0][0] = attend_back(
            0, 0, (low[0][0], low[0][3], sent["low_other"]), (), MICROS["attention_back_0_own"]
        )

    def attention_back_0_other():
        back[0][1] = attend_back(
            0, 1, (low[1][0], low[1][3], sent["low_own"]), back[0][0][4:6],
            MICROS["attention_back_0_other"],
        )
        sent["last"] = swap(back[0][1][3])
        sent["sums"] = swap(back[0][1][4])

    def attention_grads_0():
        sums["attention_sum_0"], extra["mixed_0"] = attention_grads(
            0, (back[0][0][1], back[0][1][1]), (back[0][0][2], back[0][1][2]), "attention_grads_0"
        )

    def pack():
        pieces = (
            back[0][1][4], sent["sums"], low[0][4], back[1][1][4], ffn[1][0][8],
            extra["up_0"], extra["up_1"], extra["mixed_0"], extra["mixed_1"],
            back[0][1][5], back[1][1][5],
        )
        per_row = width // TURN
        count = layers * (6 + units // width + 1 + heads // per_row)
        packed = kernel_call(
            lambda *refs: pack_body(width, layers, refs),
            shape((-(-count // 8) * 8, width), F32),
            IN_VMEM,
            pieces,
            [IN_VMEM] * len(pieces),
            [],
            "pack",
            MICROS["pack"],
        )
        sums["total"] = Total(packed, size)

    def unpack():
        outs["small"] = kernel_call(
            lambda *refs: unpack_body(refs),
            [
                shape((6, layers, width), F32),
                shape((layers, units), F32),
                shape((layers, 2, head_width), F32),
                shape((heads, layers, SPAN * SPAN), F32),
            ],
            [IN_VMEM] * 4,
            sums["total"].finish(),
            [IN_VMEM] * 2,
            [],
            "unpack",
            0.1,
        )

    def tokens_grad():
        outs["tokens_grad"] = finish(
            finish_body, F32, "finish", 0.1,
            back[0][0][0], back[0][0][3], sent["last"], att[0][0][2], att[0][0][3], vectors,
        )

    def block_output():
        outs["block_output"] = finish(
            lambda *refs: output_body(1, *refs), BF16, "output", 0.1,
            ffn[1][0][0], ffn[1][0][6], sent["block"], vectors,
        )

    def attention_end_1():
        extra["attention_1"] = sums["attention_sum_1"].join()

    def ffn_end_1():
        extra["ffn_1"] = sums["ffn_sum_1"].join()

    def attention_outputs():
        outs["attention"] = collect(
            (sums["attention_sum_0"].finish(), extra["attention_1"]),
            [(layers, 3, rows, head_width), (layers, rows, head_width)],
            "attention_collect",
        )

    def ffn_outputs():
        outs["ffn"] = collect(
            (sums["ffn_sum_0"].finish(), extra["ffn_1"]), [(layers, rows, units)] * 2, "ffn_collect"
        )

    steps = {
        item.__name__: item
        for item in (
            ffn_1_other, ffn_1_own, ffn_grads_1, attention_back_1_own, attention_back_1_other,
            attention_grads_1, ffn_back_0_other, ffn_back_0_own, ffn_grads_0,
            attention_back_0_own, attention_back_0_other, attention_grads_0, pack, unpack,
            tokens_grad, block_output, attention_end_1, ffn_end_1, attention_outputs, ffn_outputs,
        )
    }
    for name in PLAN:
        if name in steps:
            steps[name]()
        else:
            sums[name].step()

    in_grad, out_grad = outs["attention"]
    up_grad, down_grad = outs["ffn"]
    vector_grads, expand_bias_grad, pair_grad, table_grad = outs["small"]
    return (
        outs["block_output"],
        outs["tokens_grad"],
        jnp.transpose(in_grad, (0, 2, 1, 3)),
        jnp.transpose(out_grad, (0, 2, 1)),
        up_grad,
        jnp.transpose(down_grad, (0, 2, 1)),
        pair_grad,
        expand_bias_grad,
        jnp.transpose(table_grad, (1, 0, 2)),
        jnp.transpose(vector_grads, (1, 0, 2)),
    )


def solution(mesh):
    return jax.shard_map(
        shards,
        mesh=mesh,
        in_specs=(
            P(("dp", "mp"), None),
            P("dp", None),
            P(("dp", "mp"), None),
            P(),
            P(),
            P(None, None, None, "mp"),
            P(None, None, "mp"),
            P(None, "mp", None),
            P(None, "mp", None),
            P(),
            P(),
            P(),
            P(None, None, "mp"),
            P(None, "mp"),
            P(None, "mp", None),
            P(),
        ),
        out_specs=(
            P(("dp", "mp"), None),
            P(("dp", "mp"), None),
            P(None, "dp", None, "mp"),
            P(None, "mp", "dp"),
            P(None, "dp", "mp"),
            P(None, "mp", "dp"),
            P(None, None, "mp"),
            P(None, "mp"),
            P(None, "mp", None),
            P(),
        ),
        check_vma=False,
    )
```
